128 devices in a mesh: dp: 16 (over y, x_hi, core), tensor: 8 (over x_lo, z).
Axes of the slice: x: 4 (x_hi: 2, x_lo: 2; x = x_hi * 2 + x_lo), y: 4, z: 4, core: 2. Of those that a mesh axis runs over, the one named last changes fastest.
Arguments:
- hidden_in: bfloat16 [16384, 2048], P(('dp', 'tensor')), may hold values from -6 to 6
- segment_ids: int32 [16384], P('dp'), may hold values from 0 to 47, as said below
- ln1_gain: float32 [2048], replicated, may hold values from 0.5 to 1.5
- ln1_bias: float32 [2048], replicated, may hold values from -3 to 3
- ln2_gain: float32 [2048], replicated, may hold values from 0.5 to 1.5
- ln2_bias: float32 [2048], replicated, may hold values from -3 to 3
- w_qkv: bfloat16 [2048, 6144], P('dp', 'tensor'), may hold values from -0.125 to 0.125
- b_qkv: float32 [6144], P('tensor'), may hold values from -3 to 3
- w_dense: bfloat16 [2048, 2048], P('tensor', 'dp'), may hold values from -1 to 1
- b_dense: float32 [2048], replicated, may hold values from -3 to 3
- w_in: bfloat16 [2048, 8192], P('dp', 'tensor'), may hold values from -0.125 to 0.125
- b_in: float32 [8192], P('tensor'), may hold values from -3 to 3
- w_out: bfloat16 [8192, 2048], P('tensor', 'dp'), may hold values from -0.0625 to 0.0625
- b_out: float32 [2048], replicated, may hold values from -3 to 3
- cotangent: bfloat16 [16384, 2048], P(('dp', 'tensor')), may hold values from -6 to 6
Outputs:
- hidden_out: bfloat16 [16384, 2048], P(('dp', 'tensor'))
- grad_input: bfloat16 [16384, 2048], P(('dp', 'tensor'))
- grad_ln1_gain: float32 [2048], replicated
- grad_ln1_bias: float32 [2048], replicated
- grad_ln2_gain: float32 [2048], replicated
- grad_ln2_bias: float32 [2048], replicated
- grad_w_qkv: float32 [2048, 6144], P('dp', 'tensor')
- grad_b_qkv: float32 [6144], P('tensor')
- grad_w_dense: float32 [2048, 2048], P('tensor', 'dp')
- grad_b_dense: float32 [2048], replicated
- grad_w_in: float32 [2048, 8192], P('dp', 'tensor')
- grad_b_in: float32 [8192], P('tensor')
- grad_w_out: float32 [8192, 2048], P('tensor', 'dp')
- grad_b_out: float32 [2048], replicated
The draws below stay inside these ranges and needn't reach their ends.
Inputs may be any that keep to these rules, and one draw needn't show every extreme that they name: `segment_ids`: along the tokens the numbers never fall; sequence s (rows s * 1024 to (s + 1) * 1024 - 1) holds exactly three segments, numbered 3 s, 3 s + 1 and 3 s + 2, and its first and last segments hold fewer than min(128, 256) tokens each.
All inputs are finite; a program needn't handle non-finite values.
Results may differ from the reference program's by a relative error of at most 0.015.
Values may be sent and summed in bfloat16 or wider, within the bound.
No kernel may reach another device: no remote copies, remote signals or barrier semaphores. Data moves between devices by JAX's collectives and lax.ppermute only.
A program may use at most 128 MiB of HBM per device.

```python
import math
import jax
import jax.numpy as jnp
from jax import lax

D = 2048
H = 8
DH = 256
ROT = 64
FF = 8192
LENGTH = 1024
TOK_DEV = 128
TOKENS = 16384


def draw_segment_ids(key, part):
    key = jax.random.fold_in(key, 11)
    key_first, key_last = jax.random.split(key)
    count = TOKENS // LENGTH
    edge = min(TOK_DEV, LENGTH // 4)
    first = jax.random.randint(key_first, (count, 1), 1, edge)
    last = LENGTH - jax.random.randint(key_last, (count, 1), 1, edge)
    place = jnp.arange(LENGTH, dtype=jnp.int32)[None, :]
    within = (place >= first).astype(jnp.int32) + (place >= last).astype(jnp.int32)
    return (within + 3 * jnp.arange(count, dtype=jnp.int32)[:, None]).reshape(TOKENS).astype(jnp.int32)


def level_of(rng, shape, cuts, smallest, top_value):
    def one(dim, shards_of):
        steps = jax.random.uniform(jax.random.fold_in(jax.random.fold_in(rng, 6), dim), (shards_of,), jnp.float32, smallest / len(cuts), top_value / len(cuts))
        return jnp.repeat(jnp.exp(steps), shape[dim] // shards_of).reshape((-1,) + (1,) * (len(shape) - dim - 1))

    loudness = one(*cuts[0])
    for cut in cuts[1:]:
        loudness = loudness * one(*cut)
    return loudness


def scatter_about(key, shape, spread, most, shards=(), kind=jnp.bfloat16):
    loudness = level_of(key, shape, shards, -0.22, 0.18) if shards else 1.0
    values = jax.random.normal(key, shape, jnp.float32) * spread * loudness
    return jnp.minimum(jnp.maximum(values, -most), most).astype(kind)


def setup_inputs(seed: int = 0) -> dict:
    seeds = jax.random.split(jax.random.key(seed), 16)
    return {
        "hidden_in": scatter_about(seeds[0], (TOKENS, D), 1.0, 6.0, ((0, 128),)),
        "segment_ids": draw_segment_ids(jax.random.fold_in(seeds[15], 71), 0),
        "ln1_gain": jnp.clip(1.0 + 0.1 * jax.random.normal(seeds[2], (D,), jnp.float32), 0.5, 1.5),
        "ln1_bias": scatter_about(seeds[3], (D,), 0.3, 3.0, (), jnp.float32),
        "ln2_gain": jnp.clip(1.0 + 0.1 * jax.random.normal(seeds[4], (D,), jnp.float32), 0.5, 1.5),
        "ln2_bias": scatter_about(seeds[5], (D,), 0.3, 3.0, (), jnp.float32),
        "w_qkv": scatter_about(seeds[6], (D, 3 * H * DH), D ** -0.5, 0.125, ((0, 16), (1, 8))),
        "b_qkv": scatter_about(seeds[7], (3 * H * DH,), 0.3, 3.0, ((0, 8),), jnp.float32),
        "w_dense": scatter_about(seeds[8], (H * DH, D), (max(4, H * DH // 64)) ** -0.5, 1.0, ((0, 8), (1, 16))),
        "b_dense": scatter_about(seeds[9], (D,), 0.3, 3.0, (), jnp.float32),
        "w_in": scatter_about(seeds[10], (D, FF), D ** -0.5, 0.125, ((0, 16), (1, 8))),
        "b_in": scatter_about(seeds[11], (FF,), 0.3, 3.0, ((0, 8),), jnp.float32),
        "w_out": scatter_about(seeds[12], (FF, D), FF ** -0.5, 0.0625, ((0, 8), (1, 16))),
        "b_out": scatter_about(seeds[13], (D,), 0.3, 3.0, (), jnp.float32),
        "cotangent": scatter_about(seeds[14], (TOKENS, D), 1.0, 6.0, ((0, 128),)),
    }


@jax.custom_vjp
def low(v):
    return lax.optimization_barrier(v.astype(jnp.bfloat16)).astype(jnp.float32)

@jax.custom_vjp
def low_back(v):
    return v

def low_keep(v):
    return (low(v), None)

def low_pass(kept, grad):
    return (grad,)

def back_keep(v):
    return (v, None)

def back_low(kept, grad):
    return (low(grad),)
low.defvjp(low_keep, low_pass)
low_back.defvjp(back_keep, back_low)
EPS = 1e-05
NEG = -1e+30

def product(left, right):
    return jnp.dot(left, right, precision=lax.Precision.HIGHEST, preferred_element_type=jnp.float32)

def layer_norm(rows, gain, bias):
    centre = lax.optimization_barrier(jnp.mean(rows, axis=-1, keepdims=True))
    centred = rows - centre
    variance = lax.optimization_barrier(jnp.mean(centred * centred, axis=-1, keepdims=True))
    return centred * lax.rsqrt(variance + EPS) * gain + bias

def positions(segment):
    count = segment.shape[0]
    index = jnp.arange(count, dtype=jnp.int32)
    change = jnp.concatenate([jnp.ones((1,), dtype=bool), segment[1:] != segment[:-1]])
    start = lax.cummax(jnp.where(change, index, jnp.zeros_like(index)), axis=0)
    return index - start

def rotate(tensor, place, sign):
    half_dims = ROT // 2
    exponent = jnp.arange(half_dims, dtype=jnp.float32) * (2.0 / ROT)
    inverse = jnp.exp(-exponent * math.log(10000.0))
    angle = place.astype(jnp.float32)[:, None] * inverse[None, :]
    cosine = jnp.concatenate([jnp.cos(angle), jnp.cos(angle)], axis=-1)[:, None, :]
    sine = sign * jnp.concatenate([jnp.sin(angle), jnp.sin(angle)], axis=-1)[:, None, :]
    head = tensor[..., :ROT]
    turned = jnp.concatenate([-head[..., half_dims:], head[..., :half_dims]], axis=-1)
    return jnp.concatenate([head * cosine + turned * sine, tensor[..., ROT:]], axis=-1)

def sequence_forward(rows, weights, segment):
    gain_one, bias_one, gain_two, bias_two, weight_qkv, bias_qkv, weight_dense, bias_dense, weight_in, bias_in, weight_out, bias_out = weights
    length = rows.shape[0]
    place = positions(segment)
    normed_one = low(layer_norm(rows, gain_one, bias_one))
    normed_two = low(layer_norm(rows, gain_two, bias_two))
    mixed = low_back(product(normed_one, weight_qkv) + bias_qkv).reshape(length, H, 3, DH)
    scale = DH ** (-0.5)
    queries = low(rotate(mixed[:, :, 0], place, 1.0) * scale)
    keys = low(rotate(mixed[:, :, 1], place, 1.0))
    values = low(mixed[:, :, 2])
    scores = low_back(jnp.einsum('qhd,khd->hqk', queries, keys, precision=lax.Precision.HIGHEST))
    index = jnp.arange(length, dtype=jnp.int32)
    allowed = (segment[:, None] == segment[None, :]) & (index[:, None] >= index[None, :])
    scores = jnp.where(allowed[None], scores, NEG)
    log_total = jax.nn.logsumexp(scores, axis=-1)
    probs = low(jnp.exp(scores - log_total[..., None]))
    context = jnp.einsum('hqk,khd->qhd', probs, values, precision=lax.Precision.HIGHEST).reshape(length, H * DH)
    context = low(low_back(context))
    hidden = low(jax.nn.gelu(low_back(product(normed_two, weight_in) + bias_in), approximate=False))
    return rows + product(context, weight_dense) + bias_dense + product(hidden, weight_out) + bias_out

def reference(hidden_in, segment_ids, ln1_gain, ln1_bias, ln2_gain, ln2_bias, w_qkv, b_qkv, w_dense, b_dense, w_in, b_in, w_out, b_out, cotangent):
    weights = (ln1_gain, ln1_bias, ln2_gain, ln2_bias, w_qkv.astype(jnp.float32), b_qkv, w_dense.astype(jnp.float32), b_dense, w_in.astype(jnp.float32), b_in, w_out.astype(jnp.float32), b_out)
    count = TOKENS // LENGTH
    inputs = hidden_in.astype(jnp.float32).reshape(count, LENGTH, D)
    segments = segment_ids.reshape(count, LENGTH)
    incoming = cotangent.astype(jnp.float32).reshape(count, LENGTH, D)
    zeros = jax.tree.map(jnp.zeros_like, weights)

    def one_sequence(totals, item):
        sequence, segment, grad_seq = item
        result, pull = jax.vjp(lambda rows, params: sequence_forward(rows, params, segment), sequence, weights)
        grad_rows, grad_weights = pull(grad_seq)
        return (jax.tree.map(jnp.add, totals, grad_weights), (result, grad_rows))
    totals, (results, grad_rows) = lax.scan(one_sequence, zeros, (inputs, segments, incoming))
    return (results.reshape(TOKENS, D).astype(jnp.bfloat16), grad_rows.reshape(TOKENS, D).astype(jnp.bfloat16), totals[0], totals[1], totals[2], totals[3], totals[4], totals[5], totals[6], totals[7], totals[8], totals[9], totals[10], totals[11])
```

```python
import math

import jax
import jax.numpy as jnp
from jax import lax
from jax.experimental import pallas as pl
from jax.experimental.pallas import tpu as pltpu
from jax.sharding import PartitionSpec as P

DH = 256
ROT = 64
LENGTH = 1024
D = 2048
LANE = 128

EPS = 1e-05
NEG = -1e30
BF = jnp.bfloat16
F32 = jnp.float32

ORDER = ((0, 0), (0, 1), (3, 0), (1, 0), (3, 1), (2, 0), (1, 1), (2, 1))


def dp_pairs(step, flip, core):
    pairs = []
    for y in range(4):
        for xh in range(2):
            for c in range(2):
                pairs.append(
                    ((y * 2 + xh) * 2 + c, (((y + step) % 4) * 2 + (xh ^ flip)) * 2 + (c ^ core))
                )
    return pairs


def tensor_pairs(step, flip):
    return [(xl * 4 + z, (xl ^ flip) * 4 + (z + step) % 4) for xl in range(2) for z in range(4)]


def dp_move(value, step, flip, core=0):
    return lax.ppermute(value, "dp", dp_pairs(step, flip, core))


def tensor_move(value, step, flip):
    return lax.ppermute(value, "tensor", tensor_pairs(step, flip))


def gather_eight(block, move):
    rows = block.shape[0]
    half = rows // 2
    other = move(block, 0, 1)
    before = move(block, 1, 0)
    after = move(block, -1, 0)
    one_up = move(jnp.concatenate([other, before[:half]], axis=0), 1, 0)
    one_down = move(jnp.concatenate([after[half:], other], axis=0), -1, 0)
    two_up = move(one_up[:half], 1, 0)
    two_down = move(one_down[rows:], -1, 0)
    return [block, other, before, after, one_up, one_down, two_up, two_down]


def add(*terms):
    total = terms[0].astype(F32)
    for term in terms[1:]:
        total = total + term.astype(F32)
    return total.astype(BF)


def scatter_eight(chunks, move):
    rows = chunks[0].shape[0]
    half = rows // 2
    home, other, before, after, other_before, across, other_after, other_across = chunks
    got_up = move(other_across[:half], 1, 0)
    got_down = move(other_across[half:], -1, 0)
    send_up = jnp.concatenate(
        [add(other_after[:half], got_up), other_after[half:], across[:half]], axis=0
    )
    send_down = jnp.concatenate(
        [other_before[:half], add(other_before[half:], got_down), across[half:]], axis=0
    )
    from_up = move(send_up, 1, 0)
    from_down = move(send_down, -1, 0)
    last_up = move(
        jnp.concatenate([add(after[:half], from_up[rows:]), after[half:]], axis=0), 1, 0
    )
    last_down = move(
        jnp.concatenate([before[:half], add(before[half:], from_down[rows:])], axis=0), -1, 0
    )
    swapped = move(add(other, from_up[:rows], from_down[:rows]), 0, 1)
    return (
        home.astype(F32) + swapped.astype(F32) + last_up.astype(F32) + last_down.astype(F32)
    )


def split_rows(array, rows=LANE):
    return [array[i : i + rows] for i in range(0, array.shape[0], rows)]


def feature_tables():
    me = lax.axis_index("dp")
    y, xh, c = me // 4, (me // 2) % 2, me % 2
    true_of, rel_of = [], [None] * 16
    for dc in range(2):
        for dy, dx in ORDER:
            true_of.append((((y + dy) % 4) * 2 + (xh ^ dx)) * 2 + (c ^ dc))
    spot = {pair: k for k, pair in enumerate(ORDER)}
    by_step = jnp.array(
        [[spot[(dy, dx)] for dx in range(2)] for dy in range(4)], dtype=jnp.int32
    )
    for ty in range(4):
        for tx in range(2):
            for tc in range(2):
                rel_of[(ty * 2 + tx) * 2 + tc] = (tc ^ c) * 8 + by_step[(ty - y) % 4, tx ^ xh]
    return jnp.stack(true_of).astype(jnp.int32), jnp.stack(rel_of).astype(jnp.int32)


def shuffle_kernel(table, *refs):
    count = len(refs) // 2
    for src, dst in zip(refs[:count], refs[count:]):
        for k in range(16):
            start = pl.multiple_of(table[k] * LANE, LANE)
            dst[:, k * LANE : (k + 1) * LANE] = src[:, pl.ds(start, LANE)]


def shuffle(table, *arrays):
    return pl.pallas_call(
        shuffle_kernel,
        grid_spec=pltpu.PrefetchScalarGridSpec(
            num_scalar_prefetch=1,
            grid=(1,),
            in_specs=[pl.BlockSpec(a.shape, lambda i, t: (0, 0)) for a in arrays],
            out_specs=[pl.BlockSpec(a.shape, lambda i, t: (0, 0)) for a in arrays],
        ),
        out_shape=[jax.ShapeDtypeStruct(a.shape, a.dtype) for a in arrays],
        compiler_params=pltpu.CompilerParams(vmem_limit_bytes=32 * 1024 * 1024),
        name="shuffle",
    )(table, *arrays)


def positions(segment):
    count = segment.shape[0]
    index = jnp.arange(count, dtype=jnp.int32)
    change = jnp.concatenate([jnp.ones((1,), dtype=bool), segment[1:] != segment[:-1]])
    start = lax.cummax(jnp.where(change, index, jnp.zeros_like(index)), axis=0)
    return index - start


def turn_tables(place):
    half_dims = ROT // 2
    exponent = jnp.arange(half_dims, dtype=F32) * (2.0 / ROT)
    inverse = jnp.exp(-exponent * math.log(10000.0))
    angle = place.astype(F32)[:, None] * inverse[None, :]
    cosine, sine = jnp.cos(angle), jnp.sin(angle)
    return jnp.concatenate([cosine, cosine], axis=-1), jnp.concatenate([sine, sine], axis=-1)


def rotate(tensor, cosine, sine):
    half_dims = ROT // 2
    head = tensor[..., :ROT]
    turned = jnp.concatenate([-head[..., half_dims:], head[..., :half_dims]], axis=-1)
    return jnp.concatenate([head * cosine + turned * sine, tensor[..., ROT:]], axis=-1)


def dot(a, b, ca, cb):
    return lax.dot_general(a, b, (((ca,), (cb,)), ((), ())), preferred_element_type=F32)


def per_device(
    hidden_in,
    segment_ids,
    ln1_gain,
    ln1_bias,
    ln2_gain,
    ln2_bias,
    w_qkv,
    b_qkv,
    w_dense,
    b_dense,
    w_in,
    b_in,
    w_out,
    b_out,
    cotangent,
):
    true_of, rel_of = feature_tables()
    half = D // 2

    own_x, own_g = shuffle(true_of, hidden_in, cotangent)
    all_x = lax.all_gather(own_x, "tensor", axis=0, tiled=True)
    all_g = lax.all_gather(own_g, "tensor", axis=0, tiled=True)

    part_a = jnp.concatenate([w_qkv, w_in], axis=1)
    part_b = jnp.concatenate([w_dense, w_out], axis=0).T
    a_own = jnp.concatenate(gather_eight(part_a, dp_move), axis=0)
    a_far = dp_move(a_own, 0, 0, 1)
    b_own = jnp.concatenate(gather_eight(part_b, dp_move), axis=0)
    b_far = dp_move(b_own, 0, 0, 1)

    vectors = jnp.stack([ln1_gain, ln1_bias, ln2_gain, ln2_bias]).reshape(4, 16, LANE)
    vectors = jnp.take(vectors, true_of, axis=1).reshape(4, D)
    gain1, bias1, gain2, bias2 = (vectors[k][None, :] for k in range(4))

    rows_x = all_x.astype(F32)
    centre = jnp.mean(rows_x, axis=-1, keepdims=True)
    centred = rows_x - centre
    scale_rows = lax.rsqrt(jnp.mean(centred * centred, axis=-1, keepdims=True) + EPS)
    xhat = centred * scale_rows
    normed1 = (xhat * gain1 + bias1).astype(BF)
    normed2 = (xhat * gain2 + bias2).astype(BF)

    cosine, sine = turn_tables(positions(segment_ids))
    mixed = dot(normed1[:, :half], a_own[:, :768], 1, 0) + dot(normed1[:, half:], a_far[:, :768], 1, 0)
    mixed = mixed + b_qkv
    scale = DH ** (-0.5)
    queries = (rotate(mixed[:, :DH], cosine, sine) * scale).astype(BF)
    keys = rotate(mixed[:, DH : 2 * DH], cosine, sine).astype(BF)
    values = mixed[:, 2 * DH :].astype(BF)
    index = jnp.arange(LENGTH, dtype=jnp.int32)
    allowed = (segment_ids[:, None] == segment_ids[None, :]) & (index[:, None] >= index[None, :])
    scores = jnp.where(allowed, dot(queries, keys, 1, 1), NEG)
    log_total = jax.nn.logsumexp(scores, axis=-1, keepdims=True)
    context = dot(jnp.exp(scores - log_total).astype(BF), values, 1, 0).astype(BF)

    pre = dot(normed2[:, :half], a_own[:, 768:], 1, 0) + dot(normed2[:, half:], a_far[:, 768:], 1, 0)
    pre = pre + b_in
    cdf = 0.5 * (1.0 + lax.erf(pre * (0.5**0.5)))
    hidden = (pre * cdf).astype(BF)
    slope = cdf + pre * jnp.exp(-0.5 * pre * pre) * (1.0 / math.sqrt(2.0 * math.pi))

    mids = jnp.concatenate([context, hidden], axis=1)
    out_part = jnp.concatenate([dot(mids, b_own, 1, 1), dot(mids, b_far, 1, 1)], axis=1).astype(BF)
    summed = lax.psum_scatter(out_part, "tensor", scatter_dimension=0, tiled=True)

    grad_b_far = dot(all_g[:, half:], mids, 0, 0).astype(BF)
    grad_b_near = dot(all_g[:, :half], mids, 0, 0)
    grad_b = add(grad_b_near, dp_move(grad_b_far, 0, 0, 1))
    grad_b = scatter_eight(split_rows(grad_b), dp_move)

    d_mids = dot(all_g[:, :half], b_own, 1, 0) + dot(all_g[:, half:], b_far, 1, 0)
    d_context = d_mids[:, :DH].astype(BF)
    d_pre = (d_mids[:, DH:] * slope).astype(BF)

    probs = jnp.exp(scores - log_total)
    d_probs = dot(d_context, values, 1, 1)
    spread = jnp.sum(probs * d_probs, axis=-1, keepdims=True)
    d_scores = (probs * (d_probs - spread)).astype(BF)
    d_queries = dot(d_scores, keys, 1, 0)
    d_keys = dot(d_scores, queries, 0, 0)
    d_values = dot(probs.astype(BF), d_context, 0, 0)
    d_mixed = jnp.concatenate(
        [rotate(d_queries * scale, cosine, -sine), rotate(d_keys, cosine, -sine), d_values], axis=1
    ).astype(BF)

    grad_a_far = jnp.concatenate(
        [dot(normed1[:, half:], d_mixed, 0, 0), dot(normed2[:, half:], d_pre, 0, 0)], axis=1
    ).astype(BF)
    grad_a_near = jnp.concatenate(
        [dot(normed1[:, :half], d_mixed, 0, 0), dot(normed2[:, :half], d_pre, 0, 0)], axis=1
    )
    grad_a = add(grad_a_near, dp_move(grad_a_far, 0, 0, 1))
    grad_a = scatter_eight(split_rows(grad_a), dp_move)

    d_normed1 = jnp.concatenate(
        [dot(d_mixed, a_own[:, :768], 1, 1), dot(d_mixed, a_far[:, :768], 1, 1)], axis=1
    )
    d_normed2 = jnp.concatenate(
        [dot(d_pre, a_own[:, 768:], 1, 1), dot(d_pre, a_far[:, 768:], 1, 1)], axis=1
    )
    u_part = (d_normed1 * gain1 + d_normed2 * gain2).astype(BF)
    u_rows = lax.psum_scatter(u_part, "tensor", scatter_dimension=0, tiled=True).astype(F32)

    norm_sums = jnp.stack(
        [
            jnp.sum(d_normed1 * xhat, axis=0),
            jnp.sum(d_normed1, axis=0),
            jnp.sum(d_normed2 * xhat, axis=0),
            jnp.sum(d_normed2, axis=0),
            jnp.sum(own_g.astype(F32), axis=0),
        ]
    )
    norm_sums = jnp.take(norm_sums.reshape(5, 16, LANE), rel_of, axis=1).reshape(80, LANE)
    bias_sums = jnp.concatenate(
        [jnp.sum(d_mixed.astype(F32), axis=0), jnp.sum(d_pre.astype(F32), axis=0)]
    ).reshape(14, LANE)
    for step, flip in ((0, 1), (1, 0), (2, 0)):
        norm_sums = norm_sums + butterfly(norm_sums, "tensor", step, flip)
    sums = jnp.concatenate([norm_sums, bias_sums, jnp.zeros((2, LANE), F32)], axis=0)
    for step, flip, core in ((0, 0, 1), (0, 1, 0), (1, 0, 0), (2, 0, 0)):
        sums = sums + butterfly(sums, "dp", step, flip, core)
    gain_one, bias_one, gain_two, bias_two, output_total = (
        sums[16 * k : 16 * (k + 1)].reshape(D) for k in range(5)
    )
    bias_sums = sums[80:94].reshape(1792)

    own = own_x.astype(F32)
    centre = jnp.mean(own, axis=-1, keepdims=True)
    centred = own - centre
    rate = lax.rsqrt(jnp.mean(centred * centred, axis=-1, keepdims=True) + EPS)
    own_hat = centred * rate
    grad_rows = rate * (
        u_rows
        - jnp.mean(u_rows, axis=-1, keepdims=True)
        - own_hat * jnp.mean(u_rows * own_hat, axis=-1, keepdims=True)
    )
    rel_out = own + summed.astype(F32)
    hidden_out, grad_input = shuffle(rel_of, rel_out, grad_rows + own_g.astype(F32))
    hidden_out = (hidden_out + b_dense + b_out).astype(BF)
    return (
        hidden_out,
        grad_input.astype(BF),
        gain_one,
        bias_one,
        gain_two,
        bias_two,
        grad_a[:, :768],
        bias_sums[:768],
        grad_b[:, :DH].T,
        output_total,
        grad_a[:, 768:],
        bias_sums[768:],
        grad_b[:, DH:].T,
        output_total,
    )


def butterfly(value, axis, step, flip, core=0):
    pairs = []
    if axis == "dp":
        for y in range(4):
            for xh in range(2):
                for c in range(2):
                    pairs.append(
                        ((y * 2 + xh) * 2 + c, ((y ^ step) * 2 + (xh ^ flip)) * 2 + (c ^ core))
                    )
    else:
        for xl in range(2):
            for z in range(4):
                pairs.append((xl * 4 + z, (xl ^ flip) * 4 + (z ^ step)))
    return lax.ppermute(value, axis, pairs)


def solution(mesh):
    in_specs = (
        P(("dp", "tensor"), None),
        P("dp"),
        P(),
        P(),
        P(),
        P(),
        P("dp", "tensor"),
        P("tensor"),
        P("tensor", "dp"),
        P(),
        P("dp", "tensor"),
        P("tensor"),
        P("tensor", "dp"),
        P(),
        P(("dp", "tensor"), None),
    )
    out_specs = (
        P(("dp", "tensor"), None),
        P(("dp", "tensor"), None),
        P(),
        P(),
        P(),
        P(),
        P("dp", "tensor"),
        P("tensor"),
        P("tensor", "dp"),
        P(),
        P("dp", "tensor"),
        P("tensor"),
        P("tensor", "dp"),
        P(),
    )
    return jax.shard_map(
        per_device, mesh=mesh, in_specs=in_specs, out_specs=out_specs, check_vma=False
    )
```

```python
import functools
import math

import jax
import jax.numpy as jnp
from jax import lax
from jax.experimental import pallas as pl
from jax.experimental.pallas import tpu as pltpu
from jax.sharding import PartitionSpec as P

DH = 256
ROT = 64
LENGTH = 1024
D = 2048
LANE = 128
HALF = 64

EPS = 1e-05
NEG = -1e30
BF = jnp.bfloat16
F32 = jnp.float32

ORDER = ((0, 0), (0, 1), (3, 0), (1, 0), (3, 1), (2, 0), (1, 1), (2, 1))
ROOM = 64 * 1024 * 1024 - 128 * 1024
TILE = 256
SCALE = DH**-0.5
BIASES = 5
QUARTER = LENGTH // 4
QUARTERS = tuple((n * QUARTER, (n + 1) * QUARTER) for n in range(4))
FAST, SLOW, SCALAR = pltpu.VMEM, pltpu.HBM, pltpu.SMEM


def dp_pairs(step, flip, core):
    pairs = []
    for y in range(4):
        for xh in range(2):
            for c in range(2):
                pairs.append(
                    ((y * 2 + xh) * 2 + c, (((y + step) % 4) * 2 + (xh ^ flip)) * 2 + (c ^ core))
                )
    return pairs


def tensor_pairs(step, flip):
    return [(xl * 4 + z, (xl ^ flip) * 4 + (z + step) % 4) for xl in range(2) for z in range(4)]


def x_move(value, step):
    pairs = []
    for dp in range(16):
        for at in range(8):
            x = (dp // 2 % 2 * 2 + at // 4 + step) % 4
            to = dp - dp // 2 % 2 * 2 + x // 2 * 2
            pairs.append((dp * 8 + at, to * 8 + x % 2 * 4 + at % 4))
    return lax.ppermute(value, ("dp", "tensor"), pairs)


def dp_move(value, step, flip, core=0):
    return lax.ppermute(value, "dp", dp_pairs(step, flip, core))


def tensor_move(value, step, flip):
    return lax.ppermute(value, "tensor", tensor_pairs(step, flip))


def shape(rows, cols, dtype):
    return jax.ShapeDtypeStruct((rows, cols), dtype)


class Copies:
    def __init__(self, sems):
        self.sems, self.count = sems, 0

    def start(self, source, target):
        copy = pltpu.make_async_copy(source, target, self.sems.at[self.count])
        self.count += 1
        copy.start()
        return copy


def wait(copies):
    for copy in copies:
        copy.wait()


def call(body, args, outs, ins=FAST, to=FAST, scratch=(), cost=(0, 0), name=None, after=()):
    moved = sum(math.prod(a.shape) * a.dtype.itemsize for a in (*args, *outs))
    count, given, end = len(args), len(args) + len(after), len(args) + len(after) + len(outs)
    ins = [ins] * count if not isinstance(ins, (tuple, list)) else list(ins)
    to = [to] * len(outs) if not isinstance(to, (tuple, list)) else list(to)
    fast_in = [i for i, w in enumerate(ins) if w is FAST]
    fast_out = [i for i, w in enumerate(to) if w is FAST]
    held = [pltpu.VMEM(args[i].shape, args[i].dtype) for i in fast_in]
    held += [pltpu.VMEM(outs[i].shape, outs[i].dtype) for i in fast_out]
    held += [pltpu.VMEM((8, LANE), F32), pltpu.SemaphoreType.DMA((len(fast_in) + len(fast_out) + 1,))]

    def run(*refs):
        refs = list(refs)
        given_refs, out_refs, token, rest = refs[:count], refs[given:end], refs[end], refs[end + 1 :]
        own, rest = rest[: len(held)], rest[len(held) :]
        copies = Copies(own[-1])
        begun = []
        for slot, i in enumerate(fast_in):
            begun.append(copies.start(given_refs[i], own[slot]))
            given_refs[i] = own[slot]
        targets = list(out_refs)
        for slot, i in enumerate(fast_out):
            out_refs[i] = own[len(fast_in) + slot]
        own[-2][...] = jnp.zeros((8, LANE), F32)
        last = [copies.start(own[-2], token)]
        wait(begun)
        body(*given_refs, *out_refs, *rest)
        for i in fast_out:
            last.append(copies.start(out_refs[i], targets[i]))
        wait(last)

    where = lambda w: pl.BlockSpec(memory_space=SCALAR if w is SCALAR else SLOW)
    return pl.pallas_call(
        run,
        in_specs=[where(w) for w in ins] + [where(SLOW)] * len(after),
        out_specs=[where(SLOW)] * (len(outs) + 1),
        out_shape=[*outs, shape(8, LANE, F32)],
        scratch_shapes=[*held, *scratch],
        compiler_params=pltpu.CompilerParams(vmem_limit_bytes=ROOM),
        cost_estimate=pl.CostEstimate(
            flops=1, transcendentals=0, bytes_accessed=1
        ),
        name=name,
    )(*args, *after)


def stage_kernel(groups, counts, *refs):
    refs = list(refs)
    arrays = [[refs.pop(0) for _ in range(count)] for count in counts]
    outs = [[refs.pop(0) for _ in parts] for parts in groups]
    held = [refs.pop(0) for _ in groups]
    copies = Copies(refs.pop(0))
    segments = []
    for parts, given, made, room in zip(groups, arrays, outs, held):
        at = 0
        for out, part in zip(made, parts):
            to = 0
            for rows, terms in part:
                places, begun = [], []
                for index, start in terms:
                    source = given[index].at[start : start + rows, :]
                    begun.append(copies.start(source, room.at[at : at + rows, :]))
                    places.append(at)
                    at += rows
                segments.append((out.at[to : to + rows, :], room, rows, places, begun))
                to += rows
    pending = []
    for target, room, rows, places, begun in segments:
        wait(begun)
        if len(places) > 1:

            def add(i, carry, room=room, places=places):
                where = [pl.ds(pl.multiple_of(place + i * 16, 16), 16) for place in places]
                total = room[where[0], :].astype(F32)
                for one in where[1:]:
                    total = total + room[one, :].astype(F32)
                room[where[0], :] = total.astype(BF)
                return carry

            lax.fori_loop(0, rows // 16, add, 0)
        pending.append(copies.start(room.at[places[0] : places[0] + rows, :], target))
    wait(pending)


def stages(groups, after=(), name="stage"):
    scratch, outs = [], []
    for arrays, parts in groups:
        cols = arrays[0].shape[1]
        rows = sum(r * len(t) for part in parts for r, t in part)
        scratch.append(pltpu.VMEM((rows, cols), BF))
        outs += [shape(sum(r for r, _ in part), cols, BF) for part in parts]
    copies = sum(len(t) + 1 for _, parts in groups for part in parts for _, t in part)
    *made, token = call(
        functools.partial(
            stage_kernel, tuple(g[1] for g in groups), tuple(len(g[0]) for g in groups)
        ),
        tuple(array for arrays, _ in groups for array in arrays),
        outs,
        ins=SLOW,
        to=SLOW,
        scratch=[*scratch, pltpu.SemaphoreType.DMA((copies,))],
        name=name,
        after=after,
    )
    split = []
    for _, parts in groups:
        split.append(made[: len(parts)])
        made = made[len(parts) :]
    return (*split, token)


def stage(arrays, parts, after=(), name="stage"):
    made, token = stages(((arrays, parts),), after, name)
    return (*made, token)


def row_set(index, start, rows):
    return (rows, ((index, start),))


def gather_one(block, move):
    return move(block, 0, 1), move(block, 1, 0), move(block, -1, 0)


def gather_two(block, got, move, after, name):
    parts = (
        (row_set(1, 0, LANE), row_set(2, 0, HALF)),
        (row_set(3, HALF, HALF), row_set(1, 0, LANE)),
    )
    up, down, token = stage((block, *got), parts, after=after, name=name)
    return (move(up, 1, 0), move(down, -1, 0)), token


def gather_three(block, first, got, move, after, name):
    joined = tuple((n, ((2 + k, 0),)) for k, n in enumerate((LANE,) * 4)) + (
        row_set(0, 0, 192),
        row_set(1, 0, 192),
    )
    parts = ((row_set(0, 0, HALF),), (row_set(1, LANE, HALF),), joined)
    up, down, joined, token = stage((*got, block, *first), parts, after=after, name=name)
    return (move(up, 1, 0), move(down, -1, 0)), joined, token


def pair_two(block, other, move, after, name):
    both, token = stage((block, other), ((row_set(0, 0, LANE), row_set(1, 0, LANE)),), after=after, name=name)
    return both, (move(both, 1, 0), move(both, -1, 0)), token


def pair_three(both, got, move, after, name):
    parts = (
        (row_set(0, 0, HALF), row_set(0, LANE, HALF)),
        (row_set(1, HALF, HALF), row_set(1, LANE + HALF, HALF)),
        (row_set(2, 0, 2 * LANE), row_set(0, 0, 2 * LANE), row_set(1, 0, 2 * LANE)),
    )
    up, down, joined, token = stage((*got, both), parts, after=after, name=name)
    return (move(up, 1, 0), move(down, -1, 0)), joined, token


def sums_of(count, start):
    return tuple((k, start) for k in range(count))


def scatter_one(n):
    return (((HALF, sums_of(n, 7 * LANE)),), ((HALF, sums_of(n, 7 * LANE + HALF)),))


def scatter_two(n):
    add = lambda start: sums_of(n, start)
    return (
        (
            (HALF, (*add(6 * LANE), (n, 0))),
            (HALF, add(6 * LANE + HALF)),
            (HALF, add(5 * LANE)),
        ),
        (
            (HALF, add(5 * LANE + HALF)),
            (HALF, add(4 * LANE)),
            (HALF, (*add(4 * LANE + HALF), (n + 1, 0))),
        ),
    )


def scatter_three(n):
    add = lambda start: sums_of(n, start)
    return (
        ((HALF, (*add(3 * LANE), (n, LANE))), (HALF, add(3 * LANE + HALF))),
        ((HALF, add(2 * LANE)), (HALF, (*add(2 * LANE + HALF), (n + 1, 0)))),
        ((LANE, (*add(LANE), (n, 0), (n + 1, HALF))),),
    )


def both_ways(sends, move):
    got = [move(sends[0], 1, 0), move(sends[1], -1, 0)]
    return (*got, *(move(send, 0, 1) for send in sends[2:]))


def pair_scatter_one(chunks, move, after, name):
    n = len(chunks)
    add = lambda start: sums_of(n, start)
    parts = (
        ((HALF, add(5 * LANE)), (HALF, add(7 * LANE))),
        ((HALF, add(5 * LANE + HALF)), (HALF, add(7 * LANE + HALF))),
    )
    up, down, token = stage(chunks, parts, after=after, name=name)
    return (move(up, 1, 0), move(down, -1, 0)), token


def pair_scatter_two(chunks, got, move, after, name):
    n = len(chunks)
    add = lambda start: sums_of(n, start)
    parts = (
        (
            (HALF, (*add(3 * LANE), (n, 0))),
            (HALF, add(3 * LANE + HALF)),
            (HALF, (*add(6 * LANE), (n, HALF))),
            (HALF, add(6 * LANE + HALF)),
        ),
        (
            (HALF, add(2 * LANE)),
            (HALF, (*add(2 * LANE + HALF), (n + 1, 0))),
            (HALF, add(4 * LANE)),
            (HALF, (*add(4 * LANE + HALF), (n + 1, HALF))),
        ),
    )
    up, down, token = stage((*chunks, *got), parts, after=after, name=name)
    return (move(up, 1, 0), move(down, -1, 0)), token


def pair_scatter_three(chunks, got, move, after, name):
    n = len(chunks)
    parts = (((LANE, (*sums_of(n, LANE), (n, LANE), (n + 1, LANE))),),)
    swap, token = stage((*chunks, *got), parts, after=after, name=name)
    return (move(swap, 0, 1), *got), token


def feature_place(me, k):
    dp = me[0]
    dy, dx = ORDER[k % 8]
    y, xh, c = lax.shift_right_logical(dp, 2), lax.shift_right_logical(dp, 1) & 1, dp & 1
    return ((((y + dy) & 3) * 2 + (xh ^ dx)) * 2) + (c ^ (k // 8))


def token_place(me, k):
    at = me[1]
    dz, dx = ORDER[k]
    return (lax.shift_right_logical(at, 2) ^ dx) * 4 + (((at & 3) + dz) & 3)


def feature_cols(me, k):
    return pl.ds(pl.multiple_of(feature_place(me, k) * LANE, LANE), LANE)


def fixed_cols(k):
    return slice(k * LANE, (k + 1) * LANE)


def token_rows(me, k, count=LANE, offset=0):
    return pl.ds(pl.multiple_of(token_place(me, k) * LANE + offset, HALF), count)


def centred(rows):
    rows = rows.astype(F32)
    rows = rows - jnp.mean(rows, axis=-1, keepdims=True)
    return rows, lax.rsqrt(jnp.mean(rows * rows, axis=-1, keepdims=True) + EPS)


def begin_kernel(me, x, w_qkv, w_in, hat, part_a, held):
    rows, rate = centred(x[...])
    held[...] = rows * rate
    for k in range(16):
        hat[:, fixed_cols(k)] = held[:, feature_cols(me, k)].astype(BF)
    part_a[:, :768] = w_qkv[...]
    part_a[:, 768:] = w_in[...]


def begin(me, x, w_qkv, w_in):
    return call(
        begin_kernel, (me, x, w_qkv, w_in), [shape(LANE, D, BF), shape(LANE, 1792, BF)],
        ins=[SCALAR] + [FAST] * 3, scratch=[pltpu.VMEM((LANE, D), F32)], name="begin",
    )


def prepare_kernel(
    me, g, w_dense, w_out, g1, b1, g2, b2, b_qkv, b_in, near_g, part_b, vectors, bias, g_sum
):
    for k in range(16):
        to, at = fixed_cols(k), feature_cols(me, k)
        near_g[:, to] = g[:, at]
        for n, vector in enumerate((g1, b1, g2, b2)):
            vectors[n : n + 1, to] = vector[:, at]
    part_b[:, :DH] = w_dense[...].T
    part_b[:, DH:] = w_out[...].T
    bias[:, :768] = b_qkv[...]
    bias[:, 768:] = b_in[...]
    g_sum[...] = jnp.sum(g[...].astype(F32), axis=0, keepdims=True)


def prepare(me, *args, after):
    return call(
        prepare_kernel, (me, *args),
        [
            shape(LANE, D, BF), shape(LANE, 1280, BF), shape(4, D, F32), shape(1, 1792, F32), shape(1, D, F32),
        ],
        ins=[SCALAR] + [FAST] * len(args), name="prepare", after=after,
    )


def positions(segment):
    count = segment.shape[0]
    index = jnp.arange(count, dtype=jnp.int32)
    change = jnp.concatenate([jnp.ones((1,), dtype=bool), segment[1:] != segment[:-1]])
    start = lax.cummax(jnp.where(change, index, jnp.zeros_like(index)), axis=0)
    return index - start


def angles(segment):
    lane = jnp.arange(LANE, dtype=jnp.int32)
    exponent = (lane % (ROT // 2)).astype(F32) * (2.0 / ROT)
    inverse = jnp.where(lane < ROT, jnp.exp(-exponent * math.log(10000.0)), 0.0)
    angle = positions(segment).astype(F32)[:, None] * inverse[None, :]
    return jnp.cos(angle), jnp.sin(angle)


def dot(a, b, ca, cb):
    return lax.dot_general(a, b, (((ca,), (cb,)), ((), ())), preferred_element_type=F32)


def turn(head, cosine, sine):
    lane = lax.broadcasted_iota(jnp.int32, head.shape, 1)
    ahead = pltpu.roll(head, LANE - ROT // 2, 1)
    behind = pltpu.roll(head, ROT // 2, 1)
    return head * cosine + jnp.where(lane < ROT // 2, -ahead, behind) * sine


def masked_scores(q, k, seg_col, seg_row, first):
    scores = dot(q, k, 1, 1)
    row = first + lax.broadcasted_iota(jnp.int32, scores.shape, 0)
    col = lax.broadcasted_iota(jnp.int32, scores.shape, 1)
    allowed = (seg_col == seg_row) & (row >= col)
    return jnp.where(allowed, scores, NEG)


def load_weights(copies, pairs, cols, shift=0):
    place = slice(cols.start - shift, cols.stop - shift)
    started = []
    for pieces, layout, held in pairs:
        for piece, start, rows, block, offset in layout:
            at = block * LANE + offset
            started.append(
                copies.start(
                    pieces[piece].at[start : start + rows, cols], held.at[at : at + rows, place]
                )
            )
    return started


JOINED_PAIR = (
    (0, 0, 128, 0, 0),
    (0, 128, 128, 1, 0),
    (0, 256, 128, 2, 0),
    (0, 384, 128, 4, 0),
    (0, 512, 128, 3, 0),
    (0, 640, 128, 6, 0),
    (1, 0, 64, 5, 0),
    (1, 64, 64, 7, 0),
    (1, 128, 64, 5, 64),
    (1, 192, 64, 7, 64),
)
JOINED = ((0, 0, 896, 0, 0), (1, 0, 128, 7, 0))


def weighted(norm, own, other, bias, lo, hi, at):
    half = D // 2
    return (
        dot(norm[lo:hi, :half], own[:, at : at + TILE], 1, 0)
        + dot(norm[lo:hi, half:], other[:, at : at + TILE], 1, 0)
        + bias[:, at : at + TILE]
    )


def normed(hat, vectors, norm, lo, hi, k):
    x = hat[lo:hi, :].astype(F32)
    norm[lo:hi, :] = (x * vectors[k : k + 1, :] + vectors[k + 1 : k + 2, :]).astype(BF)


def attention_kernel(*refs):
    hat_hbm, near, far = refs[0], refs[1:3], refs[3:5]
    vectors, bias, cosine, sine, seg_col, seg_row = refs[5:11]
    mixed_out, context, log_total = refs[11:14]
    hat, own, other, norm, mixed, sems = refs[14:]
    copies = Copies(sems)
    pairs = ((near, JOINED, own), (far, JOINED, other))
    first = load_weights(copies, pairs, slice(0, TILE))
    rows = [copies.start(hat_hbm.at[lo:hi, :], hat.at[lo:hi, :]) for lo, hi in QUARTERS]
    second = load_weights(copies, pairs, slice(TILE, 3 * TILE))
    wait(first)
    for i in range(3):
        if i == 1:
            wait(second)
        for n, (lo, hi) in enumerate(QUARTERS):
            if i == 0:
                wait(rows[n : n + 1])
                normed(hat, vectors, norm, lo, hi, 0)
            acc = weighted(norm, own, other, bias, lo, hi, i * TILE)
            if i < 2:
                head = turn(acc[:, :LANE], cosine[lo:hi, :], sine[lo:hi, :])
                acc = jnp.concatenate([head, acc[:, LANE:]], axis=1)
            if i == 0:
                acc = acc * SCALE
            mixed[lo:hi, i * TILE : (i + 1) * TILE] = acc.astype(BF)
    saved = [copies.start(mixed, mixed_out)]
    for lo, hi in QUARTERS:
        scores = masked_scores(
            mixed[lo:hi, :DH], mixed[:hi, DH : 2 * DH], seg_col[lo:hi, :1], seg_row[:, :hi], lo
        )
        top = jnp.max(scores, axis=-1, keepdims=True)
        weights = jnp.exp(scores - top)
        total = jnp.sum(weights, axis=-1, keepdims=True)
        log_total[lo:hi, :] = jnp.broadcast_to(top + jnp.log(total), (hi - lo, LANE))
        probs = (weights * (1.0 / total)).astype(BF)
        context[lo:hi, :] = dot(probs, mixed[:hi, 2 * DH :], 1, 0).astype(BF)
    wait(saved)


def attention(hat, near, far, vectors, bias, cosine, sine, seg_col, seg_row, after):
    return call(
        attention_kernel,
        (hat, *near, *far, vectors, bias, cosine, sine, seg_col, seg_row),
        [shape(LENGTH, 768, BF), shape(LENGTH, DH, BF), shape(LENGTH, LANE, F32)],
        ins=[SLOW] * 5 + [FAST] * 6,
        to=[SLOW, FAST, FAST],
        scratch=[
            pltpu.VMEM((LENGTH, D), BF), pltpu.VMEM((1024, 768), BF),
            pltpu.VMEM((1024, 768), BF), pltpu.VMEM((LENGTH, D), BF),
            pltpu.VMEM((LENGTH, 768), BF), pltpu.SemaphoreType.DMA((16,)),
        ],
        cost=(2 * LENGTH * D * 768 + 4 * LENGTH * LENGTH * DH, LENGTH * 1024),
        name="attention", after=after,
    )


def units_kernel(*refs):
    hat_hbm, near, far, vectors, bias = refs[0], refs[1:3], refs[3:5], refs[5], refs[6]
    hidden_out, slope_out, hat, own, other, norm, hidden, slope, sems = refs[7:]
    copies = Copies(sems)
    pairs = ((near, JOINED, own), (far, JOINED, other))
    rows = [copies.start(hat_hbm.at[lo:hi, :], hat.at[lo:hi, :]) for lo, hi in QUARTERS]
    tiles = [load_weights(copies, pairs, slice(768 + i * TILE, 768 + (i + 1) * TILE), 768) for i in range(4)]
    saved = []
    for i in range(4):
        wait(tiles[i])
        cols = slice(i * TILE, (i + 1) * TILE)
        for n, (lo, hi) in enumerate(QUARTERS):
            if i == 0:
                wait(rows[n : n + 1])
                normed(hat, vectors, norm, lo, hi, 2)
            pre = weighted(norm, own, other, bias, lo, hi, i * TILE)
            cdf = 0.5 * (1.0 + lax.erf(pre * (0.5**0.5)))
            hidden[lo:hi, cols] = (pre * cdf).astype(BF)
            density = jnp.exp(-0.5 * pre * pre) * (1.0 / math.sqrt(2.0 * math.pi))
            slope[lo:hi, cols] = (cdf + pre * density).astype(BF)
        saved.append(copies.start(hidden.at[:, cols], hidden_out.at[:, cols]))
        saved.append(copies.start(slope.at[:, cols], slope_out.at[:, cols]))
    wait(saved)


def units(hat, near, far, vectors, bias, after):
    return call(
        units_kernel, (hat, *near, *far, vectors, bias), [shape(LENGTH, 1024, BF)] * 2,
        ins=[SLOW] * 5 + [FAST] * 2, to=SLOW,
        scratch=[
            pltpu.VMEM((LENGTH, D), BF), pltpu.VMEM((1024, 1024), BF),
            pltpu.VMEM((1024, 1024), BF), pltpu.VMEM((LENGTH, D), BF),
            pltpu.VMEM((LENGTH, 1024), BF), pltpu.VMEM((LENGTH, 1024), BF),
            pltpu.SemaphoreType.DMA((32,)),
        ],
        cost=(2 * LENGTH * D * 1024, LENGTH * 2048), name="units", after=after,
    )


def outer_b_kernel(first, g, context, hidden, grad_hbm, left, held_c, held_h, grad, sems):
    copies = Copies(sems)
    begun = [copies.start(context, held_c), copies.start(hidden, held_h)]
    tiles = load_tiles(copies, g, left, first)
    wait(begun)
    done = []
    for i in range(4):
        cols = slice(i * TILE, (i + 1) * TILE)
        wait(tiles[i : i + 1])
        grad[cols, :DH] = dot(left[:, cols], held_c[...], 0, 0).astype(BF)
        grad[cols, DH:] = dot(left[:, cols], held_h[...], 0, 0).astype(BF)
        done.append(copies.start(grad.at[cols, :], grad_hbm.at[cols, :]))
    wait(done)


def outer_b(g, context, hidden, first, after):
    return call(
        functools.partial(outer_b_kernel, first), (g, context, hidden), [shape(1024, 1280, BF)],
        ins=SLOW, to=SLOW,
        scratch=[
            pltpu.VMEM((LENGTH, 1024), BF), pltpu.VMEM((LENGTH, DH), BF),
            pltpu.VMEM((LENGTH, 1024), BF), pltpu.VMEM((1024, 1280), BF),
            pltpu.SemaphoreType.DMA((12,)),
        ],
        cost=(2 * LENGTH * 1024 * 1280, 0), name="outer_b", after=after,
    )


def output_kernel(*refs):
    context, hidden, near, far = refs[0], refs[1], refs[2:4], refs[4:6]
    out_hbm, held_c, held_h, own, other, out, sems = refs[6:]
    copies = Copies(sems)
    firsts = load_weights(copies, ((near, JOINED_PAIR[:2], own),), slice(0, 1280))
    begun = [copies.start(context, held_c), copies.start(hidden, held_h)]
    nears = load_weights(copies, ((near, JOINED_PAIR[2:], own),), slice(0, 1280))
    fars = load_weights(copies, ((far, JOINED_PAIR, other),), slice(0, 1280))
    wait(firsts + begun)
    done = []
    for i in range(8):
        held = own if i < 4 else other
        at = i % 4 * TILE
        cols = slice(i * TILE, (i + 1) * TILE)
        if i == 1:
            wait(nears)
        if i == 4:
            wait(fars)
        for lo, hi in QUARTERS:
            out[lo:hi, cols] = (
                dot(held_c[lo:hi, :], held[at : at + TILE, :DH], 1, 1)
                + dot(held_h[lo:hi, :], held[at : at + TILE, DH:], 1, 1)
            ).astype(BF)
        if i % 2:
            pair = slice((i - 1) * TILE, (i + 1) * TILE)
            done.append(copies.start(out.at[:, pair], out_hbm.at[:, pair]))
    wait(done)


def output(context, hidden, near, far, after):
    return call(
        output_kernel, (context, hidden, *near, *far), [shape(LENGTH, D, BF)], ins=SLOW, to=SLOW,
        scratch=[
            pltpu.VMEM((LENGTH, DH), BF), pltpu.VMEM((LENGTH, 1024), BF),
            pltpu.VMEM((1024, 1280), BF), pltpu.VMEM((1024, 1280), BF),
            pltpu.VMEM((LENGTH, D), BF), pltpu.SemaphoreType.DMA((28,)),
        ],
        cost=(2 * LENGTH * D * 1280, 0), name="output", after=after,
    )


def backward_kernel(*refs):
    g, near, far = refs[0], refs[1:3], refs[3:5]
    slope_hbm, mixed_hbm, hat_hbm, log_total, seg_col, seg_row, cosine, sine, vectors = refs[5:14]
    mixed_grad_hbm, pre_hbm, grad_hbm, sums_in, sums_qkv = refs[14:19]
    (held, own, other, slope, mixed, hat, d_context, d_pre, d_mixed, d_k, d_v, grad, sems) = refs[19:]
    half = D // 2
    copies = Copies(sems)
    pairs = ((near, JOINED_PAIR, own), (far, JOINED_PAIR, other))
    first = load_weights(copies, pairs, slice(0, TILE))
    rows = [copies.start(g.at[lo:hi, :], held.at[lo:hi, :]) for lo, hi in QUARTERS]
    rest = load_weights(copies, pairs, slice(TILE, 1280))
    slopes = [copies.start(slope_hbm, slope)]
    mixes = [copies.start(mixed_hbm, mixed)]
    hats = load_tiles(copies, hat_hbm, hat, half)
    done = []

    def product(lo, hi, cols):
        return dot(held[lo:hi, :half], own[:, cols], 1, 0) + dot(held[lo:hi, half:], other[:, cols], 1, 0)

    wait(first)
    for n, (lo, hi) in enumerate(QUARTERS):
        wait(rows[n : n + 1])
        d_context[lo:hi, :] = product(lo, hi, slice(0, TILE)).astype(BF)
    wait(rest + slopes)
    for i in range(4):
        cols = slice(i * TILE, (i + 1) * TILE)
        total = jnp.zeros((1, TILE), F32)
        for lo, hi in QUARTERS:
            acc = product(lo, hi, slice((i + 1) * TILE, (i + 2) * TILE))
            rounded = (acc * slope[lo:hi, cols].astype(F32)).astype(BF)
            d_pre[lo:hi, cols] = rounded
            total += jnp.sum(rounded.astype(F32), axis=0, keepdims=True)
        sums_in[:, cols] = total
    done.append(copies.start(d_pre, pre_hbm))

    wait(mixes)
    d_k[...] = jnp.zeros_like(d_k)
    d_v[...] = jnp.zeros_like(d_v)

    def back(lo, hi, value):
        head = turn(value[:, :LANE], cosine[lo:hi, :], -sine[lo:hi, :])
        return jnp.concatenate([head, value[:, LANE:]], axis=1)

    for lo, hi in QUARTERS:
        q, k, v = mixed[lo:hi, :DH], mixed[:hi, DH : 2 * DH], mixed[:hi, 2 * DH :]
        dc = d_context[lo:hi, :]
        scores = masked_scores(q, k, seg_col[lo:hi, :1], seg_row[:, :hi], lo)
        probs = jnp.exp(scores - log_total[lo:hi, :1])
        d_probs = dot(dc, v, 1, 1)
        spread = jnp.sum(probs * d_probs, axis=-1, keepdims=True)
        d_scores = (probs * (d_probs - spread)).astype(BF)
        d_mixed[lo:hi, :DH] = (back(lo, hi, dot(d_scores, k, 1, 0)) * SCALE).astype(BF)
        d_k[:hi, :] += dot(d_scores, q, 0, 0)
        d_v[:hi, :] += dot(probs.astype(BF), dc, 0, 0)
    total = jnp.zeros((1, 768), F32)
    for lo, hi in QUARTERS:
        d_mixed[lo:hi, DH : 2 * DH] = back(lo, hi, d_k[lo:hi, :]).astype(BF)
        d_mixed[lo:hi, 2 * DH :] = d_v[lo:hi, :].astype(BF)
        total += jnp.sum(d_mixed[lo:hi, :].astype(F32), axis=0, keepdims=True)
    sums_qkv[...] = total
    done.append(copies.start(d_mixed, mixed_grad_hbm))

    done += outer_a(copies, hat, hats, vectors, half, d_mixed, d_pre, grad, grad_hbm)
    wait(done)


def outer_a(copies, hat, hats, vectors, first, d_mixed, d_pre, grad, grad_hbm):
    done = []
    for i in range(4):
        wait(hats[i : i + 1])
        rows = slice(i * TILE, (i + 1) * TILE)
        cols = slice(first + i * TILE, first + (i + 1) * TILE)
        x = hat[:, rows].astype(F32)
        n1 = (x * vectors[0:1, cols] + vectors[1:2, cols]).astype(BF)
        n2 = (x * vectors[2:3, cols] + vectors[3:4, cols]).astype(BF)
        grad[rows, :768] = dot(n1, d_mixed[...], 0, 0).astype(BF)
        grad[rows, 768:] = dot(n2, d_pre[...], 0, 0).astype(BF)
        done.append(copies.start(grad.at[rows, :], grad_hbm.at[rows, :]))
    return done


def backward(g, near, far, slope, mixed, hat, log_total, seg_col, seg_row, cosine, sine, vectors, after):
    return call(
        backward_kernel,
        (g, *near, *far, slope, mixed, hat, log_total, seg_col, seg_row, cosine, sine, vectors),
        [
            shape(LENGTH, 768, BF), shape(LENGTH, 1024, BF), shape(1024, 1792, BF),
            shape(1, 1024, F32), shape(1, 768, F32),
        ],
        ins=[SLOW] * 8 + [FAST] * 6, to=[SLOW] * 3 + [FAST] * 2,
        scratch=[
            pltpu.VMEM((LENGTH, D), BF), pltpu.VMEM((1024, 1280), BF),
            pltpu.VMEM((1024, 1280), BF), pltpu.VMEM((LENGTH, 1024), BF),
            pltpu.VMEM((LENGTH, 768), BF), pltpu.VMEM((LENGTH, 1024), BF),
            pltpu.VMEM((LENGTH, DH), BF), pltpu.VMEM((LENGTH, 1024), BF),
            pltpu.VMEM((LENGTH, 768), BF), pltpu.VMEM((LENGTH, DH), F32),
            pltpu.VMEM((LENGTH, DH), F32), pltpu.VMEM((1024, 1792), BF),
            pltpu.SemaphoreType.DMA((64,)),
        ],
        cost=(2 * LENGTH * (D * 1280 + 1024 * 1792 + 5 * LENGTH * DH), LENGTH * LENGTH),
        name="backward", after=after,
    )


def inputs_back_kernel(me, *refs):
    mixed_hbm, pre_hbm, near, far, hat_hbm = refs[0], refs[1], refs[2:4], refs[4:6], refs[6]
    vectors, sums_qkv, sums_in, g_sum, u_hbm, sums = refs[7:13]
    d_mixed, d_pre, own, other, hat, u, sems = refs[13:]
    sums[...] = jnp.zeros_like(sums)
    sums[4:5, :] = g_sum[...]
    sums[BIASES : BIASES + 1, :768] = sums_qkv[...]
    sums[BIASES : BIASES + 1, 768:1792] = sums_in[...]
    copies = Copies(sems)
    begun = [copies.start(mixed_hbm, d_mixed), copies.start(pre_hbm, d_pre)]
    loads = []
    for i in range(8):
        pieces, held = (near, own) if i < 4 else (far, other)
        at = i % 4 * TILE
        cols = slice(i * TILE, (i + 1) * TILE)
        loads.append([copies.start(hat_hbm.at[:, cols], hat.at[:, cols])])
        for piece, first, last in ((0, at, min(at + TILE, 896)), (1, 896, 1024)):
            if piece == 0 or at + TILE > 896:
                start = first - 896 * piece
                loads[-1].append(
                    copies.start(
                        pieces[piece].at[start : start + last - first, :], held.at[first:last, :]
                    )
                )
    wait(begun)
    done = []
    for i in range(8):
        held = own if i < 4 else other
        at = i % 4 * TILE
        cols = slice(i * TILE, (i + 1) * TILE)
        wait(loads[i])
        totals = [jnp.zeros((1, TILE), F32) for _ in range(4)]
        for lo, hi in QUARTERS:
            d1 = dot(d_mixed[lo:hi, :], held[at : at + TILE, :768], 1, 1)
            d2 = dot(d_pre[lo:hi, :], held[at : at + TILE, 768:], 1, 1)
            x = hat[lo:hi, cols].astype(F32)
            u[lo:hi, cols] = (d1 * vectors[0:1, cols] + d2 * vectors[2:3, cols]).astype(BF)
            for k, term in enumerate((d1 * x, d1, d2 * x, d2)):
                totals[k] += jnp.sum(term, axis=0, keepdims=True)
        for k in range(4):
            for j in range(2):
                part = totals[k][:, fixed_cols(j)]
                sums[k : k + 1, feature_cols(me, 2 * i + j)] = part
        if i % 2:
            pair = slice((i - 1) * TILE, (i + 1) * TILE)
            done.append(copies.start(u.at[:, pair], u_hbm.at[:, pair]))
    wait(done)


def inputs_back(me, d_mixed, d_pre, near, far, hat, vectors, sums_qkv, sums_in, g_sum, after):
    return call(
        inputs_back_kernel,
        (me, d_mixed, d_pre, *near, *far, hat, vectors, sums_qkv, sums_in, g_sum),
        [shape(LENGTH, D, BF), shape(8, D, F32)],
        ins=[SCALAR] + [SLOW] * 7 + [FAST] * 4, to=[SLOW, FAST],
        scratch=[
            pltpu.VMEM((LENGTH, 768), BF), pltpu.VMEM((LENGTH, 1024), BF),
            pltpu.VMEM((1024, 1792), BF), pltpu.VMEM((1024, 1792), BF),
            pltpu.VMEM((LENGTH, D), BF), pltpu.VMEM((LENGTH, D), BF),
            pltpu.SemaphoreType.DMA((56,)),
        ],
        cost=(2 * LENGTH * D * 1792, 0), name="inputs_back", after=after,
    )


def load_tiles(copies, source, held, first):
    return [
        copies.start(
            source.at[:, first + i * TILE : first + (i + 1) * TILE],
            held.at[:, i * TILE : (i + 1) * TILE],
        )
        for i in range(4)
    ]


def outer_near_kernel(hat_hbm, vectors, mixed_hbm, pre_hbm, grad_hbm, hat, d_mixed, d_pre, grad, sems):
    copies = Copies(sems)
    begun = [copies.start(mixed_hbm, d_mixed), copies.start(pre_hbm, d_pre)]
    hats = load_tiles(copies, hat_hbm, hat, 0)
    wait(begun)
    wait(outer_a(copies, hat, hats, vectors, 0, d_mixed, d_pre, grad, grad_hbm))


def outer_near(hat, vectors, d_mixed, d_pre, after):
    return call(
        outer_near_kernel, (hat, vectors, d_mixed, d_pre), [shape(1024, 1792, BF)],
        ins=[SLOW, FAST, SLOW, SLOW], to=SLOW,
        scratch=[
            pltpu.VMEM((LENGTH, 1024), BF), pltpu.VMEM((LENGTH, 768), BF),
            pltpu.VMEM((LENGTH, 1024), BF), pltpu.VMEM((1024, 1792), BF),
            pltpu.SemaphoreType.DMA((12,)),
        ],
        cost=(2 * LENGTH * 1024 * 1792, 0), name="outer_near", after=after,
    )


def add_sums_kernel(whole, sums, *refs):
    out = refs[-1]
    row = lax.broadcasted_iota(jnp.int32, out.shape, 0)
    total = sums[...]
    for got, all_rows in zip(refs, whole):
        total = total + (got[...] if all_rows else jnp.where(row == BIASES, 0.0, got[...]))
    out[...] = total


def add_sums(sums, got, whole, after):
    return call(
        functools.partial(add_sums_kernel, whole), (sums, *got), [shape(8, D, F32)],
        name="add_sums", after=after,
    )


def finish_out_kernel(me, x, summed, b_dense, b_out, out):
    for k in range(16):
        to = feature_cols(me, k)
        value = x[:, to].astype(F32) + summed[:, fixed_cols(k)].astype(F32)
        out[:, to] = (value + b_dense[:, to] + b_out[:, to]).astype(BF)


def finish_out(me, *args, after):
    return call(
        finish_out_kernel, (me, *args), [shape(LANE, D, BF)], ins=[SCALAR] + [FAST] * 4,
        name="finish_out", after=after,
    )


def finish_grad_kernel(me, x, g, u, out):
    centre = jnp.mean(x[...].astype(F32), axis=-1, keepdims=True)
    rate = centred(x[...])[1]
    total = u[...].astype(F32)
    mean = jnp.mean(total, axis=-1, keepdims=True)
    spread = jnp.zeros((LANE, 1), F32)
    for k in range(16):
        hat = x[:, feature_cols(me, k)].astype(F32) - centre
        spread += jnp.sum(total[:, fixed_cols(k)] * hat, axis=-1, keepdims=True)
    spread = spread * rate * rate * (1.0 / D)
    for k in range(16):
        to = feature_cols(me, k)
        hat = x[:, to].astype(F32) - centre
        back = rate * (total[:, fixed_cols(k)] - mean - hat * spread)
        out[:, to] = (g[:, to].astype(F32) + back).astype(BF)


def finish_grad(me, *args, after):
    return call(
        finish_grad_kernel, (me, *args), [shape(LANE, D, BF)], ins=[SCALAR] + [FAST] * 3,
        name="finish_grad", after=after,
    )


def finish_weights_kernel(cut, flip, near, far, swapped, up, down, one, two, held, sems):
    copies = Copies(sems)
    begun = [
        copies.start(source.at[:LANE, :], held.at[k * LANE : (k + 1) * LANE, :])
        for k, source in enumerate((near, far, swapped, up, down))
    ]
    wait(begun)
    total = held[:LANE, :].astype(F32)
    for k in range(1, 5):
        total = total + held[k * LANE : (k + 1) * LANE, :].astype(F32)
    first, second = total[:, :cut], total[:, cut:]
    one[...] = first.T if flip else first
    two[...] = second.T if flip else second


def finish_weights(near, far, got, cut, flip, after=()):
    cols = near.shape[1]
    sizes = [(LANE, cut), (LANE, cols - cut)]
    outs = [shape(b, a, F32) if flip else shape(a, b, F32) for a, b in sizes]
    return call(
        functools.partial(finish_weights_kernel, cut, flip), (near, far, *got), outs, ins=SLOW,
        scratch=[pltpu.VMEM((5 * LANE, cols), BF), pltpu.SemaphoreType.DMA((5,))],
        name="finish_weights", after=after,
    )


def per_device(
    hidden_in,
    segment_ids,
    ln1_gain,
    ln1_bias,
    ln2_gain,
    ln2_bias,
    w_qkv,
    b_qkv,
    w_dense,
    b_dense,
    w_in,
    b_in,
    w_out,
    b_out,
    cotangent,
):
    me = jnp.stack([lax.axis_index("dp"), lax.axis_index("tensor")]).astype(jnp.int32)
    row = lambda vector: vector[None, :]
    dp, tensor = dp_move, tensor_move

    own_hat, part_a, token = begin(me, hidden_in, w_qkv, w_in)
    hat = lax.all_gather(own_hat, "tensor", axis=0, tiled=True)
    got_a = gather_one(part_a, dp)
    more_a, token = gather_two(part_a, got_a, dp, (token,), "a_two")
    own_g, part_b, vectors, bias, g_sum, token = prepare(
        me, cotangent, w_dense, w_out, row(ln1_gain), row(ln1_bias), row(ln2_gain), row(ln2_bias),
        row(b_qkv), row(b_in), after=(token,),
    )
    all_g = lax.all_gather(own_g, "tensor", axis=0, tiled=True)
    other_b = dp(part_b, 0, 1)
    cosine, sine = angles(segment_ids)
    seg_col = jnp.broadcast_to(segment_ids[:, None], (LENGTH, LANE))
    seg_row = row(segment_ids)

    last_a, a0, token = gather_three(
        part_a, got_a, more_a, dp, (token, cosine, sine, seg_col), "a_three"
    )
    far_a0 = dp(a0, 0, 0, 1)
    a1, token = stage(last_a, ((row_set(0, 0, HALF), row_set(1, 0, HALF)),), after=(token,), name="a_four")
    far_a1 = dp(a1, 0, 0, 1)
    both_b, more_b, token = pair_two(part_b, other_b, dp, (token,), "b_two")
    near_a, far_a = (a0, a1), (far_a0, far_a1)
    mixed, context, log_total, token = attention(
        hat, near_a, far_a, vectors, bias, cosine, sine, seg_col, seg_row, (token,)
    )
    last_b, b0, token = pair_three(both_b, more_b, dp, (token,), "b_three")
    far_b0 = dp(b0, 0, 0, 1)
    hidden, slope, token = units(hat, near_a, far_a, vectors, bias[:, 768:], (token,))
    b1, token = stage(last_b, ((row_set(0, 0, LANE), row_set(1, 0, LANE)),), after=(token,), name="b_four")
    far_b1 = dp(b1, 0, 0, 1)
    near_b, far_b = (b0, b1), (far_b0, far_b1)
    out_part, token = output(context, hidden, near_b, far_b, (token,))
    summed = lax.psum_scatter(out_part, "tensor", scatter_dimension=0, tiled=True)

    grad_b_far, token = outer_b(all_g, context, hidden, 1024, (token,))
    got_far_b = dp(grad_b_far, 0, 0, 1)
    grad_b, token = outer_b(all_g, context, hidden, 0, (token,))
    chunks_b = (grad_b, got_far_b)
    step_b, token = pair_scatter_one(chunks_b, dp, (token,), "grad_b_one")
    d_mixed, d_pre, grad_a_far, sums_in, sums_qkv, token = backward(
        all_g, near_b, far_b, slope, mixed, hat, log_total, seg_col, seg_row, cosine, sine,
        vectors, (token,),
    )
    got_far_a = dp(grad_a_far, 0, 0, 1)
    step_b, token = pair_scatter_two(chunks_b, step_b, dp, (token,), "grad_b_two")
    u, sums, token = inputs_back(
        me, d_mixed, d_pre, near_a, far_a, hat, vectors, sums_qkv, sums_in, g_sum, (token,)
    )
    others = butterfly(sums, "dp", 0, 0, 1)
    u_rows = lax.psum_scatter(u, "tensor", scatter_dimension=0, tiled=True)
    grad_a, token = outer_near(hat, vectors, d_mixed, d_pre, (token,))
    chunks_a = (grad_a, got_far_a)
    *sends, token = stage(chunks_a, scatter_one(2), (token,), "grad_a_one")
    step_a = both_ways(sends, dp)
    step_b, token = pair_scatter_three(chunks_b, step_b, dp, (token,), "grad_b_three")
    sums, token = add_sums(sums, (others,), (True,), (token,))
    others = butterfly(sums, "dp", 1, 0)
    hidden_out, token = finish_out(
        me, hidden_in, summed, row(b_dense), row(b_out), after=(token,)
    )
    *sends, token = stage((*chunks_a, *step_a), scatter_two(2), (token,), "grad_a_two")
    step_a = both_ways(sends, dp)
    sums, token = add_sums(sums, (others,), (True,), (token,))
    others = butterfly(sums, "dp", 2, 0)
    *sends, token = stage((*chunks_a, *step_a), scatter_three(2), (token,), "grad_a_three")
    step_a = both_ways(sends, dp)
    sums, token = add_sums(sums, (others,), (True,), (token,))
    others = tuple(x_move(sums, step) for step in (1, 2, 3))
    grad_dense, grad_out, token = finish_weights(
        *chunks_b, (step_b[1], step_b[2], step_b[0]), DH, True, after=(token,)
    )
    sums, token = add_sums(sums, others, (False, True, False), (token,))
    others = tuple(tensor(sums, step, 0) for step in (1, 2, 3))
    grad_qkv, grad_in, token = finish_weights(*chunks_a, step_a, 768, False, after=(token,))
    grad_input, token = finish_grad(me, hidden_in, cotangent, u_rows, after=(token,))
    sums, token = add_sums(sums, others, (False, False, False), (token,))
    return (
        hidden_out,
        grad_input,
        sums[0],
        sums[1],
        sums[2],
        sums[3],
        grad_qkv,
        sums[5, :768],
        grad_dense,
        sums[4],
        grad_in,
        sums[5, 768:1792],
        grad_out,
        sums[4],
    )


def butterfly(value, axis, step, flip, core=0):
    pairs = []
    if axis == "dp":
        for y in range(4):
            for xh in range(2):
                for c in range(2):
                    pairs.append(
                        ((y * 2 + xh) * 2 + c, ((y ^ step) * 2 + (xh ^ flip)) * 2 + (c ^ core))
                    )
    else:
        for xl in range(2):
            for z in range(4):
                pairs.append((xl * 4 + z, (xl ^ flip) * 4 + (z ^ step)))
    return lax.ppermute(value, axis, pairs)


def solution(mesh):
    in_specs = (
        P(("dp", "tensor"), None),
        P("dp"),
        P(),
        P(),
        P(),
        P(),
        P("dp", "tensor"),
        P("tensor"),
        P("tensor", "dp"),
        P(),
        P("dp", "tensor"),
        P("tensor"),
        P("tensor", "dp"),
        P(),
        P(("dp", "tensor"), None),
    )
    out_specs = (
        P(("dp", "tensor"), None),
        P(("dp", "tensor"), None),
        P(),
        P(),
        P(),
        P(),
        P("dp", "tensor"),
        P("tensor"),
        P("tensor", "dp"),
        P(),
        P("dp", "tensor"),
        P("tensor"),
        P("tensor", "dp"),
        P(),
    )
    return jax.shard_map(
        per_device, mesh=mesh, in_specs=in_specs, out_specs=out_specs, check_vma=False
    )
```

```python
import functools
import math

import jax
import jax.numpy as jnp
from jax import lax
from jax.experimental import pallas as pl
from jax.experimental.pallas import tpu as pltpu
from jax.sharding import PartitionSpec as P

DH = 256
ROT = 64
LENGTH = 1024
D = 2048
LANE = 128
HALF = 64

EPS = 1e-05
NEG = -1e30
BF = jnp.bfloat16
F32 = jnp.float32

ORDER = ((0, 0), (0, 1), (3, 0), (1, 0), (3, 1), (2, 0), (1, 1), (2, 1))
ROOM = 64 * 1024 * 1024 - 128 * 1024
TILE = 256
SCALE = DH**-0.5
BIASES = 8
QUARTER = LENGTH // 4
QUARTERS = tuple((n * QUARTER, (n + 1) * QUARTER) for n in range(4))
FAST, SLOW, SCALAR = pltpu.VMEM, pltpu.HBM, pltpu.SMEM


def dp_pairs(step, flip, core):
    pairs = []
    for y in range(4):
        for xh in range(2):
            for c in range(2):
                pairs.append(
                    ((y * 2 + xh) * 2 + c, (((y + step) % 4) * 2 + (xh ^ flip)) * 2 + (c ^ core))
                )
    return pairs


def tensor_pairs(step, flip):
    return [(xl * 4 + z, (xl ^ flip) * 4 + (z + step) % 4) for xl in range(2) for z in range(4)]


def dp_move(value, step, flip, core=0):
    return lax.ppermute(value, "dp", dp_pairs(step, flip, core))


def tensor_move(value, step, flip):
    return lax.ppermute(value, "tensor", tensor_pairs(step, flip))


def shape(rows, cols, dtype):
    return jax.ShapeDtypeStruct((rows, cols), dtype)


class Copies:
    def __init__(self, sems):
        self.sems, self.count = sems, 0

    def start(self, source, target):
        copy = pltpu.make_async_copy(source, target, self.sems.at[self.count])
        self.count += 1
        copy.start()
        return copy


def wait(copies):
    for copy in copies:
        copy.wait()


def call(
    body, args, outs, ins=FAST, to=FAST, scratch=(), cost=(0, 0), name=None, after=(), carry=()
):
    moved = sum(math.prod(a.shape) * a.dtype.itemsize for a in (*args, *outs))
    count, given = len(args), len(args) + len(after) + len(carry)
    end = given + len(outs)
    ins = [ins] * count if not isinstance(ins, (tuple, list)) else list(ins)
    to = [to] * len(outs) if not isinstance(to, (tuple, list)) else list(to)
    fast_in = [i for i, w in enumerate(ins) if w is FAST]
    fast_out = [i for i, w in enumerate(to) if w is FAST]
    held = [pltpu.VMEM(args[i].shape, args[i].dtype) for i in fast_in]
    held += [pltpu.VMEM(outs[i].shape, outs[i].dtype) for i in fast_out]
    held += [pltpu.VMEM((8, LANE), F32), pltpu.SemaphoreType.DMA((len(fast_in) + len(fast_out) + 1,))]

    def run(*refs):
        refs = list(refs)
        given_refs, out_refs, token, rest = refs[:count], refs[given:end], refs[end], refs[end + 1 + len(carry) :]
        own, rest = rest[: len(held)], rest[len(held) :]
        copies = Copies(own[-1])
        begun = []
        for slot, i in enumerate(fast_in):
            begun.append(copies.start(given_refs[i], own[slot]))
            given_refs[i] = own[slot]
        targets = list(out_refs)
        for slot, i in enumerate(fast_out):
            out_refs[i] = own[len(fast_in) + slot]
        own[-2][...] = jnp.zeros((8, LANE), F32)
        last = [copies.start(own[-2], token)]
        wait(begun)
        body(*given_refs, *out_refs, *rest)
        for i in fast_out:
            last.append(copies.start(out_refs[i], targets[i]))
        wait(last)

    where = lambda w: pl.BlockSpec(memory_space=SCALAR if w is SCALAR else SLOW)
    return pl.pallas_call(
        run,
        in_specs=[where(w) for w in ins] + [where(SLOW)] * (len(after) + len(carry)),
        out_specs=[where(SLOW)] * (len(outs) + 1 + len(carry)),
        out_shape=[*outs, shape(8, LANE, F32), *(shape(*c.shape, c.dtype) for c in carry)],
        input_output_aliases={
            count + len(after) + k: len(outs) + 1 + k for k in range(len(carry))
        },
        scratch_shapes=[*held, *scratch],
        compiler_params=pltpu.CompilerParams(vmem_limit_bytes=ROOM),
        cost_estimate=pl.CostEstimate(
            flops=1, transcendentals=0, bytes_accessed=1
        ),
        name=name,
    )(*args, *after, *carry)


def stage_kernel(groups, counts, *refs):
    refs = list(refs)
    arrays = [[refs.pop(0) for _ in range(count)] for count in counts]
    outs = [[refs.pop(0) for _ in parts] for parts in groups]
    held = [refs.pop(0) for _ in groups]
    copies = Copies(refs.pop(0))
    segments = []
    for parts, given, made, room in zip(groups, arrays, outs, held):
        at = 0
        for out, part in zip(made, parts):
            to = 0
            for rows, terms in part:
                places, begun = [], []
                for index, start in terms:
                    source = given[index].at[start : start + rows, :]
                    begun.append(copies.start(source, room.at[at : at + rows, :]))
                    places.append(at)
                    at += rows
                segments.append((out.at[to : to + rows, :], room, rows, places, begun))
                to += rows
    pending = []
    for target, room, rows, places, begun in segments:
        wait(begun)
        if len(places) > 1 and room.dtype == F32:
            total = room[places[0] : places[0] + rows, :]
            for place in places[1:]:
                total = total + room[place : place + rows, :]
            room[places[0] : places[0] + rows, :] = total
        elif len(places) > 1:

            def add(i, carry, room=room, places=places):
                where = [pl.ds(pl.multiple_of(place + i * 16, 16), 16) for place in places]
                total = room[where[0], :].astype(F32)
                for one in where[1:]:
                    total = total + room[one, :].astype(F32)
                room[where[0], :] = total.astype(BF)
                return carry

            lax.fori_loop(0, rows // 16, add, 0)
        pending.append(copies.start(room.at[places[0] : places[0] + rows, :], target))
    wait(pending)


def stages(groups, after=(), name="stage", carry=()):
    scratch, outs = [], []
    for arrays, parts in groups:
        cols, kind = arrays[0].shape[1], arrays[0].dtype
        rows = sum(r * len(t) for part in parts for r, t in part)
        scratch.append(pltpu.VMEM((rows, cols), kind))
        outs += [shape(sum(r for r, _ in part), cols, kind) for part in parts]
    copies = sum(len(t) + 1 for _, parts in groups for part in parts for _, t in part)
    made = call(
        functools.partial(
            stage_kernel, tuple(g[1] for g in groups), tuple(len(g[0]) for g in groups)
        ),
        tuple(array for arrays, _ in groups for array in arrays),
        outs,
        ins=SLOW,
        to=SLOW,
        scratch=[*scratch, pltpu.SemaphoreType.DMA((copies,))],
        name=name,
        after=after,
        carry=carry,
    )
    split = []
    for _, parts in groups:
        split.append(made[: len(parts)])
        made = made[len(parts) :]
    return (*split, *made)


def stage(arrays, parts, after=(), name="stage"):
    made, token = stages(((arrays, parts),), after, name)
    return (*made, token)


def row_set(index, start, rows):
    return (rows, ((index, start),))


def gather_one(block, move):
    return move(block, 0, 1), move(block, 1, 0), move(block, -1, 0)


def gather_two(block, got, move, after, name):
    parts = (
        (row_set(1, 0, LANE), row_set(2, 0, HALF)),
        (row_set(3, HALF, HALF), row_set(1, 0, LANE)),
    )
    up, down, token = stage((block, *got), parts, after=after, name=name)
    return (move(up, 1, 0), move(down, -1, 0)), token


def gather_three(block, first, got, move, after, name):
    joined = tuple((n, ((2 + k, 0),)) for k, n in enumerate((LANE,) * 4)) + (
        row_set(0, 0, 192),
        row_set(1, 0, 192),
    )
    parts = ((row_set(0, 0, HALF),), (row_set(1, LANE, HALF),), joined)
    up, down, joined, token = stage((*got, block, *first), parts, after=after, name=name)
    return (move(up, 1, 0), move(down, -1, 0)), joined, token


def pair_two(block, other, move, after, name):
    both, token = stage((block, other), ((row_set(0, 0, LANE), row_set(1, 0, LANE)),), after=after, name=name)
    return both, (move(both, 1, 0), move(both, -1, 0)), token


def pair_three(both, got, move, after, name):
    parts = (
        (row_set(0, 0, HALF), row_set(0, LANE, HALF)),
        (row_set(1, HALF, HALF), row_set(1, LANE + HALF, HALF)),
        (row_set(2, 0, 2 * LANE), row_set(0, 0, 2 * LANE), row_set(1, 0, 2 * LANE)),
    )
    up, down, joined, token = stage((*got, both), parts, after=after, name=name)
    return (move(up, 1, 0), move(down, -1, 0)), joined, token


def sums_of(count, start):
    return tuple((k, start) for k in range(count))


def scatter_one(n):
    return (((HALF, sums_of(n, 7 * LANE)),), ((HALF, sums_of(n, 7 * LANE + HALF)),))


def scatter_two(n):
    add = lambda start: sums_of(n, start)
    return (
        (
            (HALF, (*add(6 * LANE), (n, 0))),
            (HALF, add(6 * LANE + HALF)),
            (HALF, add(5 * LANE)),
        ),
        (
            (HALF, add(5 * LANE + HALF)),
            (HALF, add(4 * LANE)),
            (HALF, (*add(4 * LANE + HALF), (n + 1, 0))),
        ),
    )


def scatter_three(n):
    add = lambda start: sums_of(n, start)
    return (
        ((HALF, (*add(3 * LANE), (n, LANE))), (HALF, add(3 * LANE + HALF))),
        ((HALF, add(2 * LANE)), (HALF, (*add(2 * LANE + HALF), (n + 1, 0)))),
        ((LANE, (*add(LANE), (n, 0), (n + 1, HALF))),),
    )


def pair_scatter_one(n):
    add = lambda start: sums_of(n, start)
    return (
        ((HALF, add(5 * LANE)), (HALF, add(7 * LANE))),
        ((HALF, add(5 * LANE + HALF)), (HALF, add(7 * LANE + HALF))),
    )


def pair_scatter_two(n):
    add = lambda start: sums_of(n, start)
    return (
        (
            (HALF, (*add(3 * LANE), (n, 0))),
            (HALF, add(3 * LANE + HALF)),
            (HALF, (*add(6 * LANE), (n, HALF))),
            (HALF, add(6 * LANE + HALF)),
        ),
        (
            (HALF, add(2 * LANE)),
            (HALF, (*add(2 * LANE + HALF), (n + 1, 0))),
            (HALF, add(4 * LANE)),
            (HALF, (*add(4 * LANE + HALF), (n + 1, HALF))),
        ),
    )


def pair_scatter_three(n):
    return (((LANE, (*sums_of(n, LANE), (n, LANE), (n + 1, LANE))),),)


ADD_ALL = (((16, ((0, 0), (1, 0))),),)
ADD_SHARED = (((8, ((0, 0), (1, 0))), (8, ((0, 8),))),)
ADD_THREE_SHARED = (((8, ((0, 0), (1, 0), (2, 0), (3, 0))), (8, ((0, 8),))),)


def both_ways(sends, move):
    got = [move(sends[0], 1, 0), move(sends[1], -1, 0)]
    return (*got, *(move(send, 0, 1) for send in sends[2:]))


def feature_place(me, k):
    dp = me[0]
    dy, dx = ORDER[k % 8]
    y, xh, c = lax.shift_right_logical(dp, 2), lax.shift_right_logical(dp, 1) & 1, dp & 1
    return ((((y + dy) & 3) * 2 + (xh ^ dx)) * 2) + (c ^ (k // 8))


def token_place(me, k):
    at = me[1]
    dz, dx = ORDER[k]
    return (lax.shift_right_logical(at, 2) ^ dx) * 4 + (((at & 3) + dz) & 3)


def feature_cols(me, k):
    return pl.ds(pl.multiple_of(feature_place(me, k) * LANE, LANE), LANE)


def fixed_cols(k):
    return slice(k * LANE, (k + 1) * LANE)


def token_rows(me, k, count=LANE, offset=0):
    return pl.ds(pl.multiple_of(token_place(me, k) * LANE + offset, HALF), count)


def centred(rows):
    rows = rows.astype(F32)
    rows = rows - jnp.mean(rows, axis=-1, keepdims=True)
    return rows, lax.rsqrt(jnp.mean(rows * rows, axis=-1, keepdims=True) + EPS)


def begin_kernel(me, x, w_qkv, w_in, hat, part_a, held):
    rows, rate = centred(x[...])
    held[...] = rows * rate
    for k in range(16):
        hat[:, fixed_cols(k)] = held[:, feature_cols(me, k)].astype(BF)
    part_a[:, :768] = w_qkv[...]
    part_a[:, 768:] = w_in[...]


def begin(me, x, w_qkv, w_in):
    return call(
        begin_kernel, (me, x, w_qkv, w_in), [shape(LANE, D, BF), shape(LANE, 1792, BF)],
        ins=[SCALAR] + [FAST] * 3, scratch=[pltpu.VMEM((LANE, D), F32)], name="begin",
    )


def prepare_kernel(
    me, g, w_dense, w_out, g1, b1, g2, b2, b_qkv, b_in, near_g, part_b, vectors, bias, g_sum
):
    for k in range(16):
        to, at = fixed_cols(k), feature_cols(me, k)
        near_g[:, to] = g[:, at]
        for n, vector in enumerate((g1, b1, g2, b2)):
            vectors[n : n + 1, to] = vector[:, at]
    part_b[:, :DH] = w_dense[...].T
    part_b[:, DH:] = w_out[...].T
    bias[:, :768] = b_qkv[...]
    bias[:, 768:] = b_in[...]
    g_sum[...] = jnp.sum(g[...].astype(F32), axis=0, keepdims=True)


def prepare(me, *args, after):
    return call(
        prepare_kernel, (me, *args),
        [
            shape(LANE, D, BF), shape(LANE, 1280, BF), shape(4, D, F32), shape(1, 1792, F32), shape(1, D, F32),
        ],
        ins=[SCALAR] + [FAST] * len(args), name="prepare", after=after,
    )


def positions(segment):
    count = segment.shape[0]
    index = jnp.arange(count, dtype=jnp.int32)
    change = jnp.concatenate([jnp.ones((1,), dtype=bool), segment[1:] != segment[:-1]])
    start = lax.cummax(jnp.where(change, index, jnp.zeros_like(index)), axis=0)
    return index - start


def angles(segment):
    lane = jnp.arange(LANE, dtype=jnp.int32)
    exponent = (lane % (ROT // 2)).astype(F32) * (2.0 / ROT)
    inverse = jnp.where(lane < ROT, jnp.exp(-exponent * math.log(10000.0)), 0.0)
    angle = positions(segment).astype(F32)[:, None] * inverse[None, :]
    return jnp.cos(angle), jnp.sin(angle)


def dot(a, b, ca, cb):
    return lax.dot_general(a, b, (((ca,), (cb,)), ((), ())), preferred_element_type=F32)


def turn(head, cosine, sine):
    lane = lax.broadcasted_iota(jnp.int32, head.shape, 1)
    ahead = pltpu.roll(head, LANE - ROT // 2, 1)
    behind = pltpu.roll(head, ROT // 2, 1)
    return head * cosine + jnp.where(lane < ROT // 2, -ahead, behind) * sine


def masked_scores(q, k, seg_col, seg_row, first):
    scores = dot(q, k, 1, 1)
    row = first + lax.broadcasted_iota(jnp.int32, scores.shape, 0)
    col = lax.broadcasted_iota(jnp.int32, scores.shape, 1)
    allowed = (seg_col == seg_row) & (row >= col)
    return jnp.where(allowed, scores, NEG)


def load_weights(copies, pairs, cols, shift=0):
    place = slice(cols.start - shift, cols.stop - shift)
    started = []
    for pieces, layout, held in pairs:
        for piece, start, rows, block, offset in layout:
            at = block * LANE + offset
            started.append(
                copies.start(
                    pieces[piece].at[start : start + rows, cols], held.at[at : at + rows, place]
                )
            )
    return started


JOINED_PAIR = (
    (0, 0, 128, 0, 0),
    (0, 128, 128, 1, 0),
    (0, 256, 128, 2, 0),
    (0, 384, 128, 4, 0),
    (0, 512, 128, 3, 0),
    (0, 640, 128, 6, 0),
    (1, 0, 64, 5, 0),
    (1, 64, 64, 7, 0),
    (1, 128, 64, 5, 64),
    (1, 192, 64, 7, 64),
)
JOINED = ((0, 0, 896, 0, 0), (1, 0, 128, 7, 0))


def weighted(norm, own, other, bias, lo, hi, at):
    half = D // 2
    return (
        dot(norm[lo:hi, :half], own[:, at : at + TILE], 1, 0)
        + dot(norm[lo:hi, half:], other[:, at : at + TILE], 1, 0)
        + bias[:, at : at + TILE]
    )


def normed(hat, vectors, norm, lo, hi, k):
    x = hat[lo:hi, :].astype(F32)
    norm[lo:hi, :] = (x * vectors[k : k + 1, :] + vectors[k + 1 : k + 2, :]).astype(BF)


def attention_kernel(*refs):
    hat_hbm, near, far = refs[0], refs[1:3], refs[3:5]
    vectors, bias, cosine, sine, seg_col, seg_row = refs[5:11]
    mixed_out, context, log_total = refs[11:14]
    hat, own, other, norm, mixed, sems = refs[14:]
    copies = Copies(sems)
    pairs = ((near, JOINED, own), (far, JOINED, other))
    first = load_weights(copies, pairs, slice(0, TILE))
    rows = [copies.start(hat_hbm.at[lo:hi, :], hat.at[lo:hi, :]) for lo, hi in QUARTERS]
    second = load_weights(copies, pairs, slice(TILE, 3 * TILE))
    wait(first)
    for i in range(3):
        if i == 1:
            wait(second)
        for n, (lo, hi) in enumerate(QUARTERS):
            if i == 0:
                wait(rows[n : n + 1])
                normed(hat, vectors, norm, lo, hi, 0)
            acc = weighted(norm, own, other, bias, lo, hi, i * TILE)
            if i < 2:
                head = turn(acc[:, :LANE], cosine[lo:hi, :], sine[lo:hi, :])
                acc = jnp.concatenate([head, acc[:, LANE:]], axis=1)
            if i == 0:
                acc = acc * SCALE
            mixed[lo:hi, i * TILE : (i + 1) * TILE] = acc.astype(BF)
    saved = [copies.start(mixed, mixed_out)]
    for lo, hi in QUARTERS:
        scores = masked_scores(
            mixed[lo:hi, :DH], mixed[:hi, DH : 2 * DH], seg_col[lo:hi, :1], seg_row[:, :hi], lo
        )
        top = jnp.max(scores, axis=-1, keepdims=True)
        weights = jnp.exp(scores - top)
        total = jnp.sum(weights, axis=-1, keepdims=True)
        log_total[lo:hi, :] = jnp.broadcast_to(top + jnp.log(total), (hi - lo, LANE))
        probs = (weights * (1.0 / total)).astype(BF)
        context[lo:hi, :] = dot(probs, mixed[:hi, 2 * DH :], 1, 0).astype(BF)
    wait(saved)


def attention(hat, near, far, vectors, bias, cosine, sine, seg_col, seg_row, after):
    return call(
        attention_kernel,
        (hat, *near, *far, vectors, bias, cosine, sine, seg_col, seg_row),
        [shape(LENGTH, 768, BF), shape(LENGTH, DH, BF), shape(LENGTH, LANE, F32)],
        ins=[SLOW] * 5 + [FAST] * 6,
        to=[SLOW, FAST, FAST],
        scratch=[
            pltpu.VMEM((LENGTH, D), BF), pltpu.VMEM((1024, 768), BF),
            pltpu.VMEM((1024, 768), BF), pltpu.VMEM((LENGTH, D), BF),
            pltpu.VMEM((LENGTH, 768), BF), pltpu.SemaphoreType.DMA((16,)),
        ],
        cost=(2 * LENGTH * D * 768 + 4 * LENGTH * LENGTH * DH, LENGTH * 1024),
        name="attention", after=after,
    )


def units_kernel(*refs):
    hat_hbm, near, far, vectors, bias = refs[0], refs[1:3], refs[3:5], refs[5], refs[6]
    hidden_out, slope_out, hat, own, other, norm, hidden, slope, sems = refs[7:]
    copies = Copies(sems)
    pairs = ((near, JOINED, own), (far, JOINED, other))
    rows = [copies.start(hat_hbm.at[lo:hi, :], hat.at[lo:hi, :]) for lo, hi in QUARTERS]
    tiles = [load_weights(copies, pairs, slice(768 + i * TILE, 768 + (i + 1) * TILE), 768) for i in range(4)]
    saved = []
    for i in range(4):
        wait(tiles[i])
        cols = slice(i * TILE, (i + 1) * TILE)
        for n, (lo, hi) in enumerate(QUARTERS):
            if i == 0:
                wait(rows[n : n + 1])
                normed(hat, vectors, norm, lo, hi, 2)
            pre = weighted(norm, own, other, bias, lo, hi, i * TILE)
            cdf = 0.5 * (1.0 + lax.erf(pre * (0.5**0.5)))
            hidden[lo:hi, cols] = (pre * cdf).astype(BF)
            density = jnp.exp(-0.5 * pre * pre) * (1.0 / math.sqrt(2.0 * math.pi))
            slope[lo:hi, cols] = (cdf + pre * density).astype(BF)
        saved.append(copies.start(hidden.at[:, cols], hidden_out.at[:, cols]))
        saved.append(copies.start(slope.at[:, cols], slope_out.at[:, cols]))
    wait(saved)


def units(hat, near, far, vectors, bias, after):
    return call(
        units_kernel, (hat, *near, *far, vectors, bias), [shape(LENGTH, 1024, BF)] * 2,
        ins=[SLOW] * 5 + [FAST] * 2, to=SLOW,
        scratch=[
            pltpu.VMEM((LENGTH, D), BF), pltpu.VMEM((1024, 1024), BF),
            pltpu.VMEM((1024, 1024), BF), pltpu.VMEM((LENGTH, D), BF),
            pltpu.VMEM((LENGTH, 1024), BF), pltpu.VMEM((LENGTH, 1024), BF),
            pltpu.SemaphoreType.DMA((32,)),
        ],
        cost=(2 * LENGTH * D * 1024, LENGTH * 2048), name="units", after=after,
    )


def outer_b_kernel(first, g, context, hidden, grad_hbm, left, held_c, held_h, grad, sems):
    copies = Copies(sems)
    begun = [copies.start(context, held_c), copies.start(hidden, held_h)]
    tiles = load_tiles(copies, g, left, first)
    wait(begun)
    done = []
    for i in range(4):
        cols = slice(i * TILE, (i + 1) * TILE)
        wait(tiles[i : i + 1])
        grad[cols, :DH] = dot(left[:, cols], held_c[...], 0, 0).astype(BF)
        grad[cols, DH:] = dot(left[:, cols], held_h[...], 0, 0).astype(BF)
        done.append(copies.start(grad.at[cols, :], grad_hbm.at[cols, :]))
    wait(done)


def outer_b(g, context, hidden, first, after):
    return call(
        functools.partial(outer_b_kernel, first), (g, context, hidden), [shape(1024, 1280, BF)],
        ins=SLOW, to=SLOW,
        scratch=[
            pltpu.VMEM((LENGTH, 1024), BF), pltpu.VMEM((LENGTH, DH), BF),
            pltpu.VMEM((LENGTH, 1024), BF), pltpu.VMEM((1024, 1280), BF),
            pltpu.SemaphoreType.DMA((12,)),
        ],
        cost=(2 * LENGTH * 1024 * 1280, 0), name="outer_b", after=after,
    )


def output_kernel(*refs):
    context, hidden, near, far = refs[0], refs[1], refs[2:4], refs[4:6]
    out_hbm, held_c, held_h, own, other, out, sems = refs[6:]
    copies = Copies(sems)
    firsts = load_weights(copies, ((near, JOINED_PAIR[:2], own),), slice(0, 1280))
    begun = [copies.start(context, held_c), copies.start(hidden, held_h)]
    nears = load_weights(copies, ((near, JOINED_PAIR[2:], own),), slice(0, 1280))
    fars = load_weights(copies, ((far, JOINED_PAIR, other),), slice(0, 1280))
    wait(firsts + begun)
    done = []
    for i in range(8):
        held = own if i < 4 else other
        at = i % 4 * TILE
        cols = slice(i * TILE, (i + 1) * TILE)
        if i == 1:
            wait(nears)
        if i == 4:
            wait(fars)
        for lo, hi in QUARTERS:
            out[lo:hi, cols] = (
                dot(held_c[lo:hi, :], held[at : at + TILE, :DH], 1, 1)
                + dot(held_h[lo:hi, :], held[at : at + TILE, DH:], 1, 1)
            ).astype(BF)
        if i % 2:
            pair = slice((i - 1) * TILE, (i + 1) * TILE)
            done.append(copies.start(out.at[:, pair], out_hbm.at[:, pair]))
    wait(done)


def output(context, hidden, near, far, after):
    return call(
        output_kernel, (context, hidden, *near, *far), [shape(LENGTH, D, BF)], ins=SLOW, to=SLOW,
        scratch=[
            pltpu.VMEM((LENGTH, DH), BF), pltpu.VMEM((LENGTH, 1024), BF),
            pltpu.VMEM((1024, 1280), BF), pltpu.VMEM((1024, 1280), BF),
            pltpu.VMEM((LENGTH, D), BF), pltpu.SemaphoreType.DMA((28,)),
        ],
        cost=(2 * LENGTH * D * 1280, 0), name="output", after=after,
    )


def down_sums(value):
    total = value[:, :LANE]
    for k in range(1, value.shape[1] // LANE):
        total = total + value[:, fixed_cols(k)]
    return jnp.sum(total.T, axis=0, keepdims=True)


def column(row):
    parts = [jnp.broadcast_to(row[:, fixed_cols(k)], (LANE, LANE)).T for k in range(2)]
    return jnp.concatenate(parts, axis=0)


def backward_kernel(me, *refs):
    g, near, far = refs[0], refs[1:3], refs[3:5]
    slope_hbm, mixed_hbm, hat_hbm, near_a, far_a = refs[5], refs[6], refs[7], refs[8:10], refs[10:12]
    log_total, seg_col, seg_row, cosine, sine, vectors, g_sum = refs[12:19]
    mixed_grad_hbm, pre_hbm, grad_far_hbm, grad_near_hbm, sums = refs[19:24]
    held, own, other, slope, mixed, hat, own_a, other_a, d_context = refs[24:33]
    d_pre, d_mixed, d_k, d_v, grad, sum_qkv, sum_in, sems = refs[33:]
    half = D // 2
    copies = Copies(sems)
    pairs = ((near, JOINED_PAIR, own), (far, JOINED_PAIR, other))
    first = load_weights(copies, pairs, slice(0, TILE))
    rows = [copies.start(g.at[lo:hi, :], held.at[lo:hi, :]) for lo, hi in QUARTERS]
    rest = load_weights(copies, pairs, slice(TILE, 1280))
    slopes = [copies.start(slope_hbm, slope)]
    mixes = [copies.start(mixed_hbm, mixed)]
    hats = {}
    for i in (4, 5, 6, 7, 0, 1, 2, 3):
        cols = slice(i * TILE, (i + 1) * TILE)
        hats[i] = copies.start(hat_hbm.at[:, cols], hat.at[:, cols])
    inputs = load_weights(copies, ((far_a, JOINED, other_a),), slice(0, 1792))
    inputs += load_weights(copies, ((near_a, JOINED, own_a),), slice(0, 1792))
    done = []

    def product(lo, hi, cols):
        return dot(held[lo:hi, :half], own[:, cols], 1, 0) + dot(held[lo:hi, half:], other[:, cols], 1, 0)

    wait(first)
    for n, (lo, hi) in enumerate(QUARTERS):
        wait(rows[n : n + 1])
        d_context[lo:hi, :] = product(lo, hi, slice(0, TILE)).astype(BF)
    wait(rest + slopes)
    for i in range(4):
        cols = slice(i * TILE, (i + 1) * TILE)
        total = jnp.zeros((1, TILE), F32)
        for lo, hi in QUARTERS:
            acc = product(lo, hi, slice((i + 1) * TILE, (i + 2) * TILE))
            rounded = (acc * slope[lo:hi, cols].astype(F32)).astype(BF)
            d_pre[lo:hi, cols] = rounded
            total += jnp.sum(rounded.astype(F32), axis=0, keepdims=True)
        sum_in[:, cols] = total
    done.append(copies.start(d_pre, pre_hbm))

    wait(mixes)
    d_k[...] = jnp.zeros_like(d_k)
    d_v[...] = jnp.zeros_like(d_v)

    def back(lo, hi, value):
        head = turn(value[:, :LANE], cosine[lo:hi, :], -sine[lo:hi, :])
        return jnp.concatenate([head, value[:, LANE:]], axis=1)

    for lo, hi in QUARTERS:
        q, k, v = mixed[lo:hi, :DH], mixed[:hi, DH : 2 * DH], mixed[:hi, 2 * DH :]
        dc = d_context[lo:hi, :]
        scores = masked_scores(q, k, seg_col[lo:hi, :1], seg_row[:, :hi], lo)
        probs = jnp.exp(scores - log_total[lo:hi, :1])
        d_probs = dot(dc, v, 1, 1)
        spread = jnp.sum(probs * d_probs, axis=-1, keepdims=True)
        d_scores = (probs * (d_probs - spread)).astype(BF)
        d_mixed[lo:hi, :DH] = (back(lo, hi, dot(d_scores, k, 1, 0)) * SCALE).astype(BF)
        d_k[:hi, :] += dot(d_scores, q, 0, 0)
        d_v[:hi, :] += dot(probs.astype(BF), dc, 0, 0)
    total = jnp.zeros((1, 768), F32)
    for lo, hi in QUARTERS:
        d_mixed[lo:hi, DH : 2 * DH] = back(lo, hi, d_k[lo:hi, :]).astype(BF)
        d_mixed[lo:hi, 2 * DH :] = d_v[lo:hi, :].astype(BF)
        total += jnp.sum(d_mixed[lo:hi, :].astype(F32), axis=0, keepdims=True)
    sum_qkv[...] = total
    done.append(copies.start(d_mixed, mixed_grad_hbm))
    sums[...] = jnp.zeros_like(sums)
    sums[4:5, :] = g_sum[...]
    sums[BIASES : BIASES + 1, :768] = sum_qkv[...]
    sums[BIASES : BIASES + 1, 768:1792] = sum_in[...]

    wait(inputs)
    parts = ((0, 768, d_mixed, sum_qkv), (768, 1792, d_pre, sum_in))
    for i in (4, 5, 6, 7, 0, 1, 2, 3):
        cols = slice(i * TILE, (i + 1) * TILE)
        out, weights = (grad_near_hbm, own_a) if i < 4 else (grad_far_hbm, other_a)
        at = slice(i % 4 * TILE, (i % 4 + 1) * TILE)
        wait([hats[i]])
        for n, (lo, hi, upstream, total) in enumerate(parts):
            plain = dot(hat[:, cols], upstream[...], 0, 0)
            gain, bias = (column(vectors[2 * n + k : 2 * n + k + 1, cols]) for k in range(2))
            w = weights[at, lo:hi].astype(F32)
            down = jnp.broadcast_to(total[...], plain.shape)
            for k in range((hi - lo) // LANE):
                lanes = fixed_cols(k)
                grad[cols, lo + k * LANE : lo + (k + 1) * LANE] = (
                    gain * plain[:, lanes] + bias * down[:, lanes]
                ).astype(BF)
            gain_row, bias_row = down_sums(w * plain), down_sums(w * down)
            for k in range(2):
                to = feature_cols(me, 2 * i + k)
                sums[2 * n : 2 * n + 1, to] = gain_row[:, fixed_cols(k)]
                sums[2 * n + 1 : 2 * n + 2, to] = bias_row[:, fixed_cols(k)]
        done.append(copies.start(grad.at[cols, :], out.at[at, :]))
    wait(done)


def backward(me, g, near, far, slope, mixed, hat, near_a, far_a, *rest, after):
    return call(
        backward_kernel,
        (me, g, *near, *far, slope, mixed, hat, *near_a, *far_a, *rest),
        [
            shape(LENGTH, 768, BF), shape(LENGTH, 1024, BF), shape(1024, 1792, BF),
            shape(1024, 1792, BF), shape(16, D, F32),
        ],
        ins=[SCALAR] + [SLOW] * 12 + [FAST] * 7, to=[SLOW] * 4 + [FAST],
        scratch=[
            pltpu.VMEM((LENGTH, D), BF), pltpu.VMEM((1024, 1280), BF),
            pltpu.VMEM((1024, 1280), BF), pltpu.VMEM((LENGTH, 1024), BF),
            pltpu.VMEM((LENGTH, 768), BF), pltpu.VMEM((LENGTH, D), BF),
            pltpu.VMEM((1024, 1792), BF), pltpu.VMEM((1024, 1792), BF),
            pltpu.VMEM((LENGTH, DH), BF), pltpu.VMEM((LENGTH, 1024), BF),
            pltpu.VMEM((LENGTH, 768), BF), pltpu.VMEM((LENGTH, DH), F32),
            pltpu.VMEM((LENGTH, DH), F32), pltpu.VMEM((D, 1792), BF),
            pltpu.VMEM((1, 768), F32), pltpu.VMEM((1, 1024), F32),
            pltpu.SemaphoreType.DMA((80,)),
        ],
        cost=(2 * LENGTH * (D * 1280 + D * 1792 + 5 * LENGTH * DH), LENGTH * LENGTH),
        name="backward", after=after,
    )


def inputs_back_kernel(*refs):
    mixed_hbm, pre_hbm, near, far, vectors = refs[0], refs[1], refs[2:4], refs[4:6], refs[6]
    u_hbm, d_mixed, d_pre, own, other, u, sems = refs[7:]
    copies = Copies(sems)
    loads = [[copies.start(near[0].at[:TILE, :], own.at[:TILE, :])]]
    begun = []
    for lo, hi in QUARTERS:
        begun.append(
            [
                copies.start(mixed_hbm.at[lo:hi, :], d_mixed.at[lo:hi, :]),
                copies.start(pre_hbm.at[lo:hi, :], d_pre.at[lo:hi, :]),
            ]
        )
    for i in range(1, 8):
        pieces, held = (near, own) if i < 4 else (far, other)
        at = i % 4 * TILE
        last = min(at + TILE, 896)
        loads.append([copies.start(pieces[0].at[at:last, :], held.at[at:last, :])])
        if last < at + TILE:
            loads[-1].append(copies.start(pieces[1], held.at[896:, :]))
    done = []
    for i in range(8):
        held = own if i < 4 else other
        at = i % 4 * TILE
        cols = slice(i * TILE, (i + 1) * TILE)
        wait(loads[i])
        for n, (lo, hi) in enumerate(QUARTERS):
            if i == 0:
                wait(begun[n])
            d1 = dot(d_mixed[lo:hi, :], held[at : at + TILE, :768], 1, 1)
            d2 = dot(d_pre[lo:hi, :], held[at : at + TILE, 768:], 1, 1)
            u[lo:hi, cols] = (d1 * vectors[0:1, cols] + d2 * vectors[2:3, cols]).astype(BF)
        if i % 2:
            pair = slice((i - 1) * TILE, (i + 1) * TILE)
            done.append(copies.start(u.at[:, pair], u_hbm.at[:, pair]))
    wait(done)


def inputs_back(d_mixed, d_pre, near, far, vectors, after):
    return call(
        inputs_back_kernel, (d_mixed, d_pre, *near, *far, vectors), [shape(LENGTH, D, BF)],
        ins=[SLOW] * 6 + [FAST], to=SLOW,
        scratch=[
            pltpu.VMEM((LENGTH, 768), BF), pltpu.VMEM((LENGTH, 1024), BF),
            pltpu.VMEM((1024, 1792), BF), pltpu.VMEM((1024, 1792), BF),
            pltpu.VMEM((LENGTH, D), BF), pltpu.SemaphoreType.DMA((24,)),
        ],
        cost=(2 * LENGTH * D * 1792, 0), name="inputs_back", after=after,
    )


def load_tiles(copies, source, held, first):
    return [
        copies.start(
            source.at[:, first + i * TILE : first + (i + 1) * TILE],
            held.at[:, i * TILE : (i + 1) * TILE],
        )
        for i in range(4)
    ]


def finish_out_kernel(me, x, summed, b_dense, b_out, out):
    for k in range(16):
        to = feature_cols(me, k)
        value = x[:, to].astype(F32) + summed[:, fixed_cols(k)].astype(F32)
        out[:, to] = (value + b_dense[:, to] + b_out[:, to]).astype(BF)


def finish_out(me, *args, after):
    return call(
        finish_out_kernel, (me, *args), [shape(LANE, D, BF)], ins=[SCALAR] + [FAST] * 4,
        name="finish_out", after=after,
    )


def finish_grad_kernel(me, x, g, u, out):
    centre = jnp.mean(x[...].astype(F32), axis=-1, keepdims=True)
    rate = centred(x[...])[1]
    total = u[...].astype(F32)
    mean = jnp.mean(total, axis=-1, keepdims=True)
    spread = jnp.zeros((LANE, 1), F32)
    for k in range(16):
        hat = x[:, feature_cols(me, k)].astype(F32) - centre
        spread += jnp.sum(total[:, fixed_cols(k)] * hat, axis=-1, keepdims=True)
    spread = spread * rate * rate * (1.0 / D)
    for k in range(16):
        to = feature_cols(me, k)
        hat = x[:, to].astype(F32) - centre
        back = rate * (total[:, fixed_cols(k)] - mean - hat * spread)
        out[:, to] = (g[:, to].astype(F32) + back).astype(BF)


def finish_grad(me, *args, after):
    return call(
        finish_grad_kernel, (me, *args), [shape(LANE, D, BF)], ins=[SCALAR] + [FAST] * 3,
        name="finish_grad", after=after,
    )


def total_of(copies, arrays, held):
    begun = [
        copies.start(source.at[:LANE, :], held.at[k * LANE : (k + 1) * LANE, :])
        for k, source in enumerate(arrays)
    ]

    def total():
        wait(begun)
        value = held[:LANE, :].astype(F32)
        for k in range(1, len(arrays)):
            value = value + held[k * LANE : (k + 1) * LANE, :].astype(F32)
        return value

    return total


def finish_a_kernel(*refs):
    arrays, (qkv, units, held, sems) = refs[:5], refs[5:]
    value = total_of(Copies(sems), arrays, held)()
    qkv[...] = value[:, :768]
    units[...] = value[:, 768:]


def finish_a(arrays, after):
    return call(
        finish_a_kernel, arrays, [shape(LANE, 768, F32), shape(LANE, 1024, F32)], ins=SLOW,
        scratch=[pltpu.VMEM((5 * LANE, 1792), BF), pltpu.SemaphoreType.DMA((5,))],
        name="finish_a", after=after,
    )


def finish_b_kernel(*refs):
    arrays, sums, got = refs[:5], refs[5], refs[6]
    dense, out, rows, qkv, units, held, sems = refs[7], refs[8], refs[9:15], *refs[15:]
    total = total_of(Copies(sems), arrays, held)
    for k, row in enumerate(rows):
        at = min(k, 4)
        row[...] = sums[at : at + 1, :] + got[at : at + 1, :]
    biases = sums[BIASES : BIASES + 1, :] + got[BIASES : BIASES + 1, :]
    qkv[...] = biases[:, :768]
    units[...] = biases[:, 768:1792]
    value = total()
    dense[...] = value[:, :DH].T
    out[...] = value[:, DH:].T


def finish_b(arrays, sums, got, after):
    return call(
        finish_b_kernel, (*arrays, sums, got),
        [
            shape(DH, LANE, F32), shape(1024, LANE, F32), *([shape(1, D, F32)] * 6),
            shape(1, 768, F32), shape(1, 1024, F32),
        ],
        ins=[SLOW] * 5 + [FAST] * 2,
        scratch=[pltpu.VMEM((5 * LANE, 1280), BF), pltpu.SemaphoreType.DMA((5,))],
        name="finish_b", after=after,
    )


def per_device(
    hidden_in,
    segment_ids,
    ln1_gain,
    ln1_bias,
    ln2_gain,
    ln2_bias,
    w_qkv,
    b_qkv,
    w_dense,
    b_dense,
    w_in,
    b_in,
    w_out,
    b_out,
    cotangent,
):
    me = jnp.stack([lax.axis_index("dp"), lax.axis_index("tensor")]).astype(jnp.int32)
    row = lambda vector: vector[None, :]
    dp, tensor = dp_move, tensor_move

    own_hat, part_a, token = begin(me, hidden_in, w_qkv, w_in)
    hat = lax.all_gather(own_hat, "tensor", axis=0, tiled=True)
    got_a = gather_one(part_a, dp)
    more_a, token = gather_two(part_a, got_a, dp, (token,), "a_two")
    own_g, part_b, vectors, bias, g_sum, token = prepare(
        me, cotangent, w_dense, w_out, row(ln1_gain), row(ln1_bias), row(ln2_gain), row(ln2_bias),
        row(b_qkv), row(b_in), after=(token,),
    )
    all_g = lax.all_gather(own_g, "tensor", axis=0, tiled=True)
    other_b = dp(part_b, 0, 1)
    cosine, sine = angles(segment_ids)
    seg_col = jnp.broadcast_to(segment_ids[:, None], (LENGTH, LANE))
    seg_row = row(segment_ids)

    last_a, a0, token = gather_three(
        part_a, got_a, more_a, dp, (token, cosine, sine, seg_col), "a_three"
    )
    far_a0 = dp(a0, 0, 0, 1)
    a1, token = stage(last_a, ((row_set(0, 0, HALF), row_set(1, 0, HALF)),), after=(token,), name="a_four")
    far_a1 = dp(a1, 0, 0, 1)
    both_b, more_b, token = pair_two(part_b, other_b, dp, (token,), "b_two")
    near_a, far_a = (a0, a1), (far_a0, far_a1)
    mixed, context, log_total, token = attention(
        hat, near_a, far_a, vectors, bias, cosine, sine, seg_col, seg_row, (token,)
    )
    last_b, b0, token = pair_three(both_b, more_b, dp, (token,), "b_three")
    far_b0 = dp(b0, 0, 0, 1)
    hidden, slope, token = units(hat, near_a, far_a, vectors, bias[:, 768:], (token,))
    b1, token = stage(last_b, ((row_set(0, 0, LANE), row_set(1, 0, LANE)),), after=(token,), name="b_four")
    far_b1 = dp(b1, 0, 0, 1)
    near_b, far_b = (b0, b1), (far_b0, far_b1)
    out_part, token = output(context, hidden, near_b, far_b, (token,))
    summed = lax.psum_scatter(out_part, "tensor", scatter_dimension=0, tiled=True)

    grad_b_far, token = outer_b(all_g, context, hidden, 1024, (token,))
    got_far_b = dp(grad_b_far, 0, 0, 1)
    grad_b, token = outer_b(all_g, context, hidden, 0, (token,))
    chunks_b = (grad_b, got_far_b)
    d_mixed, d_pre, grad_a_far, grad_a, sums, token = backward(
        me, all_g, near_b, far_b, slope, mixed, hat, near_a, far_a, log_total, seg_col, seg_row,
        cosine, sine, vectors, g_sum, after=(token,),
    )
    got_far_a = dp(grad_a_far, 0, 0, 1)
    others = tuple(tensor(sums, step, 0) for step in (1, 2, 3))
    u, token = inputs_back(d_mixed, d_pre, near_a, far_a, vectors, (token,))
    chunks_a = (grad_a, got_far_a)
    sends_a, sends_b, (sums,), token, u = stages(
        (
            (chunks_a, scatter_one(2)),
            (chunks_b, pair_scatter_one(2)),
            ((sums, *others), ADD_THREE_SHARED),
        ),
        (token,),
        "grads_one",
        (u,),
    )
    u_rows = lax.psum_scatter(u, "tensor", scatter_dimension=0, tiled=True)
    step_a, step_b = both_ways(sends_a, dp), both_ways(sends_b, dp)
    others = butterfly(sums, "tensor", 0, 1)
    hidden_out, token = finish_out(
        me, hidden_in, summed, row(b_dense), row(b_out), after=(token,)
    )
    sends, (sums,), token = stages(
        (((*chunks_a, *step_a), scatter_two(2)), ((sums, others), ADD_SHARED)),
        (token,),
        "grad_a_two",
    )
    step_a = both_ways(sends, dp)
    others = butterfly(sums, "dp", 0, 0, 1)
    sends, (sums,), token = stages(
        (((*chunks_b, *step_b), pair_scatter_two(2)), ((sums, others), ADD_ALL)),
        (token,),
        "grad_b_two",
    )
    step_b = both_ways(sends, dp)
    others = butterfly(sums, "dp", 0, 1)
    sends, token = stages(
        (((*chunks_a, *step_a), scatter_three(2)),),
        (token,),
        "grad_a_three",
    )
    step_a = both_ways(sends, dp)
    (send,), (sums,), token = stages(
        (((*chunks_b, *step_b), pair_scatter_three(2)), ((sums, others), ADD_ALL)),
        (token,),
        "grad_b_three",
    )
    step_b = (*step_b, dp(send, 0, 1))
    others = butterfly(sums, "dp", 1, 0)
    (sums,), token = stages((((sums, others), ADD_ALL),), (token,), "sums_y")
    others = butterfly(sums, "dp", 2, 0)
    grad_qkv, grad_in, token = finish_a((*chunks_a, *step_a), (token,))
    grad_dense, grad_out, *rows, token = finish_b((*chunks_b, *step_b), sums, others, (token,))
    grad_input, token = finish_grad(me, hidden_in, cotangent, u_rows, after=(token,))
    gain1, bias1, gain2, bias2, grad_b, grad_b_again, grad_b_qkv, grad_b_in = (r[0] for r in rows)
    return (
        hidden_out,
        grad_input,
        gain1,
        bias1,
        gain2,
        bias2,
        grad_qkv,
        grad_b_qkv,
        grad_dense,
        grad_b,
        grad_in,
        grad_b_in,
        grad_out,
        grad_b_again,
    )


def butterfly(value, axis, step, flip, core=0):
    pairs = []
    if axis == "dp":
        for y in range(4):
            for xh in range(2):
                for c in range(2):
                    pairs.append(
                        ((y * 2 + xh) * 2 + c, ((y ^ step) * 2 + (xh ^ flip)) * 2 + (c ^ core))
                    )
    else:
        for xl in range(2):
            for z in range(4):
                pairs.append((xl * 4 + z, (xl ^ flip) * 4 + (z ^ step)))
    return lax.ppermute(value, axis, pairs)


def solution(mesh):
    in_specs = (
        P(("dp", "tensor"), None),
        P("dp"),
        P(),
        P(),
        P(),
        P(),
        P("dp", "tensor"),
        P("tensor"),
        P("tensor", "dp"),
        P(),
        P("dp", "tensor"),
        P("tensor"),
        P("tensor", "dp"),
        P(),
        P(("dp", "tensor"), None),
    )
    out_specs = (
        P(("dp", "tensor"), None),
        P(("dp", "tensor"), None),
        P(),
        P(),
        P(),
        P(),
        P("dp", "tensor"),
        P("tensor"),
        P("tensor", "dp"),
        P(),
        P("dp", "tensor"),
        P("tensor"),
        P("tensor", "dp"),
        P(),
    )
    return jax.shard_map(
        per_device, mesh=mesh, in_specs=in_specs, out_specs=out_specs, check_vma=False
    )
```

```python
import functools
import math

import jax
import jax.numpy as jnp
from jax import lax
from jax.experimental import pallas as pl
from jax.experimental.pallas import tpu as pltpu
from jax.sharding import PartitionSpec as P

DH = 256
ROT = 64
LENGTH = 1024
D = 2048
LANE = 128
HALF = 64

EPS = 1e-05
NEG = -1e30
BF = jnp.bfloat16
F32 = jnp.float32

ORDER = ((0, 0), (0, 1), (3, 0), (1, 0), (3, 1), (2, 0), (1, 1), (2, 1))
ROOM = 64 * 1024 * 1024 - 128 * 1024
TILE = 256
SCALE = DH**-0.5
BIASES = 8
QUARTER = LENGTH // 4
QUARTERS = tuple((n * QUARTER, (n + 1) * QUARTER) for n in range(4))
FAST, SLOW, SCALAR = pltpu.VMEM, pltpu.HBM, pltpu.SMEM


def dp_pairs(step, flip, core):
    pairs = []
    for y in range(4):
        for xh in range(2):
            for c in range(2):
                pairs.append(
                    ((y * 2 + xh) * 2 + c, (((y + step) % 4) * 2 + (xh ^ flip)) * 2 + (c ^ core))
                )
    return pairs


def tensor_pairs(step, flip):
    return [(xl * 4 + z, (xl ^ flip) * 4 + (z + step) % 4) for xl in range(2) for z in range(4)]


def dp_move(value, step, flip, core=0):
    return lax.ppermute(value, "dp", dp_pairs(step, flip, core))


def tensor_move(value, step, flip):
    return lax.ppermute(value, "tensor", tensor_pairs(step, flip))


def shape(rows, cols, dtype):
    return jax.ShapeDtypeStruct((rows, cols), dtype)


class Copies:
    def __init__(self, sems):
        self.sems, self.count = sems, 0

    def start(self, source, target):
        copy = pltpu.make_async_copy(source, target, self.sems.at[self.count])
        self.count += 1
        copy.start()
        return copy


def wait(copies):
    for copy in copies:
        copy.wait()


def call(
    body, args, outs, ins=FAST, to=FAST, scratch=(), cost=(0, 0), name=None, after=(), carry=(), lazy=False
):
    moved = sum(math.prod(a.shape) * a.dtype.itemsize for a in (*args, *outs))
    count, given = len(args), len(args) + len(after) + len(carry)
    end = given + len(outs)
    ins = [ins] * count if not isinstance(ins, (tuple, list)) else list(ins)
    to = [to] * len(outs) if not isinstance(to, (tuple, list)) else list(to)
    fast_in = [i for i, w in enumerate(ins) if w is FAST]
    fast_out = [i for i, w in enumerate(to) if w is FAST]
    held = [pltpu.VMEM(args[i].shape, args[i].dtype) for i in fast_in]
    held += [pltpu.VMEM(outs[i].shape, outs[i].dtype) for i in fast_out]
    held += [pltpu.VMEM((8, LANE), F32), pltpu.SemaphoreType.DMA((len(fast_in) + len(fast_out) + 1,))]

    def run(*refs):
        refs = list(refs)
        given_refs, out_refs, token, rest = refs[:count], refs[given:end], refs[end], refs[end + 1 + len(carry) :]
        own, rest = rest[: len(held)], rest[len(held) :]
        copies = Copies(own[-1])
        begun = []
        for slot, i in enumerate(fast_in):
            begun.append(copies.start(given_refs[i], own[slot]))
            given_refs[i] = own[slot]
        targets = list(out_refs)
        for slot, i in enumerate(fast_out):
            out_refs[i] = own[len(fast_in) + slot]
        own[-2][...] = jnp.zeros((8, LANE), F32)
        last = [copies.start(own[-2], token)]
        if lazy:
            body(lambda: wait(begun), *given_refs, *out_refs, *rest)
        else:
            wait(begun)
            body(*given_refs, *out_refs, *rest)
        for i in fast_out:
            last.append(copies.start(out_refs[i], targets[i]))
        wait(last)

    where = lambda w: pl.BlockSpec(memory_space=SCALAR if w is SCALAR else SLOW)
    return pl.pallas_call(
        run,
        in_specs=[where(w) for w in ins] + [where(SLOW)] * (len(after) + len(carry)),
        out_specs=[where(SLOW)] * (len(outs) + 1 + len(carry)),
        out_shape=[*outs, shape(8, LANE, F32), *(shape(*c.shape, c.dtype) for c in carry)],
        input_output_aliases={
            count + len(after) + k: len(outs) + 1 + k for k in range(len(carry))
        },
        scratch_shapes=[*held, *scratch],
        compiler_params=pltpu.CompilerParams(vmem_limit_bytes=ROOM),
        cost_estimate=pl.CostEstimate(
            flops=1, transcendentals=0, bytes_accessed=1
        ),
        name=name,
    )(*args, *after, *carry)


def stage_kernel(groups, counts, *refs):
    refs = list(refs)
    arrays = [[refs.pop(0) for _ in range(count)] for count in counts]
    outs = [[refs.pop(0) for _ in parts] for parts in groups]
    held = [refs.pop(0) for _ in groups]
    copies = Copies(refs.pop(0))
    segments = []
    for parts, given, made, room in zip(groups, arrays, outs, held):
        at = 0
        for out, part in zip(made, parts):
            to = 0
            for rows, terms in part:
                places, begun = [], []
                for index, start in terms:
                    source = given[index].at[start : start + rows, :]
                    begun.append(copies.start(source, room.at[at : at + rows, :]))
                    places.append(at)
                    at += rows
                segments.append((out.at[to : to + rows, :], room, rows, places, begun))
                to += rows
    pending = []
    for target, room, rows, places, begun in segments:
        wait(begun)
        if len(places) > 1 and room.dtype == F32:
            total = room[places[0] : places[0] + rows, :]
            for place in places[1:]:
                total = total + room[place : place + rows, :]
            room[places[0] : places[0] + rows, :] = total
        elif len(places) > 1:

            def add(i, carry, room=room, places=places):
                where = [pl.ds(pl.multiple_of(place + i * 16, 16), 16) for place in places]
                total = room[where[0], :].astype(F32)
                for one in where[1:]:
                    total = total + room[one, :].astype(F32)
                room[where[0], :] = total.astype(BF)
                return carry

            lax.fori_loop(0, rows // 16, add, 0)
        pending.append(copies.start(room.at[places[0] : places[0] + rows, :], target))
    wait(pending)


def stages(groups, after=(), name="stage", carry=()):
    scratch, outs = [], []
    for arrays, parts in groups:
        cols, kind = arrays[0].shape[1], arrays[0].dtype
        rows = sum(r * len(t) for part in parts for r, t in part)
        scratch.append(pltpu.VMEM((rows, cols), kind))
        outs += [shape(sum(r for r, _ in part), cols, kind) for part in parts]
    copies = sum(len(t) + 1 for _, parts in groups for part in parts for _, t in part)
    made = call(
        functools.partial(
            stage_kernel, tuple(g[1] for g in groups), tuple(len(g[0]) for g in groups)
        ),
        tuple(array for arrays, _ in groups for array in arrays),
        outs,
        ins=SLOW,
        to=SLOW,
        scratch=[*scratch, pltpu.SemaphoreType.DMA((copies,))],
        name=name,
        after=after,
        carry=carry,
    )
    split = []
    for _, parts in groups:
        split.append(made[: len(parts)])
        made = made[len(parts) :]
    return (*split, *made)


def stage(arrays, parts, after=(), name="stage"):
    made, token = stages(((arrays, parts),), after, name)
    return (*made, token)


def row_set(index, start, rows):
    return (rows, ((index, start),))


def gather_one(block, move):
    return move(block, 0, 1), move(block, 1, 0), move(block, -1, 0)


def gather_two(block, got, move, after, name):
    parts = (
        (row_set(1, 0, LANE), row_set(2, 0, HALF)),
        (row_set(3, HALF, HALF), row_set(1, 0, LANE)),
    )
    up, down, token = stage((block, *got), parts, after=after, name=name)
    return (move(up, 1, 0), move(down, -1, 0)), token


def gather_three(block, first, got, move, after, name):
    joined = tuple((n, ((2 + k, 0),)) for k, n in enumerate((LANE,) * 4)) + (
        row_set(0, 0, 192),
        row_set(1, 0, 192),
    )
    parts = ((row_set(0, 0, HALF),), (row_set(1, LANE, HALF),), joined)
    up, down, joined, token = stage((*got, block, *first), parts, after=after, name=name)
    return (move(up, 1, 0), move(down, -1, 0)), joined, token


def pair_two(block, other, move, after, name):
    both, token = stage((block, other), ((row_set(0, 0, LANE), row_set(1, 0, LANE)),), after=after, name=name)
    return both, (move(both, 1, 0), move(both, -1, 0)), token


def pair_three(both, got, move, after, name):
    parts = (
        (row_set(0, 0, HALF), row_set(0, LANE, HALF)),
        (row_set(1, HALF, HALF), row_set(1, LANE + HALF, HALF)),
        (row_set(2, 0, 2 * LANE), row_set(0, 0, 2 * LANE), row_set(1, 0, 2 * LANE)),
    )
    up, down, joined, token = stage((*got, both), parts, after=after, name=name)
    return (move(up, 1, 0), move(down, -1, 0)), joined, token


def sums_of(count, start):
    return tuple((k, start) for k in range(count))


def scatter_one(n):
    return (((HALF, sums_of(n, 7 * LANE)),), ((HALF, sums_of(n, 7 * LANE + HALF)),))


def scatter_two(n):
    add = lambda start: sums_of(n, start)
    return (
        (
            (HALF, (*add(6 * LANE), (n, 0))),
            (HALF, add(6 * LANE + HALF)),
            (HALF, add(5 * LANE)),
        ),
        (
            (HALF, add(5 * LANE + HALF)),
            (HALF, add(4 * LANE)),
            (HALF, (*add(4 * LANE + HALF), (n + 1, 0))),
        ),
    )


def scatter_three(n):
    add = lambda start: sums_of(n, start)
    return (
        ((HALF, (*add(3 * LANE), (n, LANE))), (HALF, add(3 * LANE + HALF))),
        ((HALF, add(2 * LANE)), (HALF, (*add(2 * LANE + HALF), (n + 1, 0)))),
        ((LANE, (*add(LANE), (n, 0), (n + 1, HALF))),),
    )


def pair_scatter_one(n):
    add = lambda start: sums_of(n, start)
    return (
        ((HALF, add(5 * LANE)), (HALF, add(7 * LANE))),
        ((HALF, add(5 * LANE + HALF)), (HALF, add(7 * LANE + HALF))),
    )


def pair_scatter_two(n):
    add = lambda start: sums_of(n, start)
    return (
        (
            (HALF, (*add(3 * LANE), (n, 0))),
            (HALF, add(3 * LANE + HALF)),
            (HALF, (*add(6 * LANE), (n, HALF))),
            (HALF, add(6 * LANE + HALF)),
        ),
        (
            (HALF, add(2 * LANE)),
            (HALF, (*add(2 * LANE + HALF), (n + 1, 0))),
            (HALF, add(4 * LANE)),
            (HALF, (*add(4 * LANE + HALF), (n + 1, HALF))),
        ),
    )


def pair_scatter_three(n):
    return (((LANE, (*sums_of(n, LANE), (n, LANE), (n + 1, LANE))),),)


ADD_ALL = (((16, ((0, 0), (1, 0))),),)
ADD_SHARED = (((8, ((0, 0), (1, 0))), (8, ((0, 8),))),)


def both_ways(sends, move):
    got = [move(sends[0], 1, 0), move(sends[1], -1, 0)]
    return (*got, *(move(send, 0, 1) for send in sends[2:]))


def feature_place(me, k):
    dp = me[0]
    dy, dx = ORDER[k % 8]
    y, xh, c = lax.shift_right_logical(dp, 2), lax.shift_right_logical(dp, 1) & 1, dp & 1
    return ((((y + dy) & 3) * 2 + (xh ^ dx)) * 2) + (c ^ (k // 8))


def token_place(me, k):
    at = me[1]
    dz, dx = ORDER[k]
    return (lax.shift_right_logical(at, 2) ^ dx) * 4 + (((at & 3) + dz) & 3)


def feature_cols(me, k):
    return pl.ds(pl.multiple_of(feature_place(me, k) * LANE, LANE), LANE)


def fixed_cols(k):
    return slice(k * LANE, (k + 1) * LANE)


def token_rows(me, k, count=LANE, offset=0):
    return pl.ds(pl.multiple_of(token_place(me, k) * LANE + offset, HALF), count)


def centred(rows):
    rows = rows.astype(F32)
    rows = rows - jnp.mean(rows, axis=-1, keepdims=True)
    return rows, lax.rsqrt(jnp.mean(rows * rows, axis=-1, keepdims=True) + EPS)


def begin_kernel(me, x, w_qkv, w_in, hat, part_a, held):
    rows, rate = centred(x[...])
    held[...] = rows * rate
    for k in range(16):
        hat[:, fixed_cols(k)] = held[:, feature_cols(me, k)].astype(BF)
    part_a[:, :768] = w_qkv[...]
    part_a[:, 768:] = w_in[...]


def begin(me, x, w_qkv, w_in):
    return call(
        begin_kernel, (me, x, w_qkv, w_in), [shape(LANE, D, BF), shape(LANE, 1792, BF)],
        ins=[SCALAR] + [FAST] * 3, scratch=[pltpu.VMEM((LANE, D), F32)], name="begin",
    )


def prepare_kernel(
    me, g, w_dense, w_out, g1, b1, g2, b2, b_qkv, b_in, near_g, part_b, vectors, bias, g_sum
):
    for k in range(16):
        to, at = fixed_cols(k), feature_cols(me, k)
        near_g[:, to] = g[:, at]
        for n, vector in enumerate((g1, b1, g2, b2)):
            vectors[n : n + 1, to] = vector[:, at]
    part_b[:, :DH] = w_dense[...].T
    part_b[:, DH:] = w_out[...].T
    bias[:, :768] = b_qkv[...]
    bias[:, 768:] = b_in[...]
    g_sum[...] = jnp.sum(g[...].astype(F32), axis=0, keepdims=True)


def prepare(me, *args, after):
    return call(
        prepare_kernel, (me, *args),
        [
            shape(LANE, D, BF), shape(LANE, 1280, BF), shape(4, D, F32), shape(1, 1792, F32), shape(1, D, F32),
        ],
        ins=[SCALAR] + [FAST] * len(args), name="prepare", after=after,
    )


def positions(segment):
    count = segment.shape[0]
    index = jnp.arange(count, dtype=jnp.int32)
    change = jnp.concatenate([jnp.ones((1,), dtype=bool), segment[1:] != segment[:-1]])
    start = lax.cummax(jnp.where(change, index, jnp.zeros_like(index)), axis=0)
    return index - start


def angles(segment):
    lane = jnp.arange(LANE, dtype=jnp.int32)
    exponent = (lane % (ROT // 2)).astype(F32) * (2.0 / ROT)
    inverse = jnp.where(lane < ROT, jnp.exp(-exponent * math.log(10000.0)), 0.0)
    angle = positions(segment).astype(F32)[:, None] * inverse[None, :]
    return jnp.cos(angle), jnp.sin(angle)


def dot(a, b, ca, cb):
    return lax.dot_general(a, b, (((ca,), (cb,)), ((), ())), preferred_element_type=F32)


def turn(head, cosine, sine):
    lane = lax.broadcasted_iota(jnp.int32, head.shape, 1)
    ahead = pltpu.roll(head, LANE - ROT // 2, 1)
    behind = pltpu.roll(head, ROT // 2, 1)
    return head * cosine + jnp.where(lane < ROT // 2, -ahead, behind) * sine


def masked_scores(q, k, seg_col, seg_row, first):
    scores = dot(q, k, 1, 1)
    row = first + lax.broadcasted_iota(jnp.int32, scores.shape, 0)
    col = lax.broadcasted_iota(jnp.int32, scores.shape, 1)
    allowed = (seg_col == seg_row) & (row >= col)
    return jnp.where(allowed, scores, NEG)


def load_weights(copies, pairs, cols, shift=0):
    place = slice(cols.start - shift, cols.stop - shift)
    started = []
    for pieces, layout, held in pairs:
        for piece, start, rows, block, offset in layout:
            at = block * LANE + offset
            started.append(
                copies.start(
                    pieces[piece].at[start : start + rows, cols], held.at[at : at + rows, place]
                )
            )
    return started


JOINED_PAIR = (
    (0, 0, 128, 0, 0),
    (0, 128, 128, 1, 0),
    (0, 256, 128, 2, 0),
    (0, 384, 128, 4, 0),
    (0, 512, 128, 3, 0),
    (0, 640, 128, 6, 0),
    (1, 0, 64, 5, 0),
    (1, 64, 64, 7, 0),
    (1, 128, 64, 5, 64),
    (1, 192, 64, 7, 64),
)
JOINED = ((0, 0, 896, 0, 0), (1, 0, 128, 7, 0))


def weighted(norm, own, other, bias, lo, hi, at, shift=0):
    half = D // 2
    return (
        dot(norm[lo:hi, :half], own[:, at : at + TILE], 1, 0)
        + dot(norm[lo:hi, half:], other[:, at : at + TILE], 1, 0)
        + bias[:, shift + at : shift + at + TILE]
    )


def normed(hat, vectors, norm, lo, hi, k):
    x = hat[lo:hi, :].astype(F32)
    norm[lo:hi, :] = (x * vectors[k : k + 1, :] + vectors[k + 1 : k + 2, :]).astype(BF)


def attention_kernel(ready, *refs):
    hat_hbm, near, far, cosine_hbm, sine_hbm, seg_hbm = refs[0], refs[1:3], refs[3:5], *refs[5:8]
    vectors, bias, seg_row, mixed_out, context, log_total = refs[8:14]
    hat, own, other, norm, mixed, cosine, sine, seg_col, sems = refs[14:]
    copies = Copies(sems)
    pairs = ((near, JOINED, own), (far, JOINED, other))
    rows, tiles = [], []

    def next_rows():
        if len(rows) < 4:
            part = slice(*QUARTERS[len(rows)])
            arrays = ((hat_hbm, hat), (cosine_hbm, cosine), (sine_hbm, sine))
            rows.append([copies.start(a.at[part, :], held.at[part, :]) for a, held in arrays])

    def next_tile():
        if len(tiles) < 3:
            cols = slice(len(tiles) * TILE, (len(tiles) + 1) * TILE)
            tiles.append(load_weights(copies, pairs, cols))

    next_tile()
    next_rows()
    next_rows()
    ready()
    for i in range(3):
        wait(tiles[i])
        for n, (lo, hi) in enumerate(QUARTERS):
            if i == 0:
                wait(rows[n])
                next_rows()
                normed(hat, vectors, norm, lo, hi, 0)
            if n == 1:
                next_tile()
            acc = weighted(norm, own, other, bias, lo, hi, i * TILE)
            if i < 2:
                head = turn(acc[:, :LANE], cosine[lo:hi, :], sine[lo:hi, :])
                acc = jnp.concatenate([head, acc[:, LANE:]], axis=1)
            if i == 0:
                acc = acc * SCALE
            mixed[lo:hi, i * TILE : (i + 1) * TILE] = acc.astype(BF)
        if i == 0:
            segs = [copies.start(seg_hbm, seg_col)]
    wait(segs)
    saved = [copies.start(mixed, mixed_out)]
    for lo, hi in QUARTERS:
        scores = masked_scores(
            mixed[lo:hi, :DH], mixed[:hi, DH : 2 * DH], seg_col[lo:hi, :1], seg_row[:, :hi], lo
        )
        top = jnp.max(scores, axis=-1, keepdims=True)
        weights = jnp.exp(scores - top)
        total = jnp.sum(weights, axis=-1, keepdims=True)
        log_total[lo:hi, :] = jnp.broadcast_to(top + jnp.log(total), (hi - lo, LANE))
        probs = (weights * (1.0 / total)).astype(BF)
        context[lo:hi, :] = dot(probs, mixed[:hi, 2 * DH :], 1, 0).astype(BF)
    wait(saved)


def attention(hat, near, far, cosine, sine, seg_col, vectors, bias, seg_row, after):
    return call(
        attention_kernel,
        (hat, *near, *far, cosine, sine, seg_col, vectors, bias, seg_row),
        [shape(LENGTH, 768, BF), shape(LENGTH, DH, BF), shape(LENGTH, LANE, F32)],
        ins=[SLOW] * 8 + [FAST] * 3,
        to=[SLOW, FAST, FAST],
        scratch=[
            pltpu.VMEM((LENGTH, D), BF), pltpu.VMEM((1024, 768), BF),
            pltpu.VMEM((1024, 768), BF), pltpu.VMEM((LENGTH, D), BF),
            pltpu.VMEM((LENGTH, 768), BF), pltpu.VMEM((LENGTH, LANE), F32),
            pltpu.VMEM((LENGTH, LANE), F32), pltpu.VMEM((LENGTH, LANE), jnp.int32),
            pltpu.SemaphoreType.DMA((28,)),
        ],
        cost=(2 * LENGTH * D * 768 + 4 * LENGTH * LENGTH * DH, LENGTH * 1024),
        name="attention", after=after, lazy=True,
    )


def units_kernel(ready, *refs):
    hat_hbm, near, far, vectors, bias = refs[0], refs[1:3], refs[3:5], refs[5], refs[6]
    hidden_out, slope_out, hat, own, other, norm, hidden, slope, sems = refs[7:]
    copies = Copies(sems)
    pairs = ((near, JOINED, own), (far, JOINED, other))
    rows, tiles = [], []

    def next_rows():
        if len(rows) < 4:
            part = slice(*QUARTERS[len(rows)])
            rows.append(copies.start(hat_hbm.at[part, :], hat.at[part, :]))

    def next_tile():
        if len(tiles) < 4:
            at = 768 + len(tiles) * TILE
            tiles.append(load_weights(copies, pairs, slice(at, at + TILE), 768))

    next_tile()
    next_rows()
    next_rows()
    ready()
    saved = []
    for i in range(4):
        wait(tiles[i])
        cols = slice(i * TILE, (i + 1) * TILE)
        for n, (lo, hi) in enumerate(QUARTERS):
            if i == 0:
                wait(rows[n : n + 1])
                next_rows()
                normed(hat, vectors, norm, lo, hi, 2)
            if n == 1:
                next_tile()
            pre = weighted(norm, own, other, bias, lo, hi, i * TILE, 768)
            cdf = 0.5 * (1.0 + lax.erf(pre * (0.5**0.5)))
            hidden[lo:hi, cols] = (pre * cdf).astype(BF)
            density = jnp.exp(-0.5 * pre * pre) * (1.0 / math.sqrt(2.0 * math.pi))
            slope[lo:hi, cols] = (cdf + pre * density).astype(BF)
        saved.append(copies.start(hidden.at[:, cols], hidden_out.at[:, cols]))
        saved.append(copies.start(slope.at[:, cols], slope_out.at[:, cols]))
    wait(saved)


def units(hat, near, far, vectors, bias, after):
    return call(
        units_kernel, (hat, *near, *far, vectors, bias), [shape(LENGTH, 1024, BF)] * 2,
        ins=[SLOW] * 5 + [FAST] * 2, to=SLOW,
        scratch=[
            pltpu.VMEM((LENGTH, D), BF), pltpu.VMEM((1024, 1024), BF),
            pltpu.VMEM((1024, 1024), BF), pltpu.VMEM((LENGTH, D), BF),
            pltpu.VMEM((LENGTH, 1024), BF), pltpu.VMEM((LENGTH, 1024), BF),
            pltpu.SemaphoreType.DMA((32,)),
        ],
        cost=(2 * LENGTH * D * 1024, LENGTH * 2048), name="units", after=after, lazy=True,
    )


def outer_b_kernel(first, g, context, hidden, grad_hbm, left, held_c, held_h, grad, sems):
    copies = Copies(sems)
    begun = [copies.start(context, held_c), copies.start(hidden, held_h)]
    tiles = load_tiles(copies, g, left, first)
    wait(begun)
    done = []
    for i in range(4):
        cols = slice(i * TILE, (i + 1) * TILE)
        wait(tiles[i : i + 1])
        grad[cols, :DH] = dot(left[:, cols], held_c[...], 0, 0).astype(BF)
        grad[cols, DH:] = dot(left[:, cols], held_h[...], 0, 0).astype(BF)
        done.append(copies.start(grad.at[cols, :], grad_hbm.at[cols, :]))
    wait(done)


def outer_b(g, context, hidden, first, after):
    return call(
        functools.partial(outer_b_kernel, first), (g, context, hidden), [shape(1024, 1280, BF)],
        ins=SLOW, to=SLOW,
        scratch=[
            pltpu.VMEM((LENGTH, 1024), BF), pltpu.VMEM((LENGTH, DH), BF),
            pltpu.VMEM((LENGTH, 1024), BF), pltpu.VMEM((1024, 1280), BF),
            pltpu.SemaphoreType.DMA((12,)),
        ],
        cost=(2 * LENGTH * 1024 * 1280, 0), name="outer_b", after=after,
    )


def output_kernel(*refs):
    context, hidden, near, far = refs[0], refs[1], refs[2:4], refs[4:6]
    out_hbm, held_c, held_h, own, other, out, sems = refs[6:]
    copies = Copies(sems)
    firsts = load_weights(copies, ((near, JOINED_PAIR[:2], own),), slice(0, 1280))
    begun = [copies.start(context, held_c), copies.start(hidden, held_h)]
    nears = load_weights(copies, ((near, JOINED_PAIR[2:], own),), slice(0, 1280))
    fars = load_weights(copies, ((far, JOINED_PAIR, other),), slice(0, 1280))
    wait(firsts + begun)
    done = []
    for i in range(8):
        held = own if i < 4 else other
        at = i % 4 * TILE
        cols = slice(i * TILE, (i + 1) * TILE)
        if i == 1:
            wait(nears)
        if i == 4:
            wait(fars)
        for lo, hi in QUARTERS:
            out[lo:hi, cols] = (
                dot(held_c[lo:hi, :], held[at : at + TILE, :DH], 1, 1)
                + dot(held_h[lo:hi, :], held[at : at + TILE, DH:], 1, 1)
            ).astype(BF)
        if i % 2:
            pair = slice((i - 1) * TILE, (i + 1) * TILE)
            done.append(copies.start(out.at[:, pair], out_hbm.at[:, pair]))
    wait(done)


def output(context, hidden, near, far, after):
    return call(
        output_kernel, (context, hidden, *near, *far), [shape(LENGTH, D, BF)], ins=SLOW, to=SLOW,
        scratch=[
            pltpu.VMEM((LENGTH, DH), BF), pltpu.VMEM((LENGTH, 1024), BF),
            pltpu.VMEM((1024, 1280), BF), pltpu.VMEM((1024, 1280), BF),
            pltpu.VMEM((LENGTH, D), BF), pltpu.SemaphoreType.DMA((28,)),
        ],
        cost=(2 * LENGTH * D * 1280, 0), name="output", after=after,
    )


def column(row):
    parts = [jnp.broadcast_to(row[:, fixed_cols(k)], (LANE, LANE)).T for k in range(2)]
    return jnp.concatenate(parts, axis=0)


def backward_kernel(ready, me, *refs):
    g, near, far = refs[0], refs[1:3], refs[3:5]
    slope_hbm, mixed_hbm, near_a, far_a, hat_hbm = refs[5], refs[6], refs[7:9], refs[9:11], refs[11]
    log_total, seg_col, seg_row, cosine, sine, vectors, g_sum = refs[12:19]
    mixed_grad_hbm, pre_hbm, u_hbm, sum_qkv, sum_in, sums = refs[19:25]
    held, own, other, slope, mixed, own_a, other_a, d_context, d_pre, d_mixed, d_k, d_v, u, hat, sems = refs[25:]
    half = D // 2
    copies = Copies(sems)
    pairs = ((near, JOINED_PAIR, own), (far, JOINED_PAIR, other))
    first = load_weights(copies, pairs, slice(0, TILE))
    rows = [copies.start(g.at[lo:hi, :], held.at[lo:hi, :]) for lo, hi in QUARTERS]
    tiles = [load_weights(copies, pairs, slice(k * TILE, (k + 1) * TILE)) for k in range(1, 5)]
    slopes = [copies.start(slope_hbm, slope)]
    mixes = [copies.start(mixed_hbm, mixed)]
    inputs = [load_weights(copies, ((near_a, JOINED, own_a),), slice(0, 1792))]
    inputs += [load_weights(copies, ((far_a, JOINED, other_a),), slice(0, 1792))]
    hats = [
        copies.start(hat_hbm.at[:, k * 512 : (k + 1) * 512], hat.at[:, k * 512 : (k + 1) * 512])
        for k in range(4)
    ]
    done = []

    def product(lo, hi, cols):
        return dot(held[lo:hi, :half], own[:, cols], 1, 0) + dot(held[lo:hi, half:], other[:, cols], 1, 0)

    wait(first)
    for n, (lo, hi) in enumerate(QUARTERS):
        wait(rows[n : n + 1])
        d_context[lo:hi, :] = product(lo, hi, slice(0, TILE)).astype(BF)
    wait(slopes)
    for i in range(4):
        wait(tiles[i])
        cols = slice(i * TILE, (i + 1) * TILE)
        total = jnp.zeros((1, TILE), F32)
        for lo, hi in QUARTERS:
            acc = product(lo, hi, slice((i + 1) * TILE, (i + 2) * TILE))
            rounded = (acc * slope[lo:hi, cols].astype(F32)).astype(BF)
            d_pre[lo:hi, cols] = rounded
            total += jnp.sum(rounded.astype(F32), axis=0, keepdims=True)
        sum_in[:, cols] = total
    done.append(copies.start(d_pre, pre_hbm))

    wait(mixes)
    ready()
    sums[...] = jnp.zeros_like(sums)
    d_k[...] = jnp.zeros_like(d_k)
    d_v[...] = jnp.zeros_like(d_v)

    def back(lo, hi, value):
        head = turn(value[:, :LANE], cosine[lo:hi, :], -sine[lo:hi, :])
        return jnp.concatenate([head, value[:, LANE:]], axis=1)

    for lo, hi in QUARTERS:
        q, k, v = mixed[lo:hi, :DH], mixed[:hi, DH : 2 * DH], mixed[:hi, 2 * DH :]
        dc = d_context[lo:hi, :]
        scores = masked_scores(q, k, seg_col[lo:hi, :1], seg_row[:, :hi], lo)
        probs = jnp.exp(scores - log_total[lo:hi, :1])
        d_probs = dot(dc, v, 1, 1)
        spread = jnp.sum(probs * d_probs, axis=-1, keepdims=True)
        d_scores = (probs * (d_probs - spread)).astype(BF)
        d_mixed[lo:hi, :DH] = (back(lo, hi, dot(d_scores, k, 1, 0)) * SCALE).astype(BF)
        d_k[:hi, :] += dot(d_scores, q, 0, 0)
        d_v[:hi, :] += dot(probs.astype(BF), dc, 0, 0)
    total = jnp.zeros((1, 768), F32)
    for lo, hi in QUARTERS:
        d_mixed[lo:hi, DH : 2 * DH] = back(lo, hi, d_k[lo:hi, :]).astype(BF)
        d_mixed[lo:hi, 2 * DH :] = d_v[lo:hi, :].astype(BF)
        total += jnp.sum(d_mixed[lo:hi, :].astype(F32), axis=0, keepdims=True)
    sum_qkv[...] = total
    done.append(copies.start(d_mixed, mixed_grad_hbm))
    sums[4:5, :] = g_sum[...]
    sums[BIASES : BIASES + 1, :768] = sum_qkv[...]
    sums[BIASES : BIASES + 1, 768:1792] = sum_in[...]

    for i in range(8):
        weights = own_a if i < 4 else other_a
        at = i % 4 * TILE
        cols = slice(i * TILE, (i + 1) * TILE)
        if i % 4 == 0:
            wait(inputs[i // 4])
        if i % 2 == 0:
            wait(hats[i // 2 : i // 2 + 1])
        totals = [jnp.zeros((1, TILE), F32) for _ in range(4)]
        for lo, hi in QUARTERS:
            d1 = dot(d_mixed[lo:hi, :], weights[at : at + TILE, :768], 1, 1)
            d2 = dot(d_pre[lo:hi, :], weights[at : at + TILE, 768:], 1, 1)
            x = hat[lo:hi, cols].astype(F32)
            u[lo:hi, cols] = (d1 * vectors[0:1, cols] + d2 * vectors[2:3, cols]).astype(BF)
            for k, term in enumerate((d1 * x, d1, d2 * x, d2)):
                totals[k] += jnp.sum(term, axis=0, keepdims=True)
        for k in range(4):
            for j in range(2):
                sums[k : k + 1, feature_cols(me, 2 * i + j)] = totals[k][:, fixed_cols(j)]
        done.append(copies.start(u.at[:, cols], u_hbm.at[:, cols]))
    wait(done)


def backward(me, g, near, far, slope, mixed, near_a, far_a, *rest, after):
    return call(
        backward_kernel,
        (me, g, *near, *far, slope, mixed, *near_a, *far_a, *rest),
        [
            shape(LENGTH, 768, BF), shape(LENGTH, 1024, BF), shape(LENGTH, D, BF),
            shape(1, 768, F32), shape(1, 1024, F32), shape(16, D, F32),
        ],
        ins=[SCALAR] + [SLOW] * 12 + [FAST] * 7, to=[SLOW] * 3 + [FAST] * 3,
        scratch=[
            pltpu.VMEM((LENGTH, D), BF), pltpu.VMEM((1024, 1280), BF),
            pltpu.VMEM((1024, 1280), BF), pltpu.VMEM((LENGTH, 1024), BF),
            pltpu.VMEM((LENGTH, 768), BF),
            pltpu.VMEM((1024, 1792), BF), pltpu.VMEM((1024, 1792), BF),
            pltpu.VMEM((LENGTH, DH), BF), pltpu.VMEM((LENGTH, 1024), BF),
            pltpu.VMEM((LENGTH, 768), BF), pltpu.VMEM((LENGTH, DH), F32),
            pltpu.VMEM((LENGTH, DH), F32), pltpu.VMEM((LENGTH, D), BF), pltpu.VMEM((LENGTH, D), BF),
            pltpu.SemaphoreType.DMA((128,)),
        ],
        cost=(2 * LENGTH * (D * 1280 + D * 1792 + 5 * LENGTH * DH), LENGTH * LENGTH),
        name="backward", after=after, lazy=True,
    )


def outer_a_kernel(ready, hat_hbm, mixed_hbm, pre_hbm, vectors, sum_qkv, sum_in, *refs):
    grad_far_hbm, grad_near_hbm, hat, d_mixed, d_pre, grad, sems = refs
    copies = Copies(sems)
    order = (4, 5, 6, 7, 0, 1, 2, 3)
    hats, done = [], []

    def next_hat():
        if len(hats) < 8:
            i = order[len(hats)]
            cols = slice(i * TILE, (i + 1) * TILE)
            hats.append(copies.start(hat_hbm.at[:, cols], hat.at[:, cols]))

    next_hat()
    begun = [[copies.start(mixed_hbm, d_mixed)]]
    begun.append([copies.start(pre_hbm, d_pre)])
    next_hat()
    ready()
    parts = ((0, 768, d_mixed, sum_qkv), (768, 1792, d_pre, sum_in))
    for step, i in enumerate(order):
        cols = slice(i * TILE, (i + 1) * TILE)
        out = grad_near_hbm if i < 4 else grad_far_hbm
        wait(hats[step : step + 1])
        next_hat()
        for n, (lo, hi, upstream, total) in enumerate(parts):
            if step == 0:
                wait(begun[n])
            plain = dot(hat[:, cols], upstream[...], 0, 0)
            gain, bias = (column(vectors[2 * n + k : 2 * n + k + 1, cols]) for k in range(2))
            for k in range((hi - lo) // LANE):
                lanes = fixed_cols(k)
                grad[cols, lo + k * LANE : lo + (k + 1) * LANE] = (
                    gain * plain[:, lanes] + bias * total[:, lanes]
                ).astype(BF)
        done.append(copies.start(grad.at[cols, :], out.at[i % 4 * TILE : (i % 4 + 1) * TILE, :]))
    wait(done)


def outer_a(*args, after):
    return call(
        outer_a_kernel, args, [shape(1024, 1792, BF), shape(1024, 1792, BF)],
        ins=[SLOW] * 3 + [FAST] * 3, to=[SLOW] * 2,
        scratch=[
            pltpu.VMEM((LENGTH, D), BF), pltpu.VMEM((LENGTH, 768), BF), pltpu.VMEM((LENGTH, 1024), BF),
            pltpu.VMEM((D, 1792), BF), pltpu.SemaphoreType.DMA((20,)),
        ],
        cost=(2 * LENGTH * D * 1792, 0), name="outer_a", after=after, lazy=True,
    )


def load_tiles(copies, source, held, first):
    return [
        copies.start(
            source.at[:, first + i * TILE : first + (i + 1) * TILE],
            held.at[:, i * TILE : (i + 1) * TILE],
        )
        for i in range(4)
    ]


def finish_out_kernel(me, x, summed, b_dense, b_out, out):
    for k in range(16):
        to = feature_cols(me, k)
        value = x[:, to].astype(F32) + summed[:, fixed_cols(k)].astype(F32)
        out[:, to] = (value + b_dense[:, to] + b_out[:, to]).astype(BF)


def finish_out(me, *args, after):
    return call(
        finish_out_kernel, (me, *args), [shape(LANE, D, BF)], ins=[SCALAR] + [FAST] * 4,
        name="finish_out", after=after,
    )


def finish_grad_kernel(me, x, g, u, out):
    centre = jnp.mean(x[...].astype(F32), axis=-1, keepdims=True)
    rate = centred(x[...])[1]
    total = u[...].astype(F32)
    mean = jnp.mean(total, axis=-1, keepdims=True)
    spread = jnp.zeros((LANE, 1), F32)
    for k in range(16):
        hat = x[:, feature_cols(me, k)].astype(F32) - centre
        spread += jnp.sum(total[:, fixed_cols(k)] * hat, axis=-1, keepdims=True)
    spread = spread * rate * rate * (1.0 / D)
    for k in range(16):
        to = feature_cols(me, k)
        hat = x[:, to].astype(F32) - centre
        back = rate * (total[:, fixed_cols(k)] - mean - hat * spread)
        out[:, to] = (g[:, to].astype(F32) + back).astype(BF)


def finish_grad(me, *args, after):
    return call(
        finish_grad_kernel, (me, *args), [shape(LANE, D, BF)], ins=[SCALAR] + [FAST] * 3,
        name="finish_grad", after=after,
    )


def total_of(copies, arrays, held):
    begun = [
        copies.start(source.at[:LANE, :], held.at[k * LANE : (k + 1) * LANE, :])
        for k, source in enumerate(arrays)
    ]

    def total():
        wait(begun)
        value = held[:LANE, :].astype(F32)
        for k in range(1, len(arrays)):
            value = value + held[k * LANE : (k + 1) * LANE, :].astype(F32)
        return value

    return total


def finish_a_kernel(*refs):
    arrays, (qkv, units, held, sems) = refs[:5], refs[5:]
    value = total_of(Copies(sems), arrays, held)()
    qkv[...] = value[:, :768]
    units[...] = value[:, 768:]


def finish_a(arrays, after):
    return call(
        finish_a_kernel, arrays, [shape(LANE, 768, F32), shape(LANE, 1024, F32)], ins=SLOW,
        scratch=[pltpu.VMEM((5 * LANE, 1792), BF), pltpu.SemaphoreType.DMA((5,))],
        name="finish_a", after=after,
    )


def finish_b_kernel(*refs):
    arrays, sums, got = refs[:5], refs[5], refs[6]
    dense, out, rows, qkv, units, held, sems = refs[7], refs[8], refs[9:15], *refs[15:]
    total = total_of(Copies(sems), arrays, held)
    for k, row in enumerate(rows):
        at = min(k, 4)
        row[...] = (sums[at : at + 1, :] + got[at : at + 1, :])[0]
    biases = sums[BIASES : BIASES + 1, :] + got[BIASES : BIASES + 1, :]
    qkv[...] = biases[0, :768]
    units[...] = biases[0, 768:1792]
    value = total()
    dense[...] = value[:, :DH].T
    out[...] = value[:, DH:].T


def finish_b(arrays, sums, got, after):
    return call(
        finish_b_kernel, (*arrays, sums, got),
        [
            shape(DH, LANE, F32), shape(1024, LANE, F32),
            *(jax.ShapeDtypeStruct((n,), F32) for n in (D, D, D, D, D, D, 768, 1024)),
        ],
        ins=[SLOW] * 5 + [FAST] * 2,
        scratch=[pltpu.VMEM((5 * LANE, 1280), BF), pltpu.SemaphoreType.DMA((5,))],
        name="finish_b", after=after,
    )


def per_device(
    hidden_in,
    segment_ids,
    ln1_gain,
    ln1_bias,
    ln2_gain,
    ln2_bias,
    w_qkv,
    b_qkv,
    w_dense,
    b_dense,
    w_in,
    b_in,
    w_out,
    b_out,
    cotangent,
):
    me = jnp.stack([lax.axis_index("dp"), lax.axis_index("tensor")]).astype(jnp.int32)
    row = lambda vector: vector[None, :]
    dp, tensor = dp_move, tensor_move

    own_hat, part_a, token = begin(me, hidden_in, w_qkv, w_in)
    hat = lax.all_gather(own_hat, "tensor", axis=0, tiled=True)
    got_a = gather_one(part_a, dp)
    more_a, token = gather_two(part_a, got_a, dp, (token,), "a_two")
    own_g, part_b, vectors, bias, g_sum, token = prepare(
        me, cotangent, w_dense, w_out, row(ln1_gain), row(ln1_bias), row(ln2_gain), row(ln2_bias),
        row(b_qkv), row(b_in), after=(token,),
    )
    all_g = lax.all_gather(own_g, "tensor", axis=0, tiled=True)
    other_b = dp(part_b, 0, 1)
    cosine, sine = angles(segment_ids)
    seg_col = jnp.broadcast_to(segment_ids[:, None], (LENGTH, LANE))
    seg_row = row(segment_ids)

    last_a, a0, token = gather_three(
        part_a, got_a, more_a, dp, (token, cosine, sine, seg_col), "a_three"
    )
    far_a0 = dp(a0, 0, 0, 1)
    a1, token = stage(last_a, ((row_set(0, 0, HALF), row_set(1, 0, HALF)),), after=(token,), name="a_four")
    far_a1 = dp(a1, 0, 0, 1)
    both_b, more_b, token = pair_two(part_b, other_b, dp, (token,), "b_two")
    near_a, far_a = (a0, a1), (far_a0, far_a1)
    mixed, context, log_total, token = attention(
        hat, near_a, far_a, cosine, sine, seg_col, vectors, bias, seg_row, (token,)
    )
    last_b, b0, token = pair_three(both_b, more_b, dp, (token,), "b_three")
    far_b0 = dp(b0, 0, 0, 1)
    hidden, slope, token = units(hat, near_a, far_a, vectors, bias, (token,))
    b1, token = stage(last_b, ((row_set(0, 0, LANE), row_set(1, 0, LANE)),), after=(token,), name="b_four")
    far_b1 = dp(b1, 0, 0, 1)
    near_b, far_b = (b0, b1), (far_b0, far_b1)
    out_part, token = output(context, hidden, near_b, far_b, (token,))
    summed = lax.psum_scatter(out_part, "tensor", scatter_dimension=0, tiled=True)

    d_mixed, d_pre, u, sum_qkv, sum_in, sums, token = backward(
        me, all_g, near_b, far_b, slope, mixed, near_a, far_a, hat, log_total, seg_col, seg_row,
        cosine, sine, vectors, g_sum, after=(token,),
    )
    u_rows = lax.psum_scatter(u, "tensor", scatter_dimension=0, tiled=True)
    others = butterfly(sums, "dp", 1, 0)
    grad_a_far, grad_a, token = outer_a(
        hat, d_mixed, d_pre, vectors, sum_qkv, sum_in, after=(token,)
    )
    (sums,), token, grad_a_far = stages(
        (((sums, others), ADD_ALL),), (token,), "sums_y", (grad_a_far,)
    )
    got_far_a = dp(grad_a_far, 0, 0, 1)
    others = butterfly(sums, "dp", 2, 0)
    grad_b_far, token = outer_b(all_g, context, hidden, 1024, (token,))
    chunks_a = (grad_a, got_far_a)
    sends, (sums,), token, grad_b_far = stages(
        ((chunks_a, scatter_one(2)), ((sums, others), ADD_ALL)), (token,), "grad_a_one", (grad_b_far,)
    )
    step_a = both_ways(sends, dp)
    got_far_b = dp(grad_b_far, 0, 0, 1)
    others = butterfly(sums, "dp", 0, 0, 1)
    grad_b, token = outer_b(all_g, context, hidden, 0, (token,))
    chunks_b = (grad_b, got_far_b)
    sends_a, sends_b, (sums,), token = stages(
        (
            ((*chunks_a, *step_a), scatter_two(2)),
            (chunks_b, pair_scatter_one(2)),
            ((sums, others), ADD_ALL),
        ),
        (token,),
        "grads_two",
    )
    step_a, step_b = both_ways(sends_a, dp), both_ways(sends_b, dp)
    others = butterfly(sums, "tensor", 1, 0)
    hidden_out, token = finish_out(
        me, hidden_in, summed, row(b_dense), row(b_out), after=(token,)
    )
    sends, (sums,), token = stages(
        (((*chunks_b, *step_b), pair_scatter_two(2)), ((sums, others), ADD_SHARED)),
        (token,),
        "grad_b_two",
    )
    step_b = both_ways(sends, dp)
    others = butterfly(sums, "tensor", 2, 0)
    sends, (sums,), token = stages(
        (((*chunks_a, *step_a), scatter_three(2)), ((sums, others), ADD_SHARED)),
        (token,),
        "grad_a_three",
    )
    step_a = both_ways(sends, dp)
    others = butterfly(sums, "tensor", 0, 1)
    (send,), (sums,), token = stages(
        (((*chunks_b, *step_b), pair_scatter_three(2)), ((sums, others), ADD_SHARED)),
        (token,),
        "grad_b_three",
    )
    step_b = (*step_b, dp(send, 0, 1))
    others = butterfly(sums, "dp", 0, 1)
    grad_input, token = finish_grad(me, hidden_in, cotangent, u_rows, after=(token,))
    grad_qkv, grad_in, token = finish_a((*chunks_a, *step_a), (token,))
    grad_dense, grad_out, *rows, token = finish_b((*chunks_b, *step_b), sums, others, (token,))
    gain1, bias1, gain2, bias2, grad_b, grad_b_again, grad_b_qkv, grad_b_in = rows
    return (
        hidden_out,
        grad_input,
        gain1,
        bias1,
        gain2,
        bias2,
        grad_qkv,
        grad_b_qkv,
        grad_dense,
        grad_b,
        grad_in,
        grad_b_in,
        grad_out,
        grad_b_again,
    )


def butterfly(value, axis, step, flip, core=0):
    pairs = []
    if axis == "dp":
        for y in range(4):
            for xh in range(2):
                for c in range(2):
                    pairs.append(
                        ((y * 2 + xh) * 2 + c, ((y ^ step) * 2 + (xh ^ flip)) * 2 + (c ^ core))
                    )
    else:
        for xl in range(2):
            for z in range(4):
                pairs.append((xl * 4 + z, (xl ^ flip) * 4 + (z ^ step)))
    return lax.ppermute(value, axis, pairs)


def solution(mesh):
    in_specs = (
        P(("dp", "tensor"), None),
        P("dp"),
        P(),
        P(),
        P(),
        P(),
        P("dp", "tensor"),
        P("tensor"),
        P("tensor", "dp"),
        P(),
        P("dp", "tensor"),
        P("tensor"),
        P("tensor", "dp"),
        P(),
        P(("dp", "tensor"), None),
    )
    out_specs = (
        P(("dp", "tensor"), None),
        P(("dp", "tensor"), None),
        P(),
        P(),
        P(),
        P(),
        P("dp", "tensor"),
        P("tensor"),
        P("tensor", "dp"),
        P(),
        P("dp", "tensor"),
        P("tensor"),
        P("tensor", "dp"),
        P(),
    )
    return jax.shard_map(
        per_device, mesh=mesh, in_specs=in_specs, out_specs=out_specs, check_vma=False
    )
```

```python
import functools
import math

import jax
import jax.numpy as jnp
from jax import lax
from jax.experimental import pallas as pl
from jax.experimental.pallas import tpu as pltpu
from jax.sharding import PartitionSpec as P

DH = 256
ROT = 64
LENGTH = 1024
D = 2048
LANE = 128
HALF = 64

EPS = 1e-05
NEG = -1e30
BF = jnp.bfloat16
F32 = jnp.float32

ORDER = ((0, 0), (0, 1), (3, 0), (1, 0), (3, 1), (2, 0), (1, 1), (2, 1))
ROOM = 64 * 1024 * 1024 - 128 * 1024
TILE = 256
SCALE = DH**-0.5
BIASES = 8
QUARTER = LENGTH // 4
QUARTERS = tuple((n * QUARTER, (n + 1) * QUARTER) for n in range(4))
FAST, SLOW = pltpu.VMEM, pltpu.HBM


def dp_pairs(step, flip, core):
    pairs = []
    for y in range(4):
        for xh in range(2):
            for c in range(2):
                pairs.append(
                    ((y * 2 + xh) * 2 + c, (((y + step) % 4) * 2 + (xh ^ flip)) * 2 + (c ^ core))
                )
    return pairs


def tensor_pairs(step, flip):
    return [(xl * 4 + z, (xl ^ flip) * 4 + (z + step) % 4) for xl in range(2) for z in range(4)]


def dp_move(value, step, flip, core=0):
    return lax.ppermute(value, "dp", dp_pairs(step, flip, core))


def tensor_move(value, step, flip):
    return lax.ppermute(value, "tensor", tensor_pairs(step, flip))


def shape(rows, cols, dtype):
    return jax.ShapeDtypeStruct((rows, cols), dtype)


class Copies:
    def __init__(self, sems):
        self.sems, self.count = sems, 0

    def start(self, source, target):
        copy = pltpu.make_async_copy(source, target, self.sems.at[self.count])
        self.count += 1
        copy.start()
        return copy


def wait(copies):
    for copy in copies:
        copy.wait()


def call(
    body, args, outs, ins=FAST, to=FAST, scratch=(), cost=(0, 0), name=None, after=(), carry=(), lazy=False
):
    moved = sum(math.prod(a.shape) * a.dtype.itemsize for a in (*args, *outs))
    count, given = len(args), len(args) + len(after) + len(carry)
    end = given + len(outs)
    ins = [ins] * count if not isinstance(ins, (tuple, list)) else list(ins)
    to = [to] * len(outs) if not isinstance(to, (tuple, list)) else list(to)
    fast_in = [i for i, w in enumerate(ins) if w is FAST]
    fast_out = [i for i, w in enumerate(to) if w is FAST]
    held = [pltpu.VMEM(args[i].shape, args[i].dtype) for i in fast_in]
    held += [pltpu.VMEM(outs[i].shape, outs[i].dtype) for i in fast_out]
    held += [pltpu.VMEM((8, LANE), F32), pltpu.SemaphoreType.DMA((len(fast_in) + len(fast_out) + 1,))]

    def run(*refs):
        refs = list(refs)
        given_refs, out_refs, token, rest = refs[:count], refs[given:end], refs[end], refs[end + 1 + len(carry) :]
        own, rest = rest[: len(held)], rest[len(held) :]
        copies = Copies(own[-1])
        begun = []
        for slot, i in enumerate(fast_in):
            begun.append(copies.start(given_refs[i], own[slot]))
            given_refs[i] = own[slot]
        targets = list(out_refs)
        for slot, i in enumerate(fast_out):
            out_refs[i] = own[len(fast_in) + slot]
        own[-2][...] = jnp.zeros((8, LANE), F32)
        last = [copies.start(own[-2], token)]
        if lazy:
            body(lambda: wait(begun), *given_refs, *out_refs, *rest)
        else:
            wait(begun)
            body(*given_refs, *out_refs, *rest)
        for i in fast_out:
            last.append(copies.start(out_refs[i], targets[i]))
        wait(last)

    where = lambda w: pl.BlockSpec(memory_space=SLOW)
    return pl.pallas_call(
        run,
        in_specs=[where(w) for w in ins] + [where(SLOW)] * (len(after) + len(carry)),
        out_specs=[where(SLOW)] * (len(outs) + 1 + len(carry)),
        out_shape=[*outs, shape(8, LANE, F32), *(shape(*c.shape, c.dtype) for c in carry)],
        input_output_aliases={
            count + len(after) + k: len(outs) + 1 + k for k in range(len(carry))
        },
        scratch_shapes=[*held, *scratch],
        compiler_params=pltpu.CompilerParams(vmem_limit_bytes=ROOM),
        cost_estimate=pl.CostEstimate(
            flops=1, transcendentals=0, bytes_accessed=1
        ),
        name=name,
    )(*args, *after, *carry)


def stage_kernel(groups, counts, *refs):
    refs = list(refs)
    arrays = [[refs.pop(0) for _ in range(count)] for count in counts]
    outs = [[refs.pop(0) for _ in parts] for parts in groups]
    held = [refs.pop(0) for _ in groups]
    copies = Copies(refs.pop(0))
    segments = []
    for parts, given, made, room in zip(groups, arrays, outs, held):
        at = 0
        for out, part in zip(made, parts):
            to = 0
            for rows, terms in part:
                places, begun = [], []
                for index, start in terms:
                    source = given[index].at[start : start + rows, :]
                    begun.append(copies.start(source, room.at[at : at + rows, :]))
                    places.append(at)
                    at += rows
                segments.append((out.at[to : to + rows, :], room, rows, places, begun))
                to += rows
    pending = []
    for target, room, rows, places, begun in segments:
        wait(begun)
        if len(places) > 1 and room.dtype == F32:
            total = room[places[0] : places[0] + rows, :]
            for place in places[1:]:
                total = total + room[place : place + rows, :]
            room[places[0] : places[0] + rows, :] = total
        elif len(places) > 1:

            def add(i, carry, room=room, places=places):
                where = [pl.ds(pl.multiple_of(place + i * 16, 16), 16) for place in places]
                total = room[where[0], :].astype(F32)
                for one in where[1:]:
                    total = total + room[one, :].astype(F32)
                room[where[0], :] = total.astype(BF)
                return carry

            lax.fori_loop(0, rows // 16, add, 0)
        pending.append(copies.start(room.at[places[0] : places[0] + rows, :], target))
    wait(pending)


def stages(groups, after=(), name="stage", carry=()):
    scratch, outs = [], []
    for arrays, parts in groups:
        cols, kind = arrays[0].shape[1], arrays[0].dtype
        rows = sum(r * len(t) for part in parts for r, t in part)
        scratch.append(pltpu.VMEM((rows, cols), kind))
        outs += [shape(sum(r for r, _ in part), cols, kind) for part in parts]
    copies = sum(len(t) + 1 for _, parts in groups for part in parts for _, t in part)
    made = call(
        functools.partial(
            stage_kernel, tuple(g[1] for g in groups), tuple(len(g[0]) for g in groups)
        ),
        tuple(array for arrays, _ in groups for array in arrays),
        outs,
        ins=SLOW,
        to=SLOW,
        scratch=[*scratch, pltpu.SemaphoreType.DMA((copies,))],
        name=name,
        after=after,
        carry=carry,
    )
    split = []
    for _, parts in groups:
        split.append(made[: len(parts)])
        made = made[len(parts) :]
    return (*split, *made)


def stage(arrays, parts, after=(), name="stage"):
    made, token = stages(((arrays, parts),), after, name)
    return (*made, token)


def row_set(index, start, rows):
    return (rows, ((index, start),))


def gather_one(block, move):
    return move(block, 0, 1), move(block, 1, 0), move(block, -1, 0)


def gather_two(block, got, move, after, name):
    parts = (
        (row_set(1, 0, LANE), row_set(2, 0, HALF)),
        (row_set(3, HALF, HALF), row_set(1, 0, LANE)),
    )
    up, down, token = stage((block, *got), parts, after=after, name=name)
    return (move(up, 1, 0), move(down, -1, 0)), token


def gather_three(block, first, got, move, after, name):
    joined = tuple((n, ((2 + k, 0),)) for k, n in enumerate((LANE,) * 4)) + (
        row_set(0, 0, 192),
        row_set(1, 0, 192),
    )
    parts = ((row_set(0, 0, HALF),), (row_set(1, LANE, HALF),), joined)
    up, down, joined, token = stage((*got, block, *first), parts, after=after, name=name)
    return (move(up, 1, 0), move(down, -1, 0)), joined, token


def pair_two(block, other, move, after, name):
    both, token = stage((block, other), ((row_set(0, 0, LANE), row_set(1, 0, LANE)),), after=after, name=name)
    return both, (move(both, 1, 0), move(both, -1, 0)), token


def pair_three(both, got, move, after, name):
    parts = (
        (row_set(0, 0, HALF), row_set(0, LANE, HALF)),
        (row_set(1, HALF, HALF), row_set(1, LANE + HALF, HALF)),
        (
            row_set(2, 0, 2 * LANE),
            row_set(0, 0, LANE),
            row_set(1, 0, LANE),
            row_set(0, LANE, LANE),
            row_set(1, LANE, LANE),
        ),
    )
    up, down, joined, token = stage((*got, both), parts, after=after, name=name)
    return (move(up, 1, 0), move(down, -1, 0)), joined, token


def sums_of(count, start):
    return tuple((k, start) for k in range(count))


def scatter_one(n):
    return (((HALF, sums_of(n, 7 * LANE)),), ((HALF, sums_of(n, 7 * LANE + HALF)),))


def scatter_two(n):
    add = lambda start: sums_of(n, start)
    return (
        (
            (HALF, (*add(6 * LANE), (n, 0))),
            (HALF, add(6 * LANE + HALF)),
            (HALF, add(5 * LANE)),
        ),
        (
            (HALF, add(5 * LANE + HALF)),
            (HALF, add(4 * LANE)),
            (HALF, (*add(4 * LANE + HALF), (n + 1, 0))),
        ),
    )


def scatter_three(n):
    add = lambda start: sums_of(n, start)
    return (
        ((HALF, (*add(3 * LANE), (n, LANE))), (HALF, add(3 * LANE + HALF))),
        ((HALF, add(2 * LANE)), (HALF, (*add(2 * LANE + HALF), (n + 1, 0)))),
        ((LANE, (*add(LANE), (n, 0), (n + 1, HALF))),),
    )


def pair_scatter_one(n):
    add = lambda start: sums_of(n, start)
    return (
        ((HALF, add(5 * LANE)), (HALF, add(7 * LANE))),
        ((HALF, add(5 * LANE + HALF)), (HALF, add(7 * LANE + HALF))),
    )


def pair_scatter_two(n):
    add = lambda start: sums_of(n, start)
    return (
        (
            (HALF, (*add(3 * LANE), (n, 0))),
            (HALF, add(3 * LANE + HALF)),
            (HALF, (*add(6 * LANE), (n, HALF))),
            (HALF, add(6 * LANE + HALF)),
        ),
        (
            (HALF, add(2 * LANE)),
            (HALF, (*add(2 * LANE + HALF), (n + 1, 0))),
            (HALF, add(4 * LANE)),
            (HALF, (*add(4 * LANE + HALF), (n + 1, HALF))),
        ),
    )


def pair_scatter_three(n):
    return (((LANE, (*sums_of(n, LANE), (n, LANE), (n + 1, LANE))),),)


ADD_ALL = (((16, ((0, 0), (1, 0))),),)
ADD_THREE = (((16, ((0, 0), (1, 0), (2, 0), (3, 0))),),)
ADD_SHARED = (((8, ((0, 0), (1, 0))), (8, ((0, 8),))),)


def both_ways(sends, move):
    got = [move(sends[0], 1, 0), move(sends[1], -1, 0)]
    return (*got, *(move(send, 0, 1) for send in sends[2:]))


def feature_place(k):
    dp = lax.axis_index("dp")
    dy, dx = ORDER[k % 8]
    y, xh, c = lax.shift_right_logical(dp, 2), lax.shift_right_logical(dp, 1) & 1, dp & 1
    return ((((y + dy) & 3) * 2 + (xh ^ dx)) * 2) + (c ^ (k // 8))


def feature_cols(k):
    return pl.ds(pl.multiple_of(feature_place(k) * LANE, LANE), LANE)


def fixed_cols(k):
    return slice(k * LANE, (k + 1) * LANE)


def centred(rows):
    rows = rows.astype(F32)
    rows = rows - jnp.mean(rows, axis=-1, keepdims=True)
    return rows, lax.rsqrt(jnp.mean(rows * rows, axis=-1, keepdims=True) + EPS)


def begin_kernel(x, hat, held):
    rows, rate = centred(x[...])
    held[...] = rows * rate
    for k in range(16):
        hat[:, fixed_cols(k)] = held[:, feature_cols(k)].astype(BF)


def begin(x):
    return call(
        begin_kernel, (x,), [shape(LANE, D, BF)], scratch=[pltpu.VMEM((LANE, D), F32)], name="begin"
    )


def beside_kernel(w_qkv, w_in, part_a, sems):
    copies = Copies(sems)
    begun = [copies.start(w_qkv, part_a.at[:, :768]), copies.start(w_in, part_a.at[:, 768:])]
    wait(begun)


def beside(w_qkv, w_in, after):
    return call(
        beside_kernel, (w_qkv, w_in), [shape(LANE, 1792, BF)], ins=SLOW,
        scratch=[pltpu.SemaphoreType.DMA((2,))], name="beside", after=after,
    )


def prepare_kernel(
    g, w_dense, w_out, g1, b1, g2, b2, b_qkv, b_in, near_g, part_b, vectors, bias, g_sum
):
    for k in range(16):
        to, at = fixed_cols(k), feature_cols(k)
        near_g[:, to] = g[:, at]
        for n, vector in enumerate((g1, b1, g2, b2)):
            vectors[n : n + 1, to] = vector[:, at]
    part_b[:, :DH] = w_dense[...].T
    part_b[:, DH:] = w_out[...].T
    bias[:, :768] = b_qkv[...]
    bias[:, 768:] = b_in[...]
    g_sum[...] = jnp.sum(g[...].astype(F32), axis=0, keepdims=True)


def prepare(*args, after):
    return call(
        prepare_kernel, args,
        [
            shape(LANE, D, BF), shape(LANE, 1280, BF), shape(4, D, F32), shape(1, 1792, F32), shape(1, D, F32),
        ],
        name="prepare", after=after,
    )


def positions(segment):
    count = segment.shape[0]
    index = jnp.arange(count, dtype=jnp.int32)
    change = jnp.concatenate([jnp.ones((1,), dtype=bool), segment[1:] != segment[:-1]])
    start = lax.cummax(jnp.where(change, index, jnp.zeros_like(index)), axis=0)
    return index - start


def angles(segment):
    lane = jnp.arange(LANE, dtype=jnp.int32)
    exponent = (lane % (ROT // 2)).astype(F32) * (2.0 / ROT)
    inverse = jnp.where(lane < ROT, jnp.exp(-exponent * math.log(10000.0)), 0.0)
    angle = positions(segment).astype(F32)[:, None] * inverse[None, :]
    return jnp.cos(angle), jnp.sin(angle)


def dot(a, b, ca, cb):
    return lax.dot_general(a, b, (((ca,), (cb,)), ((), ())), preferred_element_type=F32)


def turn(head, cosine, sine):
    lane = lax.broadcasted_iota(jnp.int32, head.shape, 1)
    ahead = pltpu.roll(head, LANE - ROT // 2, 1)
    behind = pltpu.roll(head, ROT // 2, 1)
    return head * cosine + jnp.where(lane < ROT // 2, -ahead, behind) * sine


def masked_scores(q, k, seg_col, seg_row, first):
    scores = dot(q, k, 1, 1)
    row = first + lax.broadcasted_iota(jnp.int32, scores.shape, 0)
    col = lax.broadcasted_iota(jnp.int32, scores.shape, 1)
    allowed = (seg_col == seg_row) & (row >= col)
    return jnp.where(allowed, scores, NEG)


def load_weights(copies, pairs, cols, shift=0):
    place = slice(cols.start - shift, cols.stop - shift)
    started = []
    for pieces, layout, held in pairs:
        for piece, start, rows, block, offset in layout:
            at = block * LANE + offset
            started.append(
                copies.start(
                    pieces[piece].at[start : start + rows, cols], held.at[at : at + rows, place]
                )
            )
    return started


JOINED_PAIR = ((0, 0, 640, 0, 0), (0, 640, 128, 6, 0), (1, 0, 128, 5, 0), (1, 128, 128, 7, 0))
JOINED = ((0, 0, 896, 0, 0), (1, 0, 128, 7, 0))


def weighted(norm, own, other, bias, lo, hi, at, shift=0):
    half = D // 2
    return (
        dot(norm[lo:hi, :half], own[:, at : at + TILE], 1, 0)
        + dot(norm[lo:hi, half:], other[:, at : at + TILE], 1, 0)
        + bias[:, shift + at : shift + at + TILE]
    )


def normed(hat, vectors, norm, lo, hi, k):
    x = hat[lo:hi, :].astype(F32)
    norm[lo:hi, :] = (x * vectors[k : k + 1, :] + vectors[k + 1 : k + 2, :]).astype(BF)


def attention_kernel(ready, *refs):
    hat_hbm, near, far, cosine_hbm, sine_hbm, seg_hbm = refs[0], refs[1:3], refs[3:5], *refs[5:8]
    vectors, bias, seg_row, mixed_out, context, log_total = refs[8:14]
    hat, own, other, norm, mixed, cosine, sine, seg_col, sems = refs[14:]
    copies = Copies(sems)
    pairs = ((near, JOINED, own), (far, JOINED, other))
    rows, tiles = [], []

    def next_rows():
        if len(rows) < 4:
            part = slice(*QUARTERS[len(rows)])
            arrays = ((hat_hbm, hat), (cosine_hbm, cosine), (sine_hbm, sine))
            rows.append([copies.start(a.at[part, :], held.at[part, :]) for a, held in arrays])

    def next_tile():
        if len(tiles) < 3:
            cols = slice(len(tiles) * TILE, (len(tiles) + 1) * TILE)
            tiles.append(load_weights(copies, pairs, cols))

    next_tile()
    next_rows()
    next_rows()
    ready()
    for i in range(3):
        wait(tiles[i])
        for n, (lo, hi) in enumerate(QUARTERS):
            if i == 0:
                wait(rows[n])
                next_rows()
                normed(hat, vectors, norm, lo, hi, 0)
            if n == 1:
                next_tile()
            acc = weighted(norm, own, other, bias, lo, hi, i * TILE)
            if i < 2:
                head = turn(acc[:, :LANE], cosine[lo:hi, :], sine[lo:hi, :])
                acc = jnp.concatenate([head, acc[:, LANE:]], axis=1)
            if i == 0:
                acc = acc * SCALE
            mixed[lo:hi, i * TILE : (i + 1) * TILE] = acc.astype(BF)
        if i == 0:
            segs = [copies.start(seg_hbm, seg_col)]
    wait(segs)
    saved = [copies.start(mixed, mixed_out)]
    for lo, hi in QUARTERS:
        scores = masked_scores(
            mixed[lo:hi, :DH], mixed[:hi, DH : 2 * DH], seg_col[lo:hi, :1], seg_row[:, :hi], lo
        )
        top = jnp.max(scores, axis=-1, keepdims=True)
        weights = jnp.exp(scores - top)
        total = jnp.sum(weights, axis=-1, keepdims=True)
        log_total[lo:hi, :] = jnp.broadcast_to(top + jnp.log(total), (hi - lo, LANE))
        probs = (weights * (1.0 / total)).astype(BF)
        context[lo:hi, :] = dot(probs, mixed[:hi, 2 * DH :], 1, 0).astype(BF)
    wait(saved)


def attention(hat, near, far, cosine, sine, seg_col, vectors, bias, seg_row, after):
    return call(
        attention_kernel,
        (hat, *near, *far, cosine, sine, seg_col, vectors, bias, seg_row),
        [shape(LENGTH, 768, BF), shape(LENGTH, DH, BF), shape(LENGTH, LANE, F32)],
        ins=[SLOW] * 8 + [FAST] * 3,
        to=[SLOW, FAST, FAST],
        scratch=[
            pltpu.VMEM((LENGTH, D), BF), pltpu.VMEM((1024, 768), BF),
            pltpu.VMEM((1024, 768), BF), pltpu.VMEM((LENGTH, D), BF),
            pltpu.VMEM((LENGTH, 768), BF), pltpu.VMEM((LENGTH, LANE), F32),
            pltpu.VMEM((LENGTH, LANE), F32), pltpu.VMEM((LENGTH, LANE), jnp.int32),
            pltpu.SemaphoreType.DMA((28,)),
        ],
        cost=(2 * LENGTH * D * 768 + 4 * LENGTH * LENGTH * DH, LENGTH * 1024),
        name="attention", after=after, lazy=True,
    )


def units_kernel(ready, *refs):
    hat_hbm, near, far, vectors, bias = refs[0], refs[1:3], refs[3:5], refs[5], refs[6]
    hidden_out, slope_out, hat, own, other, norm, hidden, slope, sems = refs[7:]
    copies = Copies(sems)
    pairs = ((near, JOINED, own), (far, JOINED, other))
    rows, tiles = [], []

    def next_rows():
        if len(rows) < 4:
            part = slice(*QUARTERS[len(rows)])
            rows.append(copies.start(hat_hbm.at[part, :], hat.at[part, :]))

    def next_tile():
        if len(tiles) < 4:
            at = 768 + len(tiles) * TILE
            tiles.append(load_weights(copies, pairs, slice(at, at + TILE), 768))

    next_tile()
    next_rows()
    next_rows()
    ready()
    saved = []
    for i in range(4):
        wait(tiles[i])
        cols = slice(i * TILE, (i + 1) * TILE)
        for n, (lo, hi) in enumerate(QUARTERS):
            if i == 0:
                wait(rows[n : n + 1])
                next_rows()
                normed(hat, vectors, norm, lo, hi, 2)
            if n == 1:
                next_tile()
            pre = weighted(norm, own, other, bias, lo, hi, i * TILE, 768)
            cdf = 0.5 * (1.0 + lax.erf(pre * (0.5**0.5)))
            hidden[lo:hi, cols] = (pre * cdf).astype(BF)
            density = jnp.exp(-0.5 * pre * pre) * (1.0 / math.sqrt(2.0 * math.pi))
            slope[lo:hi, cols] = (cdf + pre * density).astype(BF)
        saved.append(copies.start(hidden.at[:, cols], hidden_out.at[:, cols]))
        saved.append(copies.start(slope.at[:, cols], slope_out.at[:, cols]))
    wait(saved)


def units(hat, near, far, vectors, bias, after):
    return call(
        units_kernel, (hat, *near, *far, vectors, bias), [shape(LENGTH, 1024, BF)] * 2,
        ins=[SLOW] * 5 + [FAST] * 2, to=SLOW,
        scratch=[
            pltpu.VMEM((LENGTH, D), BF), pltpu.VMEM((1024, 1024), BF),
            pltpu.VMEM((1024, 1024), BF), pltpu.VMEM((LENGTH, D), BF),
            pltpu.VMEM((LENGTH, 1024), BF), pltpu.VMEM((LENGTH, 1024), BF),
            pltpu.SemaphoreType.DMA((32,)),
        ],
        cost=(2 * LENGTH * D * 1024, LENGTH * 2048), name="units", after=after, lazy=True,
    )


def outer_b_kernel(first, g, context, hidden, grad_hbm, left, held_c, held_h, grad, sems):
    copies = Copies(sems)
    begun = [copies.start(context, held_c), copies.start(hidden, held_h)]
    tiles = load_tiles(copies, g, left, first)
    wait(begun)
    done = []
    for i in range(4):
        cols = slice(i * TILE, (i + 1) * TILE)
        wait(tiles[i : i + 1])
        grad[cols, :DH] = dot(left[:, cols], held_c[...], 0, 0).astype(BF)
        grad[cols, DH:] = dot(left[:, cols], held_h[...], 0, 0).astype(BF)
        done.append(copies.start(grad.at[cols, :], grad_hbm.at[cols, :]))
    wait(done)


def outer_b(g, context, hidden, first, after):
    return call(
        functools.partial(outer_b_kernel, first), (g, context, hidden), [shape(1024, 1280, BF)],
        ins=SLOW, to=SLOW,
        scratch=[
            pltpu.VMEM((LENGTH, 1024), BF), pltpu.VMEM((LENGTH, DH), BF),
            pltpu.VMEM((LENGTH, 1024), BF), pltpu.VMEM((1024, 1280), BF),
            pltpu.SemaphoreType.DMA((12,)),
        ],
        cost=(2 * LENGTH * 1024 * 1280, 0), name="outer_b", after=after,
    )


def output_kernel(*refs):
    context, hidden, near, far = refs[0], refs[1], refs[2:4], refs[4:6]
    out_hbm, held_c, held_h, own, other, out, sems = refs[6:]
    copies = Copies(sems)
    firsts = load_weights(copies, ((near, JOINED_PAIR[:1], own),), slice(0, 1280))
    begun = [copies.start(context, held_c), copies.start(hidden, held_h)]
    nears = load_weights(copies, ((near, JOINED_PAIR[1:], own),), slice(0, 1280))
    fars = load_weights(copies, ((far, JOINED_PAIR, other),), slice(0, 1280))
    wait(firsts + begun)
    done = []
    for i in range(8):
        held = own if i < 4 else other
        at = i % 4 * TILE
        cols = slice(i * TILE, (i + 1) * TILE)
        if i == 1:
            wait(nears)
        if i == 4:
            wait(fars)
        for lo, hi in QUARTERS:
            out[lo:hi, cols] = (
                dot(held_c[lo:hi, :], held[at : at + TILE, :DH], 1, 1)
                + dot(held_h[lo:hi, :], held[at : at + TILE, DH:], 1, 1)
            ).astype(BF)
        if i % 2:
            pair = slice((i - 1) * TILE, (i + 1) * TILE)
            done.append(copies.start(out.at[:, pair], out_hbm.at[:, pair]))
    wait(done)


def output(context, hidden, near, far, after):
    return call(
        output_kernel, (context, hidden, *near, *far), [shape(LENGTH, D, BF)], ins=SLOW, to=SLOW,
        scratch=[
            pltpu.VMEM((LENGTH, DH), BF), pltpu.VMEM((LENGTH, 1024), BF),
            pltpu.VMEM((1024, 1280), BF), pltpu.VMEM((1024, 1280), BF),
            pltpu.VMEM((LENGTH, D), BF), pltpu.SemaphoreType.DMA((16,)),
        ],
        cost=(2 * LENGTH * D * 1280, 0), name="output", after=after,
    )


def column(row):
    parts = [jnp.broadcast_to(row[:, fixed_cols(k)], (LANE, LANE)).T for k in range(2)]
    return jnp.concatenate(parts, axis=0)


def backward_kernel(ready, *refs):
    g, near, far = refs[0], refs[1:3], refs[3:5]
    slope_hbm, mixed_hbm, near_a, far_a, hat_hbm = refs[5], refs[6], refs[7:9], refs[9:11], refs[11]
    log_total, seg_col, seg_row, cosine, sine, vectors, g_sum = refs[12:19]
    mixed_grad_hbm, pre_hbm, u_hbm, sum_qkv, sum_in, sums = refs[19:25]
    held, own, other, slope, mixed, own_a, other_a, d_context, d_pre, d_mixed, d_k, d_v, u, hat, sems = refs[25:]
    half = D // 2
    copies = Copies(sems)
    pairs = ((near, JOINED_PAIR, own), (far, JOINED_PAIR, other))
    first = load_weights(copies, pairs, slice(0, TILE))
    rows = [copies.start(g.at[lo:hi, :], held.at[lo:hi, :]) for lo, hi in QUARTERS]
    tiles = [load_weights(copies, pairs, slice(k * TILE, (k + 1) * TILE)) for k in range(1, 5)]
    slopes = [copies.start(slope_hbm, slope)]
    mixes = [copies.start(mixed_hbm, mixed)]
    inputs = [load_weights(copies, ((near_a, JOINED, own_a),), slice(0, 1792))]
    inputs += [load_weights(copies, ((far_a, JOINED, other_a),), slice(0, 1792))]
    hats = [
        copies.start(hat_hbm.at[:, k * 512 : (k + 1) * 512], hat.at[:, k * 512 : (k + 1) * 512])
        for k in range(4)
    ]
    done = []

    def product(lo, hi, cols):
        return dot(held[lo:hi, :half], own[:, cols], 1, 0) + dot(held[lo:hi, half:], other[:, cols], 1, 0)

    wait(first)
    for n, (lo, hi) in enumerate(QUARTERS):
        wait(rows[n : n + 1])
        d_context[lo:hi, :] = product(lo, hi, slice(0, TILE)).astype(BF)
    wait(slopes)
    for i in range(4):
        wait(tiles[i])
        cols = slice(i * TILE, (i + 1) * TILE)
        total = jnp.zeros((1, TILE), F32)
        for lo, hi in QUARTERS:
            acc = product(lo, hi, slice((i + 1) * TILE, (i + 2) * TILE))
            rounded = (acc * slope[lo:hi, cols].astype(F32)).astype(BF)
            d_pre[lo:hi, cols] = rounded
            total += jnp.sum(rounded.astype(F32), axis=0, keepdims=True)
        sum_in[:, cols] = total
    done.append(copies.start(d_pre, pre_hbm))

    wait(mixes)
    ready()
    sums[...] = jnp.zeros_like(sums)
    d_k[...] = jnp.zeros_like(d_k)
    d_v[...] = jnp.zeros_like(d_v)

    def back(lo, hi, value):
        head = turn(value[:, :LANE], cosine[lo:hi, :], -sine[lo:hi, :])
        return jnp.concatenate([head, value[:, LANE:]], axis=1)

    for lo, hi in QUARTERS:
        q, k, v = mixed[lo:hi, :DH], mixed[:hi, DH : 2 * DH], mixed[:hi, 2 * DH :]
        dc = d_context[lo:hi, :]
        scores = masked_scores(q, k, seg_col[lo:hi, :1], seg_row[:, :hi], lo)
        probs = jnp.exp(scores - log_total[lo:hi, :1])
        d_probs = dot(dc, v, 1, 1)
        spread = jnp.sum(probs * d_probs, axis=-1, keepdims=True)
        d_scores = (probs * (d_probs - spread)).astype(BF)
        d_mixed[lo:hi, :DH] = (back(lo, hi, dot(d_scores, k, 1, 0)) * SCALE).astype(BF)
        d_k[:hi, :] += dot(d_scores, q, 0, 0)
        d_v[:hi, :] += dot(probs.astype(BF), dc, 0, 0)
    total = jnp.zeros((1, 768), F32)
    for lo, hi in QUARTERS:
        d_mixed[lo:hi, DH : 2 * DH] = back(lo, hi, d_k[lo:hi, :]).astype(BF)
        d_mixed[lo:hi, 2 * DH :] = d_v[lo:hi, :].astype(BF)
        total += jnp.sum(d_mixed[lo:hi, :].astype(F32), axis=0, keepdims=True)
    sum_qkv[...] = total
    done.append(copies.start(d_mixed, mixed_grad_hbm))
    sums[4:5, :] = g_sum[...]
    sums[BIASES : BIASES + 1, :768] = sum_qkv[...]
    sums[BIASES : BIASES + 1, 768:1792] = sum_in[...]

    for i in range(8):
        weights = own_a if i < 4 else other_a
        at = i % 4 * TILE
        cols = slice(i * TILE, (i + 1) * TILE)
        if i % 4 == 0:
            wait(inputs[i // 4])
        if i % 2 == 0:
            wait(hats[i // 2 : i // 2 + 1])
        totals = [jnp.zeros((1, TILE), F32) for _ in range(4)]
        for lo, hi in QUARTERS:
            d1 = dot(d_mixed[lo:hi, :], weights[at : at + TILE, :768], 1, 1)
            d2 = dot(d_pre[lo:hi, :], weights[at : at + TILE, 768:], 1, 1)
            x = hat[lo:hi, cols].astype(F32)
            u[lo:hi, cols] = (d1 * vectors[0:1, cols] + d2 * vectors[2:3, cols]).astype(BF)
            for k, term in enumerate((d1 * x, d1, d2 * x, d2)):
                totals[k] += jnp.sum(term, axis=0, keepdims=True)
        for k in range(4):
            for j in range(2):
                sums[k : k + 1, feature_cols(2 * i + j)] = totals[k][:, fixed_cols(j)]
        done.append(copies.start(u.at[:, cols], u_hbm.at[:, cols]))
    wait(done)


def backward(g, near, far, slope, mixed, near_a, far_a, *rest, after):
    return call(
        backward_kernel,
        (g, *near, *far, slope, mixed, *near_a, *far_a, *rest),
        [
            shape(LENGTH, 768, BF), shape(LENGTH, 1024, BF), shape(LENGTH, D, BF),
            shape(1, 768, F32), shape(1, 1024, F32), shape(16, D, F32),
        ],
        ins=[SLOW] * 12 + [FAST] * 7, to=[SLOW] * 3 + [FAST] * 3,
        scratch=[
            pltpu.VMEM((LENGTH, D), BF), pltpu.VMEM((1024, 1280), BF),
            pltpu.VMEM((1024, 1280), BF), pltpu.VMEM((LENGTH, 1024), BF),
            pltpu.VMEM((LENGTH, 768), BF),
            pltpu.VMEM((1024, 1792), BF), pltpu.VMEM((1024, 1792), BF),
            pltpu.VMEM((LENGTH, DH), BF), pltpu.VMEM((LENGTH, 1024), BF),
            pltpu.VMEM((LENGTH, 768), BF), pltpu.VMEM((LENGTH, DH), F32),
            pltpu.VMEM((LENGTH, DH), F32), pltpu.VMEM((LENGTH, D), BF), pltpu.VMEM((LENGTH, D), BF),
            pltpu.SemaphoreType.DMA((80,)),
        ],
        cost=(2 * LENGTH * (D * 1280 + D * 1792 + 5 * LENGTH * DH), LENGTH * LENGTH),
        name="backward", after=after, lazy=True,
    )


def outer_a_kernel(ready, hat_hbm, mixed_hbm, pre_hbm, vectors, sum_qkv, sum_in, *refs):
    grad_far_hbm, grad_near_hbm, hat, d_mixed, d_pre, grad, sems = refs
    copies = Copies(sems)
    order = (4, 5, 6, 7, 0, 1, 2, 3)
    hats, done = [], []

    def next_hat():
        if len(hats) < 8:
            i = order[len(hats)]
            cols = slice(i * TILE, (i + 1) * TILE)
            hats.append(copies.start(hat_hbm.at[:, cols], hat.at[:, cols]))

    next_hat()
    begun = [[copies.start(mixed_hbm, d_mixed)]]
    begun.append([copies.start(pre_hbm, d_pre)])
    next_hat()
    ready()
    parts = ((0, 768, d_mixed, sum_qkv), (768, 1792, d_pre, sum_in))
    for step, i in enumerate(order):
        cols = slice(i * TILE, (i + 1) * TILE)
        out = grad_near_hbm if i < 4 else grad_far_hbm
        wait(hats[step : step + 1])
        next_hat()
        for n, (lo, hi, upstream, total) in enumerate(parts):
            if step == 0:
                wait(begun[n])
            plain = dot(hat[:, cols], upstream[...], 0, 0)
            gain, bias = (column(vectors[2 * n + k : 2 * n + k + 1, cols]) for k in range(2))
            for k in range((hi - lo) // LANE):
                lanes = fixed_cols(k)
                grad[cols, lo + k * LANE : lo + (k + 1) * LANE] = (
                    gain * plain[:, lanes] + bias * total[:, lanes]
                ).astype(BF)
        done.append(copies.start(grad.at[cols, :], out.at[i % 4 * TILE : (i % 4 + 1) * TILE, :]))
    wait(done)


def outer_a(*args, after):
    return call(
        outer_a_kernel, args, [shape(1024, 1792, BF), shape(1024, 1792, BF)],
        ins=[SLOW] * 3 + [FAST] * 3, to=[SLOW] * 2,
        scratch=[
            pltpu.VMEM((LENGTH, D), BF), pltpu.VMEM((LENGTH, 768), BF), pltpu.VMEM((LENGTH, 1024), BF),
            pltpu.VMEM((D, 1792), BF), pltpu.SemaphoreType.DMA((20,)),
        ],
        cost=(2 * LENGTH * D * 1792, 0), name="outer_a", after=after, lazy=True,
    )


def load_tiles(copies, source, held, first):
    return [
        copies.start(
            source.at[:, first + i * TILE : first + (i + 1) * TILE],
            held.at[:, i * TILE : (i + 1) * TILE],
        )
        for i in range(4)
    ]


def finish_out_kernel(x, summed, b_dense, b_out, out):
    for k in range(16):
        to = feature_cols(k)
        value = x[:, to].astype(F32) + summed[:, fixed_cols(k)].astype(F32)
        out[:, to] = (value + b_dense[:, to] + b_out[:, to]).astype(BF)


def finish_out(*args, after):
    return call(
        finish_out_kernel, args, [shape(LANE, D, BF)], name="finish_out", after=after,
    )


def finish_grad_kernel(x, g, u, out):
    centre = jnp.mean(x[...].astype(F32), axis=-1, keepdims=True)
    rate = centred(x[...])[1]
    total = u[...].astype(F32)
    mean = jnp.mean(total, axis=-1, keepdims=True)
    spread = jnp.zeros((LANE, 1), F32)
    for k in range(16):
        hat = x[:, feature_cols(k)].astype(F32) - centre
        spread += jnp.sum(total[:, fixed_cols(k)] * hat, axis=-1, keepdims=True)
    spread = spread * rate * rate * (1.0 / D)
    for k in range(16):
        to = feature_cols(k)
        hat = x[:, to].astype(F32) - centre
        back = rate * (total[:, fixed_cols(k)] - mean - hat * spread)
        out[:, to] = (g[:, to].astype(F32) + back).astype(BF)


def finish_grad(*args, after):
    return call(
        finish_grad_kernel, args, [shape(LANE, D, BF)], name="finish_grad", after=after,
    )


def total_of(copies, arrays, held):
    begun = [
        copies.start(source.at[:LANE, :], held.at[k * LANE : (k + 1) * LANE, :])
        for k, source in enumerate(arrays)
    ]

    def total():
        wait(begun)
        value = held[:LANE, :].astype(F32)
        for k in range(1, len(arrays)):
            value = value + held[k * LANE : (k + 1) * LANE, :].astype(F32)
        return value

    return total


def finish_a_kernel(*refs):
    arrays, (qkv, units, held, sems) = refs[:5], refs[5:]
    value = total_of(Copies(sems), arrays, held)()
    qkv[...] = value[:, :768]
    units[...] = value[:, 768:]


def finish_a(arrays, after):
    return call(
        finish_a_kernel, arrays, [shape(LANE, 768, F32), shape(LANE, 1024, F32)], ins=SLOW,
        scratch=[pltpu.VMEM((5 * LANE, 1792), BF), pltpu.SemaphoreType.DMA((5,))],
        name="finish_a", after=after,
    )


def finish_b_kernel(*refs):
    arrays, sums, got = refs[:5], refs[5], refs[6]
    dense, out, rows, qkv, units, held, sems = refs[7], refs[8], refs[9:15], *refs[15:]
    total = total_of(Copies(sems), arrays, held)
    for k, row in enumerate(rows):
        at = min(k, 4)
        row[...] = (sums[at : at + 1, :] + got[at : at + 1, :])[0]
    biases = sums[BIASES : BIASES + 1, :]
    qkv[...] = biases[0, :768]
    units[...] = biases[0, 768:1792]
    value = total()
    dense[...] = value[:, :DH].T
    out[...] = value[:, DH:].T


def finish_b(arrays, sums, got, after):
    return call(
        finish_b_kernel, (*arrays, sums, got),
        [
            shape(DH, LANE, F32), shape(1024, LANE, F32),
            *(jax.ShapeDtypeStruct((n,), F32) for n in (D, D, D, D, D, D, 768, 1024)),
        ],
        ins=[SLOW] * 5 + [FAST] * 2,
        scratch=[pltpu.VMEM((5 * LANE, 1280), BF), pltpu.SemaphoreType.DMA((5,))],
        name="finish_b", after=after,
    )


def per_device(
    hidden_in,
    segment_ids,
    ln1_gain,
    ln1_bias,
    ln2_gain,
    ln2_bias,
    w_qkv,
    b_qkv,
    w_dense,
    b_dense,
    w_in,
    b_in,
    w_out,
    b_out,
    cotangent,
):
    row = lambda vector: vector[None, :]
    dp, tensor = dp_move, tensor_move

    own_hat, token = begin(hidden_in)
    part_a, token = beside(w_qkv, w_in, (token,))
    hat = lax.all_gather(own_hat, "tensor", axis=0, tiled=True)
    got_a = gather_one(part_a, dp)
    more_a, token = gather_two(part_a, got_a, dp, (token,), "a_two")
    own_g, part_b, vectors, bias, g_sum, token = prepare(
        cotangent, w_dense, w_out, row(ln1_gain), row(ln1_bias), row(ln2_gain), row(ln2_bias),
        row(b_qkv), row(b_in), after=(token,),
    )
    all_g = lax.all_gather(own_g, "tensor", axis=0, tiled=True)
    other_b = dp(part_b, 0, 1)
    cosine, sine = angles(segment_ids)
    seg_col = jnp.broadcast_to(segment_ids[:, None], (LENGTH, LANE))
    seg_row = row(segment_ids)

    last_a, a0, token = gather_three(
        part_a, got_a, more_a, dp, (token, cosine, sine, seg_col), "a_three"
    )
    far_a0 = dp(a0, 0, 0, 1)
    a1, token = stage(last_a, ((row_set(0, 0, HALF), row_set(1, 0, HALF)),), after=(token,), name="a_four")
    far_a1 = dp(a1, 0, 0, 1)
    both_b, more_b, token = pair_two(part_b, other_b, dp, (token,), "b_two")
    near_a, far_a = (a0, a1), (far_a0, far_a1)
    mixed, context, log_total, token = attention(
        hat, near_a, far_a, cosine, sine, seg_col, vectors, bias, seg_row, (token,)
    )
    last_b, b0, token = pair_three(both_b, more_b, dp, (token,), "b_three")
    far_b0 = dp(b0, 0, 0, 1)
    hidden, slope, token = units(hat, near_a, far_a, vectors, bias, (token,))
    halves = tuple(row_set(k, at, HALF) for at in (0, HALF) for k in (0, 1))
    b1, token = stage(last_b, (halves,), after=(token,), name="b_four")
    far_b1 = dp(b1, 0, 0, 1)
    near_b, far_b = (b0, b1), (far_b0, far_b1)
    out_part, token = output(context, hidden, near_b, far_b, (token,))
    summed = lax.psum_scatter(out_part, "tensor", scatter_dimension=0, tiled=True)

    d_mixed, d_pre, u, sum_qkv, sum_in, sums, token = backward(
        all_g, near_b, far_b, slope, mixed, near_a, far_a, hat, log_total, seg_col, seg_row,
        cosine, sine, vectors, g_sum, after=(token,),
    )
    u_rows = lax.psum_scatter(u, "tensor", scatter_dimension=0, tiled=True)
    others = tuple(butterfly(sums, "dp", y, 0, core) for y, core in ((1, 0), (0, 1), (1, 1)))
    grad_a_far, grad_a, token = outer_a(
        hat, d_mixed, d_pre, vectors, sum_qkv, sum_in, after=(token,)
    )
    (sums,), token, grad_a_far = stages(
        (((sums, *others), ADD_THREE),), (token,), "sums_y", (grad_a_far,)
    )
    got_far_a = dp(grad_a_far, 0, 0, 1)
    others = butterfly(sums, "dp", 2, 0)
    grad_b_far, token = outer_b(all_g, context, hidden, 1024, (token,))
    chunks_a = (grad_a, got_far_a)
    sends, (sums,), token, grad_b_far = stages(
        ((chunks_a, scatter_one(2)), ((sums, others), ADD_ALL)), (token,), "grad_a_one", (grad_b_far,)
    )
    step_a = both_ways(sends, dp)
    got_far_b = dp(grad_b_far, 0, 0, 1)
    others = butterfly(sums, "dp", 0, 1)
    grad_b, token = outer_b(all_g, context, hidden, 0, (token,))
    chunks_b = (grad_b, got_far_b)
    sends_b, sends_a, (sums,), token = stages(
        (
            (chunks_b, pair_scatter_one(2)),
            ((*chunks_a, *step_a), scatter_two(2)),
            ((sums, others), ADD_ALL),
        ),
        (token,),
        "grads_two",
    )
    step_b, step_a = both_ways(sends_b, dp), both_ways(sends_a, dp)
    others = butterfly(sums, "tensor", 1, 0)
    hidden_out, token = finish_out(
        hidden_in, summed, row(b_dense), row(b_out), after=(token,)
    )
    sends, (sums,), token = stages(
        (((*chunks_b, *step_b), pair_scatter_two(2)), ((sums, others), ADD_SHARED)),
        (token,),
        "grad_b_two",
    )
    step_b = both_ways(sends, dp)
    others = butterfly(sums, "tensor", 2, 0)
    sends, token = stages(
        (((*chunks_a, *step_a), scatter_three(2)),), (token,), "grad_a_three"
    )
    step_a = both_ways(sends, dp)
    (send,), (sums,), token = stages(
        (((*chunks_b, *step_b), pair_scatter_three(2)), ((sums, others), ADD_SHARED)),
        (token,),
        "grad_b_three",
    )
    step_b = (*step_b, dp(send, 0, 1))
    others = butterfly(sums, "tensor", 0, 1)
    grad_input, token = finish_grad(hidden_in, cotangent, u_rows, after=(token,))
    grad_qkv, grad_in, token = finish_a((*chunks_a, *step_a), (token,))
    grad_dense, grad_out, *rows, token = finish_b((*chunks_b, *step_b), sums, others, (token,))
    gain1, bias1, gain2, bias2, grad_b, grad_b_again, grad_b_qkv, grad_b_in = rows
    return (
        hidden_out,
        grad_input,
        gain1,
        bias1,
        gain2,
        bias2,
        grad_qkv,
        grad_b_qkv,
        grad_dense,
        grad_b,
        grad_in,
        grad_b_in,
        grad_out,
        grad_b_again,
    )


def butterfly(value, axis, step, flip, core=0):
    pairs = []
    if axis == "dp":
        for y in range(4):
            for xh in range(2):
                for c in range(2):
                    pairs.append(
                        ((y * 2 + xh) * 2 + c, ((y ^ step) * 2 + (xh ^ flip)) * 2 + (c ^ core))
                    )
    else:
        for xl in range(2):
            for z in range(4):
                pairs.append((xl * 4 + z, (xl ^ flip) * 4 + (z ^ step)))
    return lax.ppermute(value, axis, pairs)


def solution(mesh):
    in_specs = (
        P(("dp", "tensor"), None),
        P("dp"),
        P(),
        P(),
        P(),
        P(),
        P("dp", "tensor"),
        P("tensor"),
        P("tensor", "dp"),
        P(),
        P("dp", "tensor"),
        P("tensor"),
        P("tensor", "dp"),
        P(),
        P(("dp", "tensor"), None),
    )
    out_specs = (
        P(("dp", "tensor"), None),
        P(("dp", "tensor"), None),
        P(),
        P(),
        P(),
        P(),
        P("dp", "tensor"),
        P("tensor"),
        P("tensor", "dp"),
        P(),
        P("dp", "tensor"),
        P("tensor"),
        P("tensor", "dp"),
        P(),
    )
    return jax.shard_map(
        per_device, mesh=mesh, in_specs=in_specs, out_specs=out_specs, check_vma=False
    )
```

```python
import functools
import math

import jax
import jax.numpy as jnp
from jax import lax
from jax.experimental import pallas as pl
from jax.experimental.pallas import tpu as pltpu
from jax.sharding import PartitionSpec as P

DH = 256
ROT = 64
LENGTH = 1024
D = 2048
LANE = 128
HALF = 64

EPS = 1e-05
NEG = -1e30
BF = jnp.bfloat16
F32 = jnp.float32

ORDER = ((0, 0), (0, 1), (3, 0), (1, 0), (3, 1), (2, 0), (1, 1), (2, 1))
ROOM = 64 * 1024 * 1024 - 128 * 1024
TILE = 256
SCALE = DH**-0.5
BIASES = 8
QUARTER = LENGTH // 4
QUARTERS = tuple((n * QUARTER, (n + 1) * QUARTER) for n in range(4))
FAST, SLOW = pltpu.VMEM, pltpu.HBM


def dp_pairs(step, flip, core):
    pairs = []
    for y in range(4):
        for xh in range(2):
            for c in range(2):
                pairs.append(
                    ((y * 2 + xh) * 2 + c, (((y + step) % 4) * 2 + (xh ^ flip)) * 2 + (c ^ core))
                )
    return pairs


def tensor_pairs(step, flip):
    return [(xl * 4 + z, (xl ^ flip) * 4 + (z + step) % 4) for xl in range(2) for z in range(4)]


def dp_move(value, step, flip, core=0):
    return lax.ppermute(value, "dp", dp_pairs(step, flip, core))


def tensor_move(value, step, flip):
    return lax.ppermute(value, "tensor", tensor_pairs(step, flip))


def shape(rows, cols, dtype):
    return jax.ShapeDtypeStruct((rows, cols), dtype)


class Copies:
    def __init__(self, sems):
        self.sems, self.count = sems, 0

    def start(self, source, target):
        copy = pltpu.make_async_copy(source, target, self.sems.at[self.count])
        self.count += 1
        copy.start()
        return copy


def wait(copies):
    for copy in copies:
        copy.wait()


def call(
    body, args, outs, ins=FAST, to=FAST, scratch=(), cost=(0, 0), name=None, after=(), carry=(), lazy=False
):
    moved = sum(math.prod(a.shape) * a.dtype.itemsize for a in (*args, *outs))
    count, given = len(args), len(args) + len(after) + len(carry)
    end = given + len(outs)
    ins = [ins] * count if not isinstance(ins, (tuple, list)) else list(ins)
    to = [to] * len(outs) if not isinstance(to, (tuple, list)) else list(to)
    fast_in = [i for i, w in enumerate(ins) if w is FAST]
    fast_out = [i for i, w in enumerate(to) if w is FAST]
    held = [pltpu.VMEM(args[i].shape, args[i].dtype) for i in fast_in]
    held += [pltpu.VMEM(outs[i].shape, outs[i].dtype) for i in fast_out]
    held += [pltpu.VMEM((8, LANE), F32), pltpu.SemaphoreType.DMA((len(fast_in) + len(fast_out) + 1,))]

    def run(*refs):
        refs = list(refs)
        given_refs, out_refs, token, rest = refs[:count], refs[given:end], refs[end], refs[end + 1 + len(carry) :]
        own, rest = rest[: len(held)], rest[len(held) :]
        copies = Copies(own[-1])
        begun = []
        for slot, i in enumerate(fast_in):
            begun.append(copies.start(given_refs[i], own[slot]))
            given_refs[i] = own[slot]
        targets = list(out_refs)
        for slot, i in enumerate(fast_out):
            out_refs[i] = own[len(fast_in) + slot]
        own[-2][...] = jnp.zeros((8, LANE), F32)
        last = [copies.start(own[-2], token)]
        if lazy:
            body(lambda: wait(begun), *given_refs, *out_refs, *rest)
        else:
            wait(begun)
            body(*given_refs, *out_refs, *rest)
        for i in fast_out:
            last.append(copies.start(out_refs[i], targets[i]))
        wait(last)

    where = lambda w: pl.BlockSpec(memory_space=SLOW)
    return pl.pallas_call(
        run,
        in_specs=[where(w) for w in ins] + [where(SLOW)] * (len(after) + len(carry)),
        out_specs=[where(SLOW)] * (len(outs) + 1 + len(carry)),
        out_shape=[*outs, shape(8, LANE, F32), *(shape(*c.shape, c.dtype) for c in carry)],
        input_output_aliases={
            count + len(after) + k: len(outs) + 1 + k for k in range(len(carry))
        },
        scratch_shapes=[*held, *scratch],
        compiler_params=pltpu.CompilerParams(vmem_limit_bytes=ROOM),
        cost_estimate=pl.CostEstimate(
            flops=1, transcendentals=0, bytes_accessed=1
        ),
        name=name,
    )(*args, *after, *carry)


def stage_kernel(groups, counts, *refs):
    refs = list(refs)
    arrays = [[refs.pop(0) for _ in range(count)] for count in counts]
    outs = [[refs.pop(0) for _ in parts] for parts in groups]
    held = [refs.pop(0) for _ in groups]
    copies = Copies(refs.pop(0))
    segments = []
    for parts, given, made, room in zip(groups, arrays, outs, held):
        at = 0
        for out, part in zip(made, parts):
            to = 0
            for rows, terms in part:
                places, begun = [], []
                for index, start in terms:
                    source = given[index].at[start : start + rows, :]
                    begun.append(copies.start(source, room.at[at : at + rows, :]))
                    places.append(at)
                    at += rows
                segments.append((out.at[to : to + rows, :], room, rows, places, begun))
                to += rows
    pending = []
    for target, room, rows, places, begun in segments:
        wait(begun)
        if len(places) > 1 and room.dtype == F32:
            total = room[places[0] : places[0] + rows, :]
            for place in places[1:]:
                total = total + room[place : place + rows, :]
            room[places[0] : places[0] + rows, :] = total
        elif len(places) > 1:

            def add(i, carry, room=room, places=places):
                where = [pl.ds(pl.multiple_of(place + i * 16, 16), 16) for place in places]
                total = room[where[0], :].astype(F32)
                for one in where[1:]:
                    total = total + room[one, :].astype(F32)
                room[where[0], :] = total.astype(BF)
                return carry

            lax.fori_loop(0, rows // 16, add, 0)
        pending.append(copies.start(room.at[places[0] : places[0] + rows, :], target))
    wait(pending)


def stages(groups, after=(), name="stage", carry=()):
    scratch, outs = [], []
    for arrays, parts in groups:
        cols, kind = arrays[0].shape[1], arrays[0].dtype
        rows = sum(r * len(t) for part in parts for r, t in part)
        scratch.append(pltpu.VMEM((rows, cols), kind))
        outs += [shape(sum(r for r, _ in part), cols, kind) for part in parts]
    copies = sum(len(t) + 1 for _, parts in groups for part in parts for _, t in part)
    made = call(
        functools.partial(
            stage_kernel, tuple(g[1] for g in groups), tuple(len(g[0]) for g in groups)
        ),
        tuple(array for arrays, _ in groups for array in arrays),
        outs,
        ins=SLOW,
        to=SLOW,
        scratch=[*scratch, pltpu.SemaphoreType.DMA((copies,))],
        name=name,
        after=after,
        carry=carry,
    )
    split = []
    for _, parts in groups:
        split.append(made[: len(parts)])
        made = made[len(parts) :]
    return (*split, *made)


def stage(arrays, parts, after=(), name="stage"):
    made, token = stages(((arrays, parts),), after, name)
    return (*made, token)


def row_set(index, start, rows):
    return (rows, ((index, start),))


def gather_one(block, move):
    return move(block, 0, 1), move(block, 1, 0), move(block, -1, 0)


def gather_two(block, got, move, after, name):
    parts = (
        (row_set(1, 0, LANE), row_set(2, 0, HALF)),
        (row_set(3, HALF, HALF), row_set(1, 0, LANE)),
    )
    up, down, token = stage((block, *got), parts, after=after, name=name)
    return (move(up, 1, 0), move(down, -1, 0)), token


def gather_three(block, first, got, move, after, name):
    joined = tuple((n, ((2 + k, 0),)) for k, n in enumerate((LANE,) * 4)) + (
        row_set(0, 0, 192),
        row_set(1, 0, 192),
    )
    parts = ((row_set(0, 0, HALF),), (row_set(1, LANE, HALF),), joined)
    up, down, joined, token = stage((*got, block, *first), parts, after=after, name=name)
    return (move(up, 1, 0), move(down, -1, 0)), joined, token


def pair_two(block, other, move, after, name):
    both, token = stage((block, other), ((row_set(0, 0, LANE), row_set(1, 0, LANE)),), after=after, name=name)
    return both, (move(both, 1, 0), move(both, -1, 0)), token


def pair_three(both, got, move, after, name):
    parts = (
        (row_set(0, 0, HALF), row_set(0, LANE, HALF)),
        (row_set(1, HALF, HALF), row_set(1, LANE + HALF, HALF)),
        (
            row_set(2, 0, 2 * LANE),
            row_set(0, 0, LANE),
            row_set(1, 0, LANE),
            row_set(0, LANE, LANE),
            row_set(1, LANE, LANE),
        ),
    )
    up, down, joined, token = stage((*got, both), parts, after=after, name=name)
    return (move(up, 1, 0), move(down, -1, 0)), joined, token


def sums_of(count, start):
    return tuple((k, start) for k in range(count))


def scatter_one(n):
    return (((HALF, sums_of(n, 7 * LANE)),), ((HALF, sums_of(n, 7 * LANE + HALF)),))


def scatter_two(n):
    add = lambda start: sums_of(n, start)
    return (
        (
            (HALF, (*add(6 * LANE), (n, 0))),
            (HALF, add(6 * LANE + HALF)),
            (HALF, add(5 * LANE)),
        ),
        (
            (HALF, add(5 * LANE + HALF)),
            (HALF, add(4 * LANE)),
            (HALF, (*add(4 * LANE + HALF), (n + 1, 0))),
        ),
    )


def scatter_three(n):
    add = lambda start: sums_of(n, start)
    return (
        ((HALF, (*add(3 * LANE), (n, LANE))), (HALF, add(3 * LANE + HALF))),
        ((HALF, add(2 * LANE)), (HALF, (*add(2 * LANE + HALF), (n + 1, 0)))),
        ((LANE, (*add(LANE), (n, 0), (n + 1, HALF))),),
    )


def pair_scatter_one(n):
    add = lambda start: sums_of(n, start)
    return (
        ((HALF, add(5 * LANE)), (HALF, add(7 * LANE))),
        ((HALF, add(5 * LANE + HALF)), (HALF, add(7 * LANE + HALF))),
    )


def pair_scatter_two(n):
    add = lambda start: sums_of(n, start)
    return (
        (
            (HALF, (*add(3 * LANE), (n, 0))),
            (HALF, add(3 * LANE + HALF)),
            (HALF, (*add(6 * LANE), (n, HALF))),
            (HALF, add(6 * LANE + HALF)),
        ),
        (
            (HALF, add(2 * LANE)),
            (HALF, (*add(2 * LANE + HALF), (n + 1, 0))),
            (HALF, add(4 * LANE)),
            (HALF, (*add(4 * LANE + HALF), (n + 1, HALF))),
        ),
    )


def pair_scatter_three(n):
    return (((LANE, (*sums_of(n, LANE), (n, LANE), (n + 1, LANE))),),)


ADD_ALL = (((16, ((0, 0), (1, 0))),),)
ADD_THREE = (((16, ((0, 0), (1, 0), (2, 0), (3, 0))),),)
ADD_SHARED = (((8, ((0, 0), (1, 0))),),)
ADD_SPLIT = (((8, ((0, 0), (1, 0))),), ((8, ((0, 8), (1, 8))),))


def both_ways(sends, move):
    got = [move(sends[0], 1, 0), move(sends[1], -1, 0)]
    return (*got, *(move(send, 0, 1) for send in sends[2:]))


def feature_place(k):
    dp = lax.axis_index("dp")
    dy, dx = ORDER[k % 8]
    y, xh, c = lax.shift_right_logical(dp, 2), lax.shift_right_logical(dp, 1) & 1, dp & 1
    return ((((y + dy) & 3) * 2 + (xh ^ dx)) * 2) + (c ^ (k // 8))


def feature_cols(k):
    return pl.ds(pl.multiple_of(feature_place(k) * LANE, LANE), LANE)


def fixed_cols(k):
    return slice(k * LANE, (k + 1) * LANE)


def centred(rows):
    rows = rows.astype(F32)
    rows = rows - jnp.mean(rows, axis=-1, keepdims=True)
    return rows, lax.rsqrt(jnp.mean(rows * rows, axis=-1, keepdims=True) + EPS)


def begin_kernel(x, hat, held):
    rows, rate = centred(x[...])
    held[...] = rows * rate
    for k in range(16):
        hat[:, fixed_cols(k)] = held[:, feature_cols(k)].astype(BF)


def begin(x):
    return call(
        begin_kernel, (x,), [shape(LANE, D, BF)], scratch=[pltpu.VMEM((LANE, D), F32)], name="begin"
    )


def beside_kernel(w_qkv, w_in, part_a, sems):
    copies = Copies(sems)
    begun = [copies.start(w_qkv, part_a.at[:, :768]), copies.start(w_in, part_a.at[:, 768:])]
    wait(begun)


def beside(w_qkv, w_in, after):
    return call(
        beside_kernel, (w_qkv, w_in), [shape(LANE, 1792, BF)], ins=SLOW,
        scratch=[pltpu.SemaphoreType.DMA((2,))], name="beside", after=after,
    )


def prepare_kernel(
    g, w_dense, w_out, g1, b1, g2, b2, b_qkv, b_in, near_g, part_b, vectors, bias, g_sum
):
    for k in range(16):
        to, at = fixed_cols(k), feature_cols(k)
        near_g[:, to] = g[:, at]
        for n, vector in enumerate((g1, b1, g2, b2)):
            vectors[n : n + 1, to] = vector[:, at]
    part_b[:, :DH] = w_dense[...].T
    part_b[:, DH:] = w_out[...].T
    bias[:, :768] = b_qkv[...]
    bias[:, 768:] = b_in[...]
    g_sum[...] = jnp.sum(g[...].astype(F32), axis=0, keepdims=True)


def prepare(*args, after):
    return call(
        prepare_kernel, args,
        [
            shape(LANE, D, BF), shape(LANE, 1280, BF), shape(4, D, F32), shape(1, 1792, F32), shape(1, D, F32),
        ],
        name="prepare", after=after,
    )


def positions(segment):
    count = segment.shape[0]
    index = jnp.arange(count, dtype=jnp.int32)
    change = jnp.concatenate([jnp.ones((1,), dtype=bool), segment[1:] != segment[:-1]])
    start = lax.cummax(jnp.where(change, index, jnp.zeros_like(index)), axis=0)
    return index - start


def angles(segment):
    lane = jnp.arange(LANE, dtype=jnp.int32)
    exponent = (lane % (ROT // 2)).astype(F32) * (2.0 / ROT)
    inverse = jnp.where(lane < ROT, jnp.exp(-exponent * math.log(10000.0)), 0.0)
    angle = positions(segment).astype(F32)[:, None] * inverse[None, :]
    return jnp.cos(angle), jnp.sin(angle)


def dot(a, b, ca, cb):
    return lax.dot_general(a, b, (((ca,), (cb,)), ((), ())), preferred_element_type=F32)


def turn(head, cosine, sine):
    lane = lax.broadcasted_iota(jnp.int32, head.shape, 1)
    ahead = pltpu.roll(head, LANE - ROT // 2, 1)
    behind = pltpu.roll(head, ROT // 2, 1)
    return head * cosine + jnp.where(lane < ROT // 2, -ahead, behind) * sine


def masked_scores(q, k, seg_col, seg_row, first):
    scores = dot(q, k, 1, 1)
    row = first + lax.broadcasted_iota(jnp.int32, scores.shape, 0)
    col = lax.broadcasted_iota(jnp.int32, scores.shape, 1)
    allowed = (seg_col == seg_row) & (row >= col)
    return jnp.where(allowed, scores, NEG)


def load_weights(copies, pairs, cols, shift=0):
    place = slice(cols.start - shift, cols.stop - shift)
    started = []
    for pieces, layout, held in pairs:
        for piece, start, rows, block, offset in layout:
            at = block * LANE + offset
            started.append(
                copies.start(
                    pieces[piece].at[start : start + rows, cols], held.at[at : at + rows, place]
                )
            )
    return started


JOINED_PAIR = ((0, 0, 640, 0, 0), (0, 640, 128, 6, 0), (1, 0, 128, 5, 0), (1, 128, 128, 7, 0))
JOINED = ((0, 0, 896, 0, 0), (1, 0, 128, 7, 0))


def weighted(norm, own, other, bias, lo, hi, at, shift=0):
    half = D // 2
    return (
        dot(norm[lo:hi, :half], own[:, at : at + TILE], 1, 0)
        + dot(norm[lo:hi, half:], other[:, at : at + TILE], 1, 0)
        + bias[:, shift + at : shift + at + TILE]
    )


def normed(hat, vectors, norm, lo, hi, k):
    x = hat[lo:hi, :].astype(F32)
    norm[lo:hi, :] = (x * vectors[k : k + 1, :] + vectors[k + 1 : k + 2, :]).astype(BF)


def attention_kernel(ready, *refs):
    hat_hbm, near, far, cosine_hbm, sine_hbm, seg_hbm = refs[0], refs[1:3], refs[3:5], *refs[5:8]
    vectors, bias, seg_row, mixed_out, context, log_total = refs[8:14]
    hat, own, other, norm, mixed, cosine, sine, seg_col, sems = refs[14:]
    copies = Copies(sems)
    pairs = ((near, JOINED, own), (far, JOINED, other))
    rows, tiles = [], []

    def next_rows():
        if len(rows) < 4:
            part = slice(*QUARTERS[len(rows)])
            arrays = ((hat_hbm, hat), (cosine_hbm, cosine), (sine_hbm, sine))
            rows.append([copies.start(a.at[part, :], held.at[part, :]) for a, held in arrays])

    def next_tile():
        if len(tiles) < 3:
            cols = slice(len(tiles) * TILE, (len(tiles) + 1) * TILE)
            tiles.append(load_weights(copies, pairs, cols))

    next_tile()
    next_rows()
    next_rows()
    ready()
    for i in range(3):
        wait(tiles[i])
        for n, (lo, hi) in enumerate(QUARTERS):
            if i == 0:
                wait(rows[n])
                next_rows()
                normed(hat, vectors, norm, lo, hi, 0)
            if n == 1:
                next_tile()
            acc = weighted(norm, own, other, bias, lo, hi, i * TILE)
            if i < 2:
                head = turn(acc[:, :LANE], cosine[lo:hi, :], sine[lo:hi, :])
                acc = jnp.concatenate([head, acc[:, LANE:]], axis=1)
            if i == 0:
                acc = acc * SCALE
            mixed[lo:hi, i * TILE : (i + 1) * TILE] = acc.astype(BF)
        if i == 0:
            segs = [copies.start(seg_hbm, seg_col)]
    wait(segs)
    saved = [copies.start(mixed, mixed_out)]
    for lo, hi in QUARTERS:
        scores = masked_scores(
            mixed[lo:hi, :DH], mixed[:hi, DH : 2 * DH], seg_col[lo:hi, :1], seg_row[:, :hi], lo
        )
        top = jnp.max(scores, axis=-1, keepdims=True)
        weights = jnp.exp(scores - top)
        total = jnp.sum(weights, axis=-1, keepdims=True)
        log_total[lo:hi, :] = jnp.broadcast_to(top + jnp.log(total), (hi - lo, LANE))
        probs = (weights * (1.0 / total)).astype(BF)
        context[lo:hi, :] = dot(probs, mixed[:hi, 2 * DH :], 1, 0).astype(BF)
    wait(saved)


def attention(hat, near, far, cosine, sine, seg_col, vectors, bias, seg_row, after):
    return call(
        attention_kernel,
        (hat, *near, *far, cosine, sine, seg_col, vectors, bias, seg_row),
        [shape(LENGTH, 768, BF), shape(LENGTH, DH, BF), shape(LENGTH, LANE, F32)],
        ins=[SLOW] * 8 + [FAST] * 3,
        to=[SLOW, FAST, FAST],
        scratch=[
            pltpu.VMEM((LENGTH, D), BF), pltpu.VMEM((1024, 768), BF),
            pltpu.VMEM((1024, 768), BF), pltpu.VMEM((LENGTH, D), BF),
            pltpu.VMEM((LENGTH, 768), BF), pltpu.VMEM((LENGTH, LANE), F32),
            pltpu.VMEM((LENGTH, LANE), F32), pltpu.VMEM((LENGTH, LANE), jnp.int32),
            pltpu.SemaphoreType.DMA((28,)),
        ],
        cost=(2 * LENGTH * D * 768 + 4 * LENGTH * LENGTH * DH, LENGTH * 1024),
        name="attention", after=after, lazy=True,
    )


def units_kernel(ready, *refs):
    hat_hbm, near, far, vectors, bias = refs[0], refs[1:3], refs[3:5], refs[5], refs[6]
    hidden_out, slope_out, hat, own, other, norm, hidden, slope, sems = refs[7:]
    copies = Copies(sems)
    pairs = ((near, JOINED, own), (far, JOINED, other))
    rows, tiles = [], []

    def next_rows():
        if len(rows) < 4:
            part = slice(*QUARTERS[len(rows)])
            rows.append(copies.start(hat_hbm.at[part, :], hat.at[part, :]))

    def next_tile():
        if len(tiles) < 4:
            at = 768 + len(tiles) * TILE
            tiles.append(load_weights(copies, pairs, slice(at, at + TILE), 768))

    next_tile()
    next_rows()
    next_rows()
    ready()
    saved = []
    for i in range(4):
        wait(tiles[i])
        cols = slice(i * TILE, (i + 1) * TILE)
        for n, (lo, hi) in enumerate(QUARTERS):
            if i == 0:
                wait(rows[n : n + 1])
                next_rows()
                normed(hat, vectors, norm, lo, hi, 2)
            if n == 1:
                next_tile()
            pre = weighted(norm, own, other, bias, lo, hi, i * TILE, 768)
            cdf = 0.5 * (1.0 + lax.erf(pre * (0.5**0.5)))
            hidden[lo:hi, cols] = (pre * cdf).astype(BF)
            density = jnp.exp(-0.5 * pre * pre) * (1.0 / math.sqrt(2.0 * math.pi))
            slope[lo:hi, cols] = (cdf + pre * density).astype(BF)
        saved.append(copies.start(hidden.at[:, cols], hidden_out.at[:, cols]))
        saved.append(copies.start(slope.at[:, cols], slope_out.at[:, cols]))
    wait(saved)


def units(hat, near, far, vectors, bias, after):
    return call(
        units_kernel, (hat, *near, *far, vectors, bias), [shape(LENGTH, 1024, BF)] * 2,
        ins=[SLOW] * 5 + [FAST] * 2, to=SLOW,
        scratch=[
            pltpu.VMEM((LENGTH, D), BF), pltpu.VMEM((1024, 1024), BF),
            pltpu.VMEM((1024, 1024), BF), pltpu.VMEM((LENGTH, D), BF),
            pltpu.VMEM((LENGTH, 1024), BF), pltpu.VMEM((LENGTH, 1024), BF),
            pltpu.SemaphoreType.DMA((32,)),
        ],
        cost=(2 * LENGTH * D * 1024, LENGTH * 2048), name="units", after=after, lazy=True,
    )


def outer_b_kernel(first, g, context, hidden, grad_hbm, left, held_c, held_h, grad, sems):
    copies = Copies(sems)
    begun = [copies.start(context, held_c), copies.start(hidden, held_h)]
    tiles = load_tiles(copies, g, left, first)
    wait(begun)
    done = []
    for i in range(4):
        cols = slice(i * TILE, (i + 1) * TILE)
        wait(tiles[i : i + 1])
        grad[cols, :DH] = dot(left[:, cols], held_c[...], 0, 0).astype(BF)
        grad[cols, DH:] = dot(left[:, cols], held_h[...], 0, 0).astype(BF)
        done.append(copies.start(grad.at[cols, :], grad_hbm.at[cols, :]))
    wait(done)


def outer_b(g, context, hidden, first, after):
    return call(
        functools.partial(outer_b_kernel, first), (g, context, hidden), [shape(1024, 1280, BF)],
        ins=SLOW, to=SLOW,
        scratch=[
            pltpu.VMEM((LENGTH, 1024), BF), pltpu.VMEM((LENGTH, DH), BF),
            pltpu.VMEM((LENGTH, 1024), BF), pltpu.VMEM((1024, 1280), BF),
            pltpu.SemaphoreType.DMA((12,)),
        ],
        cost=(2 * LENGTH * 1024 * 1280, 0), name="outer_b", after=after,
    )


def output_kernel(*refs):
    context, hidden, near, far = refs[0], refs[1], refs[2:4], refs[4:6]
    out_hbm, held_c, held_h, own, other, out, sems = refs[6:]
    copies = Copies(sems)
    firsts = load_weights(copies, ((near, JOINED_PAIR[:1], own),), slice(0, 1280))
    begun = [copies.start(context, held_c), copies.start(hidden, held_h)]
    nears = load_weights(copies, ((near, JOINED_PAIR[1:], own),), slice(0, 1280))
    fars = load_weights(copies, ((far, JOINED_PAIR, other),), slice(0, 1280))
    wait(firsts + begun)
    done = []
    for i in range(8):
        held = own if i < 4 else other
        at = i % 4 * TILE
        cols = slice(i * TILE, (i + 1) * TILE)
        if i == 1:
            wait(nears)
        if i == 4:
            wait(fars)
        for lo, hi in QUARTERS:
            out[lo:hi, cols] = (
                dot(held_c[lo:hi, :], held[at : at + TILE, :DH], 1, 1)
                + dot(held_h[lo:hi, :], held[at : at + TILE, DH:], 1, 1)
            ).astype(BF)
        if i % 2:
            pair = slice((i - 1) * TILE, (i + 1) * TILE)
            done.append(copies.start(out.at[:, pair], out_hbm.at[:, pair]))
    wait(done)


def output(context, hidden, near, far, after):
    return call(
        output_kernel, (context, hidden, *near, *far), [shape(LENGTH, D, BF)], ins=SLOW, to=SLOW,
        scratch=[
            pltpu.VMEM((LENGTH, DH), BF), pltpu.VMEM((LENGTH, 1024), BF),
            pltpu.VMEM((1024, 1280), BF), pltpu.VMEM((1024, 1280), BF),
            pltpu.VMEM((LENGTH, D), BF), pltpu.SemaphoreType.DMA((16,)),
        ],
        cost=(2 * LENGTH * D * 1280, 0), name="output", after=after,
    )


def column(row):
    parts = [jnp.broadcast_to(row[:, fixed_cols(k)], (LANE, LANE)).T for k in range(2)]
    return jnp.concatenate(parts, axis=0)


def backward_kernel(ready, *refs):
    g, near, far = refs[0], refs[1:3], refs[3:5]
    slope_hbm, mixed_hbm, near_a, far_a, hat_hbm = refs[5], refs[6], refs[7:9], refs[9:11], refs[11]
    log_total, seg_col, seg_row, cosine, sine, vectors, g_sum = refs[12:19]
    mixed_grad_hbm, pre_hbm, u_hbm, sum_qkv, sum_in, sums = refs[19:25]
    held, own, other, slope, mixed, own_a, other_a, d_context, d_pre, d_mixed, d_k, d_v, u, hat, sems = refs[25:]
    half = D // 2
    copies = Copies(sems)
    pairs = ((near, JOINED_PAIR, own), (far, JOINED_PAIR, other))
    first = load_weights(copies, pairs, slice(0, TILE))
    rows = [copies.start(g.at[lo:hi, :], held.at[lo:hi, :]) for lo, hi in QUARTERS]
    tiles = [load_weights(copies, pairs, slice(k * TILE, (k + 1) * TILE)) for k in range(1, 5)]
    slopes = [copies.start(slope_hbm, slope)]
    mixes = [copies.start(mixed_hbm, mixed)]
    inputs = [load_weights(copies, ((near_a, JOINED, own_a),), slice(0, 1792))]
    inputs += [load_weights(copies, ((far_a, JOINED, other_a),), slice(0, 1792))]
    hats = [
        copies.start(hat_hbm.at[:, k * 512 : (k + 1) * 512], hat.at[:, k * 512 : (k + 1) * 512])
        for k in range(4)
    ]
    done = []

    def product(lo, hi, cols):
        return dot(held[lo:hi, :half], own[:, cols], 1, 0) + dot(held[lo:hi, half:], other[:, cols], 1, 0)

    wait(first)
    for n, (lo, hi) in enumerate(QUARTERS):
        wait(rows[n : n + 1])
        d_context[lo:hi, :] = product(lo, hi, slice(0, TILE)).astype(BF)
    wait(slopes)
    for i in range(4):
        wait(tiles[i])
        cols = slice(i * TILE, (i + 1) * TILE)
        total = jnp.zeros((1, TILE), F32)
        for lo, hi in QUARTERS:
            acc = product(lo, hi, slice((i + 1) * TILE, (i + 2) * TILE))
            rounded = (acc * slope[lo:hi, cols].astype(F32)).astype(BF)
            d_pre[lo:hi, cols] = rounded
            total += jnp.sum(rounded.astype(F32), axis=0, keepdims=True)
        sum_in[:, cols] = total
    done.append(copies.start(d_pre, pre_hbm))

    wait(mixes)
    ready()
    sums[...] = jnp.zeros_like(sums)
    d_k[...] = jnp.zeros_like(d_k)
    d_v[...] = jnp.zeros_like(d_v)

    def back(lo, hi, value):
        head = turn(value[:, :LANE], cosine[lo:hi, :], -sine[lo:hi, :])
        return jnp.concatenate([head, value[:, LANE:]], axis=1)

    for lo, hi in QUARTERS:
        q, k, v = mixed[lo:hi, :DH], mixed[:hi, DH : 2 * DH], mixed[:hi, 2 * DH :]
        dc = d_context[lo:hi, :]
        scores = masked_scores(q, k, seg_col[lo:hi, :1], seg_row[:, :hi], lo)
        probs = jnp.exp(scores - log_total[lo:hi, :1])
        d_probs = dot(dc, v, 1, 1)
        spread = jnp.sum(probs * d_probs, axis=-1, keepdims=True)
        d_scores = (probs * (d_probs - spread)).astype(BF)
        d_mixed[lo:hi, :DH] = (back(lo, hi, dot(d_scores, k, 1, 0)) * SCALE).astype(BF)
        d_k[:hi, :] += dot(d_scores, q, 0, 0)
        d_v[:hi, :] += dot(probs.astype(BF), dc, 0, 0)
    total = jnp.zeros((1, 768), F32)
    for lo, hi in QUARTERS:
        d_mixed[lo:hi, DH : 2 * DH] = back(lo, hi, d_k[lo:hi, :]).astype(BF)
        d_mixed[lo:hi, 2 * DH :] = d_v[lo:hi, :].astype(BF)
        total += jnp.sum(d_mixed[lo:hi, :].astype(F32), axis=0, keepdims=True)
    sum_qkv[...] = total
    done.append(copies.start(d_mixed, mixed_grad_hbm))
    sums[4:5, :] = g_sum[...]
    sums[BIASES : BIASES + 1, :768] = sum_qkv[...]
    sums[BIASES : BIASES + 1, 768:1792] = sum_in[...]

    for i in range(8):
        weights = own_a if i < 4 else other_a
        at = i % 4 * TILE
        cols = slice(i * TILE, (i + 1) * TILE)
        if i % 4 == 0:
            wait(inputs[i // 4])
        if i % 2 == 0:
            wait(hats[i // 2 : i // 2 + 1])
        totals = [jnp.zeros((1, TILE), F32) for _ in range(4)]
        for lo, hi in QUARTERS:
            d1 = dot(d_mixed[lo:hi, :], weights[at : at + TILE, :768], 1, 1)
            d2 = dot(d_pre[lo:hi, :], weights[at : at + TILE, 768:], 1, 1)
            x = hat[lo:hi, cols].astype(F32)
            u[lo:hi, cols] = (d1 * vectors[0:1, cols] + d2 * vectors[2:3, cols]).astype(BF)
            for k, term in enumerate((d1 * x, d1, d2 * x, d2)):
                totals[k] += jnp.sum(term, axis=0, keepdims=True)
        for k in range(4):
            for j in range(2):
                sums[k : k + 1, feature_cols(2 * i + j)] = totals[k][:, fixed_cols(j)]
        done.append(copies.start(u.at[:, cols], u_hbm.at[:, cols]))
    wait(done)


def backward(g, near, far, slope, mixed, near_a, far_a, *rest, after):
    return call(
        backward_kernel,
        (g, *near, *far, slope, mixed, *near_a, *far_a, *rest),
        [
            shape(LENGTH, 768, BF), shape(LENGTH, 1024, BF), shape(LENGTH, D, BF),
            shape(1, 768, F32), shape(1, 1024, F32), shape(16, D, F32),
        ],
        ins=[SLOW] * 12 + [FAST] * 7, to=[SLOW] * 3 + [FAST] * 3,
        scratch=[
            pltpu.VMEM((LENGTH, D), BF), pltpu.VMEM((1024, 1280), BF),
            pltpu.VMEM((1024, 1280), BF), pltpu.VMEM((LENGTH, 1024), BF),
            pltpu.VMEM((LENGTH, 768), BF),
            pltpu.VMEM((1024, 1792), BF), pltpu.VMEM((1024, 1792), BF),
            pltpu.VMEM((LENGTH, DH), BF), pltpu.VMEM((LENGTH, 1024), BF),
            pltpu.VMEM((LENGTH, 768), BF), pltpu.VMEM((LENGTH, DH), F32),
            pltpu.VMEM((LENGTH, DH), F32), pltpu.VMEM((LENGTH, D), BF), pltpu.VMEM((LENGTH, D), BF),
            pltpu.SemaphoreType.DMA((80,)),
        ],
        cost=(2 * LENGTH * (D * 1280 + D * 1792 + 5 * LENGTH * DH), LENGTH * LENGTH),
        name="backward", after=after, lazy=True,
    )


def outer_a_kernel(ready, hat_hbm, mixed_hbm, pre_hbm, vectors, sum_qkv, sum_in, *refs):
    grad_far_hbm, grad_near_hbm, hat, d_mixed, d_pre, grad, sems = refs
    copies = Copies(sems)
    order = (4, 5, 6, 7, 0, 1, 2, 3)
    hats, done = [], []

    def next_hat():
        if len(hats) < 8:
            i = order[len(hats)]
            cols = slice(i * TILE, (i + 1) * TILE)
            hats.append(copies.start(hat_hbm.at[:, cols], hat.at[:, cols]))

    next_hat()
    begun = [[copies.start(mixed_hbm, d_mixed)]]
    begun.append([copies.start(pre_hbm, d_pre)])
    next_hat()
    ready()
    parts = ((0, 768, d_mixed, sum_qkv), (768, 1792, d_pre, sum_in))
    for step, i in enumerate(order):
        cols = slice(i * TILE, (i + 1) * TILE)
        out = grad_near_hbm if i < 4 else grad_far_hbm
        wait(hats[step : step + 1])
        next_hat()
        for n, (lo, hi, upstream, total) in enumerate(parts):
            if step == 0:
                wait(begun[n])
            plain = dot(hat[:, cols], upstream[...], 0, 0)
            gain, bias = (column(vectors[2 * n + k : 2 * n + k + 1, cols]) for k in range(2))
            for k in range((hi - lo) // LANE):
                lanes = fixed_cols(k)
                grad[cols, lo + k * LANE : lo + (k + 1) * LANE] = (
                    gain * plain[:, lanes] + bias * total[:, lanes]
                ).astype(BF)
        done.append(copies.start(grad.at[cols, :], out.at[i % 4 * TILE : (i % 4 + 1) * TILE, :]))
    wait(done)


def outer_a(*args, after):
    return call(
        outer_a_kernel, args, [shape(1024, 1792, BF), shape(1024, 1792, BF)],
        ins=[SLOW] * 3 + [FAST] * 3, to=[SLOW] * 2,
        scratch=[
            pltpu.VMEM((LENGTH, D), BF), pltpu.VMEM((LENGTH, 768), BF), pltpu.VMEM((LENGTH, 1024), BF),
            pltpu.VMEM((D, 1792), BF), pltpu.SemaphoreType.DMA((20,)),
        ],
        cost=(2 * LENGTH * D * 1792, 0), name="outer_a", after=after, lazy=True,
    )


def load_tiles(copies, source, held, first):
    return [
        copies.start(
            source.at[:, first + i * TILE : first + (i + 1) * TILE],
            held.at[:, i * TILE : (i + 1) * TILE],
        )
        for i in range(4)
    ]


def finish_out_kernel(x, summed, b_dense, b_out, out):
    for k in range(16):
        to = feature_cols(k)
        value = x[:, to].astype(F32) + summed[:, fixed_cols(k)].astype(F32)
        out[:, to] = (value + b_dense[:, to] + b_out[:, to]).astype(BF)


def finish_out(*args, after):
    return call(
        finish_out_kernel, args, [shape(LANE, D, BF)], name="finish_out", after=after,
    )


def finish_grad_kernel(x, g, u, out):
    centre = jnp.mean(x[...].astype(F32), axis=-1, keepdims=True)
    rate = centred(x[...])[1]
    total = u[...].astype(F32)
    mean = jnp.mean(total, axis=-1, keepdims=True)
    spread = jnp.zeros((LANE, 1), F32)
    for k in range(16):
        hat = x[:, feature_cols(k)].astype(F32) - centre
        spread += jnp.sum(total[:, fixed_cols(k)] * hat, axis=-1, keepdims=True)
    spread = spread * rate * rate * (1.0 / D)
    for k in range(16):
        to = feature_cols(k)
        hat = x[:, to].astype(F32) - centre
        back = rate * (total[:, fixed_cols(k)] - mean - hat * spread)
        out[:, to] = (g[:, to].astype(F32) + back).astype(BF)


def finish_grad(*args, after):
    return call(
        finish_grad_kernel, args, [shape(LANE, D, BF)], name="finish_grad", after=after,
    )


def total_of(copies, arrays, held):
    begun = [
        copies.start(source.at[:LANE, :], held.at[k * LANE : (k + 1) * LANE, :])
        for k, source in enumerate(arrays)
    ]

    def total():
        wait(begun)
        value = held[:LANE, :].astype(F32)
        for k in range(1, len(arrays)):
            value = value + held[k * LANE : (k + 1) * LANE, :].astype(F32)
        return value

    return total


def finish_a_kernel(*refs):
    arrays, (qkv, units, held, sems) = refs[:5], refs[5:]
    value = total_of(Copies(sems), arrays, held)()
    qkv[...] = value[:, :768]
    units[...] = value[:, 768:]


def finish_a(arrays, after):
    return call(
        finish_a_kernel, arrays, [shape(LANE, 768, F32), shape(LANE, 1024, F32)], ins=SLOW,
        scratch=[pltpu.VMEM((5 * LANE, 1792), BF), pltpu.SemaphoreType.DMA((5,))],
        name="finish_a", after=after,
    )


def finish_b_kernel(*refs):
    arrays, sums, got, split_sums = refs[:5], refs[5], refs[6], refs[7]
    dense, out, rows, qkv, units, held, sems = refs[8], refs[9], refs[10:16], *refs[16:]
    total = total_of(Copies(sems), arrays, held)
    for k, row in enumerate(rows):
        at = min(k, 4)
        row[...] = (sums[at : at + 1, :] + got[at : at + 1, :])[0]
    biases = split_sums[BIASES - 8 : BIASES - 7, :]
    qkv[...] = biases[0, :768]
    units[...] = biases[0, 768:1792]
    value = total()
    dense[...] = value[:, :DH].T
    out[...] = value[:, DH:].T


def finish_b(arrays, sums, got, split_sums, after):
    return call(
        finish_b_kernel, (*arrays, sums, got, split_sums),
        [
            shape(DH, LANE, F32), shape(1024, LANE, F32),
            *(jax.ShapeDtypeStruct((n,), F32) for n in (D, D, D, D, D, D, 768, 1024)),
        ],
        ins=[SLOW] * 5 + [FAST] * 3,
        scratch=[pltpu.VMEM((5 * LANE, 1280), BF), pltpu.SemaphoreType.DMA((5,))],
        name="finish_b", after=after,
    )


def per_device(
    hidden_in,
    segment_ids,
    ln1_gain,
    ln1_bias,
    ln2_gain,
    ln2_bias,
    w_qkv,
    b_qkv,
    w_dense,
    b_dense,
    w_in,
    b_in,
    w_out,
    b_out,
    cotangent,
):
    row = lambda vector: vector[None, :]
    dp, tensor = dp_move, tensor_move

    own_hat, token = begin(hidden_in)
    part_a, token = beside(w_qkv, w_in, (token,))
    hat = lax.all_gather(own_hat, "tensor", axis=0, tiled=True)
    got_a = gather_one(part_a, dp)
    more_a, token = gather_two(part_a, got_a, dp, (token,), "a_two")
    own_g, part_b, vectors, bias, g_sum, token = prepare(
        cotangent, w_dense, w_out, row(ln1_gain), row(ln1_bias), row(ln2_gain), row(ln2_bias),
        row(b_qkv), row(b_in), after=(token,),
    )
    all_g = lax.all_gather(own_g, "tensor", axis=0, tiled=True)
    other_b = dp(part_b, 0, 1)
    cosine, sine = angles(segment_ids)
    seg_col = jnp.broadcast_to(segment_ids[:, None], (LENGTH, LANE))
    seg_row = row(segment_ids)

    last_a, a0, token = gather_three(
        part_a, got_a, more_a, dp, (token, cosine, sine, seg_col), "a_three"
    )
    far_a0 = dp(a0, 0, 0, 1)
    a1, token = stage(last_a, ((row_set(0, 0, HALF), row_set(1, 0, HALF)),), after=(token,), name="a_four")
    far_a1 = dp(a1, 0, 0, 1)
    both_b, more_b, token = pair_two(part_b, other_b, dp, (token,), "b_two")
    near_a, far_a = (a0, a1), (far_a0, far_a1)
    mixed, context, log_total, token = attention(
        hat, near_a, far_a, cosine, sine, seg_col, vectors, bias, seg_row, (token,)
    )
    last_b, b0, token = pair_three(both_b, more_b, dp, (token,), "b_three")
    far_b0 = dp(b0, 0, 0, 1)
    hidden, slope, token = units(hat, near_a, far_a, vectors, bias, (token,))
    halves = tuple(row_set(k, at, HALF) for at in (0, HALF) for k in (0, 1))
    b1, token = stage(last_b, (halves,), after=(token,), name="b_four")
    far_b1 = dp(b1, 0, 0, 1)
    near_b, far_b = (b0, b1), (far_b0, far_b1)
    out_part, token = output(context, hidden, near_b, far_b, (token,))
    summed = lax.psum_scatter(out_part, "tensor", scatter_dimension=0, tiled=True)

    d_mixed, d_pre, u, sum_qkv, sum_in, sums, token = backward(
        all_g, near_b, far_b, slope, mixed, near_a, far_a, hat, log_total, seg_col, seg_row,
        cosine, sine, vectors, g_sum, after=(token,),
    )
    u_rows = lax.psum_scatter(u, "tensor", scatter_dimension=0, tiled=True)
    others = tuple(butterfly(sums, "dp", y, 0, core) for y, core in ((1, 0), (0, 1), (1, 1)))
    grad_a_far, grad_a, token = outer_a(
        hat, d_mixed, d_pre, vectors, sum_qkv, sum_in, after=(token,)
    )
    (sums,), token, grad_a_far = stages(
        (((sums, *others), ADD_THREE),), (token,), "sums_y", (grad_a_far,)
    )
    got_far_a = dp(grad_a_far, 0, 0, 1)
    others = butterfly(sums, "dp", 2, 0)
    grad_b_far, token = outer_b(all_g, context, hidden, 1024, (token,))
    chunks_a = (grad_a, got_far_a)
    sends, (sums,), token, grad_b_far = stages(
        ((chunks_a, scatter_one(2)), ((sums, others), ADD_ALL)), (token,), "grad_a_one", (grad_b_far,)
    )
    step_a = both_ways(sends, dp)
    got_far_b = dp(grad_b_far, 0, 0, 1)
    others = butterfly(sums, "dp", 0, 1)
    grad_b, token = outer_b(all_g, context, hidden, 0, (token,))
    chunks_b = (grad_b, got_far_b)
    sends_b, sends_a, (sums, split_sums), token = stages(
        (
            (chunks_b, pair_scatter_one(2)),
            ((*chunks_a, *step_a), scatter_two(2)),
            ((sums, others), ADD_SPLIT),
        ),
        (token,),
        "grads_two",
    )
    step_b, step_a = both_ways(sends_b, dp), both_ways(sends_a, dp)
    others = butterfly(sums, "tensor", 1, 0)
    hidden_out, token = finish_out(
        hidden_in, summed, row(b_dense), row(b_out), after=(token,)
    )
    sends, (sums,), token = stages(
        (((*chunks_b, *step_b), pair_scatter_two(2)), ((sums, others), ADD_SHARED)),
        (token,),
        "grad_b_two",
    )
    step_b = both_ways(sends, dp)
    others = butterfly(sums, "tensor", 2, 0)
    sends, token = stages(
        (((*chunks_a, *step_a), scatter_three(2)),), (token,), "grad_a_three"
    )
    step_a = both_ways(sends, dp)
    (send,), (sums,), token = stages(
        (((*chunks_b, *step_b), pair_scatter_three(2)), ((sums, others), ADD_SHARED)),
        (token,),
        "grad_b_three",
    )
    step_b = (*step_b, dp(send, 0, 1))
    others = butterfly(sums, "tensor", 0, 1)
    grad_input, token = finish_grad(hidden_in, cotangent, u_rows, after=(token,))
    grad_qkv, grad_in, token = finish_a((*chunks_a, *step_a), (token,))
    grad_dense, grad_out, *rows, token = finish_b((*chunks_b, *step_b), sums, others, split_sums, (token,))
    gain1, bias1, gain2, bias2, grad_b, grad_b_again, grad_b_qkv, grad_b_in = rows
    return (
        hidden_out,
        grad_input,
        gain1,
        bias1,
        gain2,
        bias2,
        grad_qkv,
        grad_b_qkv,
        grad_dense,
        grad_b,
        grad_in,
        grad_b_in,
        grad_out,
        grad_b_again,
    )


def butterfly(value, axis, step, flip, core=0):
    pairs = []
    if axis == "dp":
        for y in range(4):
            for xh in range(2):
                for c in range(2):
                    pairs.append(
                        ((y * 2 + xh) * 2 + c, ((y ^ step) * 2 + (xh ^ flip)) * 2 + (c ^ core))
                    )
    else:
        for xl in range(2):
            for z in range(4):
                pairs.append((xl * 4 + z, (xl ^ flip) * 4 + (z ^ step)))
    return lax.ppermute(value, axis, pairs)


def solution(mesh):
    in_specs = (
        P(("dp", "tensor"), None),
        P("dp"),
        P(),
        P(),
        P(),
        P(),
        P("dp", "tensor"),
        P("tensor"),
        P("tensor", "dp"),
        P(),
        P("dp", "tensor"),
        P("tensor"),
        P("tensor", "dp"),
        P(),
        P(("dp", "tensor"), None),
    )
    out_specs = (
        P(("dp", "tensor"), None),
        P(("dp", "tensor"), None),
        P(),
        P(),
        P(),
        P(),
        P("dp", "tensor"),
        P("tensor"),
        P("tensor", "dp"),
        P(),
        P("dp", "tensor"),
        P("tensor"),
        P("tensor", "dp"),
        P(),
    )
    return jax.shard_map(
        per_device, mesh=mesh, in_specs=in_specs, out_specs=out_specs, check_vma=False
    )
```
